512 devices in a mesh: tm: 32 (over x, z_lo), space: 16 (over y, z_hi, core).
Axes of the slice: x: 4, y: 4, z: 16 (z_hi: 2, z_lo: 8; z = z_hi * 8 + z_lo), core: 2. Of those that a mesh axis runs over, the one named last changes fastest.
Arguments:
- u_old: float32 [32, 5, 256, 16, 128], P('tm', None, 'space'), may hold values from -2.5 to 2.5
- u_init: float32 [256, 16, 128], P('space'), may hold values from -2.5 to 2.5
Outputs:
- u_new: float32 [32, 5, 256, 16, 128], P('tm', None, 'space')
The draws below stay inside these ranges and needn't reach their ends.
All inputs are finite; a program needn't handle non-finite values.
Results may differ from the reference program's by a relative error of at most 0.0003.
Values sent between devices are 32-bit elements; how exact they have to be, the bound alone decides.
No kernel may reach another device: no remote copies, remote signals or barrier semaphores. Data moves between devices by JAX's collectives and lax.ppermute only.
A program may use at most 64 MiB of HBM per device.

```python
import math
import jax
import jax.numpy as jnp
from jax import lax

NZ = 256
NX = 16
NY = 128
FINE_NODES = 5
SLICES = 32
N_TM = 32


def steps_of(key, extent, pieces, smallest, high):
    factor_of, own = 1.0, jax.random.fold_in(key, 6)
    for dim, shards_of in pieces:
        draws = jnp.exp(jax.random.uniform(jax.random.fold_in(own, dim), (shards_of,), jnp.float32, smallest / len(pieces), high / len(pieces)))
        factor_of = factor_of * jnp.repeat(draws, extent[dim] // shards_of).reshape([-1 if axis == dim else 1 for axis in range(len(extent))])
    return factor_of


def bell_draw(own_key, extent, spread, most, split=(), held_as=jnp.bfloat16):
    drawn = jax.random.normal(own_key, extent, jnp.float32) * spread
    if len(split) > 0:
        drawn = steps_of(own_key, extent, split, -0.22, 0.18) * drawn
    return jnp.clip(drawn, min=-most, max=most).astype(held_as)


def setup_inputs(seed: int = 0) -> dict:
    key_of = jax.random.split(jax.random.key(seed), 3)
    return {
        "u_old": bell_draw(key_of[0], (SLICES, FINE_NODES, NZ, NX, NY), 0.6, 2.5, ((0, 32), (2, 16)), jnp.float32),
        "u_init": bell_draw(key_of[1], (NZ, NX, NY), 0.6, 2.5, ((0, 16),), jnp.float32),
    }


step_length = 0.4
diffusion = 1.0
reaction = 1.0

def basis_coefficients(nodes, chosen):
    polynomial = [1.0]
    for other, point in enumerate(nodes):
        if other == chosen:
            continue
        divisor = nodes[chosen] - point
        widened = [0.0] * (len(polynomial) + 1)
        for power, value in enumerate(polynomial):
            widened[power + 1] += value / divisor
            widened[power] -= value * point / divisor
        polynomial = widened
    return polynomial

def basis_value(nodes, chosen, where):
    result = 1.0
    for other, point in enumerate(nodes):
        if other != chosen:
            result *= (where - point) / (nodes[chosen] - point)
    return result

def node_tables():
    root = math.sqrt(3.0 / 7.0)
    fine_tau = [0.0, (1.0 - root) / 2.0, 0.5, (1.0 + root) / 2.0, 1.0]
    coarse_tau = [0.0, 0.5, 1.0]
    integ = []
    for j in range(4):
        row_values = []
        for k in range(5):
            polynomial = basis_coefficients(fine_tau, k)
            total = 0.0
            for power, value in enumerate(polynomial):
                total += value * (fine_tau[j + 1] ** (power + 1) - fine_tau[j] ** (power + 1)) / (power + 1)
            row_values.append(total)
        integ.append(row_values)
    interp = [[basis_value(coarse_tau, c, fine_tau[m]) for c in range(3)] for m in range(5)]
    spacing = [float(fine_tau[j + 1] - fine_tau[j]) for j in range(4)]
    return (jnp.asarray(integ, jnp.float32), spacing, jnp.asarray(interp, jnp.float32))

def fine_force(field):
    near = jnp.roll(field, 1, 0) + jnp.roll(field, -1, 0) + jnp.roll(field, 1, 1) + jnp.roll(field, -1, 1)
    near = near + jnp.roll(field, 1, 2) + jnp.roll(field, -1, 2)
    return diffusion * (near - 6.0 * field) + reaction * (field - field * field * field)

def coarse_lap(field):
    near = jnp.roll(field, 1, 0) + jnp.roll(field, -1, 0) + jnp.roll(field, 1, 1) + jnp.roll(field, -1, 1)
    near = near + jnp.roll(field, 1, 2) + jnp.roll(field, -1, 2)
    return 0.25 * (near - 6.0 * field)

def restrict(field):
    depth, rows, cols = field.shape
    return field.reshape(depth // 2, 2, rows // 2, 2, cols // 2, 2).mean(axis=(1, 3, 5))

def reference(u_old, u_init):
    integ, spacing, interp = node_tables()
    depth_c, rows_c, cols_c = (NZ // 2, NX // 2, NY // 2)
    angle_z = 2.0 * jnp.cos(2.0 * jnp.pi * jnp.arange(depth_c, dtype=jnp.float32) / depth_c)
    angle_x = 2.0 * jnp.cos(2.0 * jnp.pi * jnp.arange(rows_c, dtype=jnp.float32) / rows_c)
    angle_y = 2.0 * jnp.cos(2.0 * jnp.pi * jnp.arange(cols_c, dtype=jnp.float32) / cols_c)
    eigen = 0.25 * (angle_z[:, None, None] + angle_x[None, :, None] + angle_y[None, None, :] - 6.0)
    denom = 1.0 - 0.5 * step_length * diffusion * eigen

    def solve(right):
        return jnp.real(jnp.fft.ifftn(jnp.fft.fftn(right) / denom)).astype(jnp.float32)
    carry = restrict(u_init)
    results = []
    for slice_index in range(N_TM):
        fine_old = u_old[slice_index]
        start = u_init if slice_index == 0 else u_old[slice_index - 1, 4]
        fold = jnp.stack([fine_force(fine_old[k]) for k in range(5)])
        iold = step_length * jnp.einsum('jk,kzxy->jzxy', integ, fold, precision=lax.Precision.HIGHEST)
        states = [start]
        forces = []
        for section in range(4):
            force_now = fine_force(states[section])
            forces.append(force_now)
            states.append(states[section] + step_length * spacing[section] * (force_now - fold[section]) + iold[section])
        forces.append(fine_force(states[4]))
        inew = step_length * jnp.einsum('jk,kzxy->jzxy', integ, jnp.stack(forces), precision=lax.Precision.HIGHEST)
        coarse = [restrict(states[0]), restrict(states[2]), restrict(states[4])]
        lifted0 = restrict(inew[0] + inew[1]) - 0.5 * step_length * diffusion * coarse_lap(coarse[1])
        lifted1 = restrict(inew[2] + inew[3]) - 0.5 * step_length * diffusion * coarse_lap(coarse[2])
        begin = carry
        middle = solve(begin + lifted0)
        finish = solve(middle + lifted1)
        carry = finish
        delta = jnp.stack([begin - coarse[0], middle - coarse[1], finish - coarse[2]])
        timed = jnp.einsum('mc,czxy->mzxy', interp, delta, precision=lax.Precision.HIGHEST)
        upper = jnp.repeat(jnp.repeat(jnp.repeat(timed, 2, 1), 2, 2), 2, 3)
        results.append(jnp.stack(states) + upper)
    return jnp.stack(results)
```

```python
import math

import jax
import jax.numpy as jnp
import numpy as np
from jax import lax
from jax.experimental import pallas as pl
from jax.experimental.pallas import tpu as pltpu
from jax.sharding import Mesh
from jax.sharding import PartitionSpec as P

TM = ("x", "zl")
SPACE = ("y", "zh", "c")

step_length = 0.4
diffusion = 1.0
reaction = 1.0

G_AT = (0, 4, 7, 9)
U_AT = 10
PACK = 14
REACH = 5


def basis_coefficients(nodes, chosen):
    polynomial = [1.0]
    for other, point in enumerate(nodes):
        if other == chosen:
            continue
        divisor = nodes[chosen] - point
        widened = [0.0] * (len(polynomial) + 1)
        for power, value in enumerate(polynomial):
            widened[power + 1] += value / divisor
            widened[power] -= value * point / divisor
        polynomial = widened
    return polynomial


def basis_value(nodes, chosen, where):
    result = 1.0
    for other, point in enumerate(nodes):
        if other != chosen:
            result *= (where - point) / (nodes[chosen] - point)
    return result


def node_tables():
    root = math.sqrt(3.0 / 7.0)
    fine_tau = [0.0, (1.0 - root) / 2.0, 0.5, (1.0 + root) / 2.0, 1.0]
    coarse_tau = [0.0, 0.5, 1.0]
    integ = []
    for j in range(4):
        row_values = []
        for k in range(5):
            polynomial = basis_coefficients(fine_tau, k)
            total = 0.0
            for power, value in enumerate(polynomial):
                total += (
                    value
                    * (fine_tau[j + 1] ** (power + 1) - fine_tau[j] ** (power + 1))
                    / (power + 1)
                )
            row_values.append(total)
        integ.append(row_values)
    interp = [[basis_value(coarse_tau, c, fine_tau[m]) for c in range(3)] for m in range(5)]
    spacing = [float(fine_tau[j + 1] - fine_tau[j]) for j in range(4)]
    return integ, spacing, interp


INTEG, SPACING, INTERP = node_tables()
MIX = [
    [step_length * (INTEG[j][k] - (SPACING[j] if j == k else 0.0)) for k in range(5)]
    for j in range(4)
]
QUAD = [[step_length * (INTEG[2 * c][k] + INTEG[2 * c + 1][k]) for k in range(5)] for c in range(2)]


def hartley(length):
    counter = np.arange(length)
    phase = 2.0 * np.pi * (counter[:, None] * counter[None, :] % length) / length
    return (np.cos(phase) + np.sin(phase)) / math.sqrt(length)


def block_pair(table):
    rows, cols = table.shape
    both = np.zeros((2 * rows, 2 * cols))
    both[:rows, :cols] = table
    both[rows:, cols:] = table
    return both


def tables(planes, rows, cols, depth):
    rows_c, cols_c = rows // 2, cols // 2
    hx, hy, hz = hartley(rows_c), hartley(cols_c), hartley(depth)
    down_y = 0.5 * np.repeat(hy, 2, 0)
    up_y = np.repeat(hy, 2, 0).T
    wide_x = np.repeat(hx, 2, 0)
    down_x = np.zeros((rows_c, planes, planes, rows))
    up_x = np.zeros((planes, rows, rows_c, planes))
    for p in range(planes):
        down_x[:, p, p, :] = 0.25 * wide_x.T
        up_x[p, :, :, p] = wide_x
    down_x = down_x.reshape(rows_c * planes, planes * rows)
    up_x = up_x.reshape(planes * rows, rows_c * planes)
    cos_z = np.cos(2.0 * np.pi * np.arange(depth) / depth)
    cos_y = np.cos(2.0 * np.pi * np.arange(cols_c) / cols_c)
    half = 0.5 * step_length * diffusion * 0.25
    denom = 1.0 - half * (2.0 * cos_z[:, None] + 2.0 * cos_y[None, :] - 6.0)
    denom = np.concatenate([denom, denom], 1)
    shift_x = half * 2.0 * np.cos(2.0 * np.pi * np.arange(rows_c) / rows_c)
    inverse_z = hz.reshape(4, 2, 2, planes, depth).transpose(1, 0, 2, 3, 4)
    inverse_z = inverse_z.reshape(2, 8 * planes, depth)
    f32 = lambda a: jnp.asarray(a, jnp.float32)
    return (
        f32(block_pair(down_y)), f32(down_x), f32(hz), f32(inverse_z), f32(denom), f32(shift_x),
        f32(up_x), f32(block_pair(up_y)),
    )


def dot(a, b):
    return jnp.dot(a, b, precision=lax.Precision.HIGHEST, preferred_element_type=jnp.float32)


def plane_part(f):
    near = pltpu.roll(f, 1, 0) + pltpu.roll(f, f.shape[0] - 1, 0)
    near = near + pltpu.roll(f, 1, 1) + pltpu.roll(f, f.shape[1] - 1, 1)
    return diffusion * near - f * ((6.0 * diffusion - reaction) + reaction * (f * f))


def old_kernel(place, u, g, near, far):
    planes = u.shape[1]
    core = place[1]

    for p in range(planes):
        total = [None] * 4
        for k in range(5):
            field = u[k, p]
            force = plane_part(field)
            if p > 0:
                force = force + diffusion * u[k, p - 1]
            if p < planes - 1:
                force = force + diffusion * u[k, p + 1]
            for j in range(4):
                term = MIX[j][k] * force
                total[j] = term if total[j] is None else total[j] + term
        for j in range(4):
            g[j, p] = total[j]

    def packed(out, plane_of):
        for j in range(4):
            for i in range(4 - j):
                out[G_AT[j] + i] = g[j, plane_of(i)]
            edge = plane_of(0)
            out[U_AT + j] = diffusion * sum(MIX[j][k] * u[k, edge] for k in range(5))

    top = lambda i: planes - 1 - i
    bottom = lambda i: i

    @pl.when(core == 0)
    def _():
        packed(near, top)
        packed(far, bottom)

    @pl.when(core != 0)
    def _():
        packed(near, bottom)
        packed(far, top)


def sweep_kernel(
    place, first, previous, start_near, start_far, g, own_near, own_far, got_near, got_far,
    down_y, down_x, w, send, hats, quad,
):
    planes = first.shape[0]
    coarse = planes // 2
    position, core = place[0], place[1]

    def with_sides(body):
        @pl.when(core == 0)
        def _():
            body(start_far, own_far, got_far, start_near, own_near, got_near)

        @pl.when(core != 0)
        def _():
            body(start_near, own_near, got_near, start_far, own_far, got_far)

    @pl.when(position == 0)
    def _():
        w[0, REACH : REACH + planes] = first[...]

    @pl.when(position != 0)
    def _():
        w[0, REACH : REACH + planes] = previous[...]

    def run(start_lo, own_lo, got_lo, start_hi, own_hi, got_hi):
        for i in range(REACH):
            w[0, REACH - 1 - i] = start_lo[i]
            w[0, REACH + planes + i] = start_hi[i]
        for m in range(5):
            margin = 4 - m
            held = [None, None]
            for p in range(-margin, planes + margin):
                at = p + REACH
                field = w[m, at]
                force = plane_part(field) + diffusion * (w[m, at - 1] + w[m, at + 1])
                if m < 4:
                    if p < 0:
                        source = got_lo[G_AT[m] - p - 1]
                        if p == -1:
                            source = source + own_lo[U_AT + m]
                    elif p >= planes:
                        source = got_hi[G_AT[m] + p - planes]
                        if p == planes:
                            source = source + own_hi[U_AT + m]
                    else:
                        source = g[m, p]
                        if p == 0:
                            source = source + got_lo[U_AT + m]
                        if p == planes - 1:
                            source = source + got_hi[U_AT + m]
                    w[m + 1, at] = field + step_length * SPACING[m] * force + source
                if 0 <= p < planes:
                    if p % 2 == 0:
                        held = force
                    else:
                        both = held + force
                        for c in range(2):
                            term = QUAD[c][m] * both
                            quad[c, p // 2] = term if m == 0 else quad[c, p // 2] + term

    with_sides(run)

    def paired(m):
        return jnp.concatenate(
            [w[m, REACH + 2 * i] + w[m, REACH + 2 * i + 1] for i in range(coarse)], 0
        )

    rows = coarse * first.shape[1]
    restart = paired(0)
    mask = jnp.where(position == 0, 1.0, 0.0)
    q0 = quad[0].reshape(rows, -1) + mask * restart
    q1 = quad[1].reshape(rows, -1)
    table = down_y[...]
    left = [
        dot(jnp.concatenate(pair, 1), table)
        for pair in ((q0, q1), (paired(2), paired(4)), (restart, restart))
    ]
    spectral = dot(down_x[...], jnp.concatenate(left, 1))
    width = left[0].shape[1]
    for y in range(4):
        for c in range(2):
            kx = 2 * y + c
            block = spectral[kx * coarse : (kx + 1) * coarse, : 2 * width]
            send[4 * y + c] = block
            send[4 * y + 2 + c] = block
    hats[...] = spectral[:, width:]


def lanes_swapped(a):
    return pltpu.roll(a, a.shape[1] // 2, 1)


def left_half(a):
    return lax.broadcasted_iota(jnp.int32, a.shape, 1) < a.shape[1] // 2


def spectrum_kernel(place, shift_x, got, table, denom, lifted, offset, copies):
    depth = table.shape[0]
    half = depth // 2
    d = denom[...] - shift_x[place[4]]
    inv = 1.0 / d
    spectra = dot(table[...], got[...].reshape(depth, -1))
    width = d.shape[1]
    lift = spectra[:, :width] - (1.0 - d) * spectra[:, width:]
    weighted = lift * inv
    weighted = jnp.where(left_half(d), weighted * inv, weighted)
    total = weighted + lanes_swapped(weighted)
    lifted[...] = lift
    offset[...] = total
    packed = jnp.where(left_half(total[:half]), total[:half], total[half:])
    for i in range(copies.shape[0]):
        copies[i] = packed


def scan_kernel(place, shift_x, all_offsets, lifted, offset, denom, inverse_z, out):
    zl, block, zh = place[2], place[3], place[5]
    slices = all_offsets.shape[0]
    half = all_offsets.shape[1]
    d = denom[...] - shift_x[place[4]]
    inv = 1.0 / d
    left = left_half(inv[:half])
    inv_packed = jnp.where(left, inv[:half], inv[half:])
    inv2 = inv_packed * inv_packed
    prefix = jnp.zeros_like(inv2)
    total = jnp.zeros_like(inv2)
    power = jnp.ones_like(inv2)
    whole = jnp.ones_like(inv2)
    for m in range(slices):
        piece = all_offsets[m]
        total = total * inv2 + piece
        prefix = jnp.where(m < zl, prefix * inv2 + piece, prefix)
        power = jnp.where(m < zl, power * inv2, power)
        whole = whole * inv2
    inverse = inverse_z[zh]
    weights = jnp.where(left_half(inv), inv, inv * inv)
    own = jnp.where(left_half(inv), lifted[...] * inv, offset[...])
    carried = total * power
    targets = out.shape[0] // 8
    for xp in range(targets):
        packed = jnp.where(xp == block, prefix, jnp.where(xp > block, carried, 0.0))
        carried = jnp.where(xp > block, carried * whole, carried)
        turned = lanes_swapped(packed)
        begin = jnp.concatenate(
            [jnp.where(left, packed, turned), jnp.where(left, turned, packed)], 0
        )
        later = begin * weights + jnp.where(xp == block, own, 0.0)
        planar = dot(inverse, jnp.concatenate([later, begin], 1))
        out[8 * xp : 8 * xp + 8] = planar.reshape(8, -1, planar.shape[1])


def finish_kernel(place, w, got, hats, up_x, up_y, out):
    planes = out.shape[1]
    coarse = planes // 2
    rows = out.shape[2]
    cols = out.shape[3]
    total = got[0:8] + got[8:16] + (got[16:24] + got[24:32])
    delta = total.reshape(-1, total.shape[2]) - hats[...]
    half = delta.shape[1] // 2
    later = delta[:, :half]
    begin = jnp.where(place[0] == 0, 0.0, delta[:, half:])
    spread = dot(up_x[...], jnp.concatenate([later, begin], 1))
    table = up_y[...]
    after = dot(spread[:, :half], table)
    before = dot(spread[:, half:], table[:, :cols])
    parts = [before, after[:, :cols], after[:, cols:]]
    for m in range(5):
        mixed = None
        for c in range(3):
            weight = INTERP[m][c]
            if abs(weight) < 1e-14:
                continue
            term = parts[c] if weight == 1.0 else weight * parts[c]
            mixed = term if mixed is None else mixed + term
        for i in range(coarse):
            piece = mixed[i * rows : (i + 1) * rows]
            out[m, 2 * i] = w[m, REACH + 2 * i] + piece
            out[m, 2 * i + 1] = w[m, REACH + 2 * i + 1] + piece


def call(kernel, outs, scalars, *args, scratch=()):
    smem = pl.BlockSpec(memory_space=pltpu.SMEM)
    vmem = pl.BlockSpec(memory_space=pltpu.VMEM)
    single = not isinstance(outs, list)
    shapes = [jax.ShapeDtypeStruct(s, jnp.float32) for s in ([outs] if single else outs)]
    result = pl.pallas_call(
        kernel,
        out_shape=shapes[0] if single else shapes,
        in_specs=[smem] * len(scalars) + [vmem] * len(args),
        out_specs=vmem if single else [vmem] * len(shapes),
        scratch_shapes=[pltpu.VMEM(s, jnp.float32) for s in scratch],
        compiler_params=pltpu.CompilerParams(vmem_limit_bytes=32 * 1024 * 1024),
    )(*scalars, *args)
    return result


def shards(u_old, u_init):
    planes, rows, cols = u_init.shape
    coarse, rows_c, cols_c = planes // 2, rows // 2, cols // 2
    slices = lax.axis_size(TM)
    blocks = lax.axis_size(SPACE)
    depth_c = coarse * blocks
    down_y, down_x, table_z, inverse_z, denom, shift_x, up_x, up_y = tables(
        coarse, rows, cols, depth_c
    )
    fine_old = u_old[0]
    position = lax.axis_index(TM)
    core = lax.axis_index("c")
    kx = 2 * lax.axis_index("y") + core
    place = jnp.stack(
        [position, core, lax.axis_index("zl"), lax.axis_index("x"), kx, lax.axis_index("zh")]
    ).astype(jnp.int32)

    last = fine_old[4]
    previous = lax.ppermute(last, TM, [(i, i + 1) for i in range(slices - 1)])

    def far_block(s):
        return (s + 1) % blocks if s % 2 else (s - 1) % blocks

    bottom = lambda a: a[:REACH]
    top = lambda a: a[::-1][:REACH]
    source = jnp.where(position == slices - 1, u_init, last)
    start_out = jnp.where(core == 0, bottom(source), top(source))
    across = [
        (n * blocks + s, (n + 1) % slices * blocks + far_block(s))
        for n in range(slices)
        for s in range(blocks)
    ]
    start_far = lax.ppermute(start_out, TM + SPACE, across)

    g, own_near, own_far = call(
        old_kernel,
        [(4, planes, rows, cols), (PACK, rows, cols), (PACK, rows, cols)],
        [place],
        fine_old,
    )
    got_far = lax.ppermute(own_far, SPACE, [(s, far_block(s)) for s in range(blocks)])
    start = jnp.where(position == 0, u_init, previous)
    start_edge = jnp.where(core == 0, top(start), bottom(start))
    near = lax.ppermute(jnp.concatenate([own_near, start_edge], 0), "c", [(0, 1), (1, 0)])
    got_near, start_near = near[:PACK], near[PACK:]

    w, send, hats = call(
        sweep_kernel,
        [
            (5, planes + 2 * REACH, rows, cols),
            (blocks, coarse, 4 * cols_c),
            (rows_c * coarse, 4 * cols_c),
        ],
        [place],
        u_init, previous, start_near, start_far, g, own_near, own_far, got_near, got_far,
        down_y, down_x,
        scratch=[(2, coarse, rows, cols)],
    )
    columns = lax.all_to_all(send, SPACE, 0, 0, tiled=True)
    packed = (lax.axis_size("zl"), depth_c // 2, 2 * cols_c)
    lifted, offset, copies = call(
        spectrum_kernel,
        [(depth_c, 2 * cols_c), (depth_c, 2 * cols_c), packed],
        [place, shift_x],
        columns, table_z, denom,
    )
    gathered = lax.all_to_all(copies, "zl", 0, 0, tiled=True)
    back = call(
        scan_kernel,
        (4 * rows_c, coarse, 4 * cols_c),
        [place, shift_x],
        gathered, lifted, offset, denom, inverse_z,
    )
    returned = lax.all_to_all(back, ("x", "y", "c"), 0, 0, tiled=True)
    out = call(
        finish_kernel, (5, planes, rows, cols), [place], w, returned, hats, up_x, up_y
    )
    return out[None]


def solution(mesh):
    finer = Mesh(mesh.devices.reshape(4, 8, 4, 2, 2), TM + SPACE)
    in_specs = (P(TM, None, SPACE, None, None), P(SPACE, None, None))
    out_specs = P(TM, None, SPACE, None, None)
    return jax.shard_map(
        shards, mesh=finer, in_specs=in_specs, out_specs=out_specs, check_vma=False
    )
```

```python
import math

import jax
import jax.numpy as jnp
import numpy as np
from jax import lax
from jax.experimental import pallas as pl
from jax.experimental.pallas import tpu as pltpu
from jax.sharding import Mesh
from jax.sharding import PartitionSpec as P

TM = ("x", "zl")
SPACE = ("y", "zh", "c")

step_length = 0.4
diffusion = 1.0
reaction = 1.0

G_AT = (0, 4, 7, 9)
U_AT = 10
PACK = 14
REACH = 5


def basis_coefficients(nodes, chosen):
    polynomial = [1.0]
    for other, point in enumerate(nodes):
        if other == chosen:
            continue
        divisor = nodes[chosen] - point
        widened = [0.0] * (len(polynomial) + 1)
        for power, value in enumerate(polynomial):
            widened[power + 1] += value / divisor
            widened[power] -= value * point / divisor
        polynomial = widened
    return polynomial


def basis_value(nodes, chosen, where):
    result = 1.0
    for other, point in enumerate(nodes):
        if other != chosen:
            result *= (where - point) / (nodes[chosen] - point)
    return result


def node_tables():
    root = math.sqrt(3.0 / 7.0)
    fine_tau = [0.0, (1.0 - root) / 2.0, 0.5, (1.0 + root) / 2.0, 1.0]
    coarse_tau = [0.0, 0.5, 1.0]
    integ = []
    for j in range(4):
        row_values = []
        for k in range(5):
            polynomial = basis_coefficients(fine_tau, k)
            total = 0.0
            for power, value in enumerate(polynomial):
                total += (
                    value
                    * (fine_tau[j + 1] ** (power + 1) - fine_tau[j] ** (power + 1))
                    / (power + 1)
                )
            row_values.append(total)
        integ.append(row_values)
    interp = [[basis_value(coarse_tau, c, fine_tau[m]) for c in range(3)] for m in range(5)]
    spacing = [float(fine_tau[j + 1] - fine_tau[j]) for j in range(4)]
    return integ, spacing, interp


INTEG, SPACING, INTERP = node_tables()
MIX = [
    [step_length * (INTEG[j][k] - (SPACING[j] if j == k else 0.0)) for k in range(5)]
    for j in range(4)
]
QUAD = [[step_length * (INTEG[2 * c][k] + INTEG[2 * c + 1][k]) for k in range(5)] for c in range(2)]


def hartley(length):
    counter = np.arange(length)
    phase = 2.0 * np.pi * (counter[:, None] * counter[None, :] % length) / length
    return (np.cos(phase) + np.sin(phase)) / math.sqrt(length)


def block_pair(table):
    rows, cols = table.shape
    both = np.zeros((2 * rows, 2 * cols))
    both[:rows, :cols] = table
    both[rows:, cols:] = table
    return both


def tables(planes, rows, cols, depth):
    rows_c, cols_c = rows // 2, cols // 2
    hx, hy, hz = hartley(rows_c), hartley(cols_c), hartley(depth)
    down_y = 0.5 * np.repeat(hy, 2, 0)
    up_y = np.repeat(hy, 2, 0).T
    wide_x = np.repeat(hx, 2, 0)
    down_x = np.zeros((rows_c, planes, planes, rows))
    up_x = np.zeros((planes, rows, rows_c, planes))
    for p in range(planes):
        down_x[:, p, p, :] = 0.25 * wide_x.T
        up_x[p, :, :, p] = wide_x
    down_x = down_x.reshape(rows_c * planes, planes * rows)
    up_x = up_x.reshape(planes * rows, rows_c * planes)
    cos_z = np.cos(2.0 * np.pi * np.arange(depth) / depth)
    cos_y = np.cos(2.0 * np.pi * np.arange(cols_c) / cols_c)
    half = 0.5 * step_length * diffusion * 0.25
    denom = 1.0 - half * (2.0 * cos_z[:, None] + 2.0 * cos_y[None, :] - 6.0)
    denom = np.concatenate([denom, denom], 1)
    shift_x = half * 2.0 * np.cos(2.0 * np.pi * np.arange(rows_c) / rows_c)
    inverse_z = hz.reshape(4, 2, 2, planes, depth).transpose(1, 0, 2, 3, 4)
    inverse_z = inverse_z.reshape(2, 8 * planes, depth)
    f32 = lambda a: jnp.asarray(a, jnp.float32)
    return (
        f32(block_pair(down_y)), f32(down_x), f32(hz), f32(inverse_z), f32(denom), f32(shift_x),
        f32(up_x), f32(block_pair(up_y)),
    )


def dot(a, b):
    return jnp.dot(a, b, precision=lax.Precision.HIGHEST, preferred_element_type=jnp.float32)


def plane_part(f):
    near = pltpu.roll(f, 1, 0) + pltpu.roll(f, f.shape[0] - 1, 0)
    near = near + pltpu.roll(f, 1, 1) + pltpu.roll(f, f.shape[1] - 1, 1)
    return diffusion * near - f * ((6.0 * diffusion - reaction) + reaction * (f * f))


def old_kernel(place, u, g, near, far):
    planes = u.shape[1]
    core = place[1]

    for p in range(planes):
        total = [None] * 4
        for k in range(5):
            field = u[k, p]
            force = plane_part(field)
            if p > 0:
                force = force + diffusion * u[k, p - 1]
            if p < planes - 1:
                force = force + diffusion * u[k, p + 1]
            for j in range(4):
                term = MIX[j][k] * force
                total[j] = term if total[j] is None else total[j] + term
        for j in range(4):
            g[j, p] = total[j]

    def packed(out, plane_of):
        for j in range(4):
            for i in range(4 - j):
                out[G_AT[j] + i] = g[j, plane_of(i)]
            edge = plane_of(0)
            out[U_AT + j] = diffusion * sum(MIX[j][k] * u[k, edge] for k in range(5))

    top = lambda i: planes - 1 - i
    bottom = lambda i: i

    @pl.when(core == 0)
    def _():
        packed(near, top)
        packed(far, bottom)

    @pl.when(core != 0)
    def _():
        packed(near, bottom)
        packed(far, top)


def edge_planes(out, at, field, core, low):
    planes = field.shape[0]

    @pl.when((core == 0) == low)
    def _():
        for i in range(REACH):
            out[at + i] = field[i]

    @pl.when((core == 0) != low)
    def _():
        for i in range(REACH):
            out[at + i] = field[planes - 1 - i]


def last_kernel(place, u, first, last, start_out):
    position, core, slices = place[0], place[1], place[6]
    last[...] = u[0, 0]

    @pl.when(position == slices - 1)
    def _():
        edge_planes(start_out, 0, first, core, True)

    @pl.when(position != slices - 1)
    def _():
        edge_planes(start_out, 0, last, core, True)


def relay_kernel(got, out):
    out[...] = got[...]


def near_kernel(place, first, previous, own_near, out):
    position, core = place[0], place[1]
    out[:PACK] = own_near[...]

    @pl.when(position == 0)
    def _():
        edge_planes(out, PACK, first, core, False)

    @pl.when(position != 0)
    def _():
        edge_planes(out, PACK, previous, core, False)


def sweep_kernel(
    place, first, previous, near, start_far, g, own_near, own_far, got_far,
    down_y, down_x, w, send, hats, quad,
):
    got_near, start_near = near.at[:PACK], near.at[PACK:]
    planes = first.shape[0]
    coarse = planes // 2
    position, core = place[0], place[1]

    def with_sides(body):
        @pl.when(core == 0)
        def _():
            body(start_far, own_far, got_far, start_near, own_near, got_near)

        @pl.when(core != 0)
        def _():
            body(start_near, own_near, got_near, start_far, own_far, got_far)

    @pl.when(position == 0)
    def _():
        w[0, REACH : REACH + planes] = first[...]

    @pl.when(position != 0)
    def _():
        w[0, REACH : REACH + planes] = previous[...]

    def run(start_lo, own_lo, got_lo, start_hi, own_hi, got_hi):
        for i in range(REACH):
            w[0, REACH - 1 - i] = start_lo[i]
            w[0, REACH + planes + i] = start_hi[i]
        for m in range(5):
            margin = 4 - m
            held = [None, None]
            for p in range(-margin, planes + margin):
                at = p + REACH
                field = w[m, at]
                force = plane_part(field) + diffusion * (w[m, at - 1] + w[m, at + 1])
                if m < 4:
                    if p < 0:
                        source = got_lo[G_AT[m] - p - 1]
                        if p == -1:
                            source = source + own_lo[U_AT + m]
                    elif p >= planes:
                        source = got_hi[G_AT[m] + p - planes]
                        if p == planes:
                            source = source + own_hi[U_AT + m]
                    else:
                        source = g[m, p]
                        if p == 0:
                            source = source + got_lo[U_AT + m]
                        if p == planes - 1:
                            source = source + got_hi[U_AT + m]
                    w[m + 1, at] = field + step_length * SPACING[m] * force + source
                if 0 <= p < planes:
                    if p % 2 == 0:
                        held = force
                    else:
                        both = held + force
                        for c in range(2):
                            term = QUAD[c][m] * both
                            quad[c, p // 2] = term if m == 0 else quad[c, p // 2] + term

    with_sides(run)

    def paired(m):
        return jnp.concatenate(
            [w[m, REACH + 2 * i] + w[m, REACH + 2 * i + 1] for i in range(coarse)], 0
        )

    rows = coarse * first.shape[1]
    restart = paired(0)
    mask = jnp.where(position == 0, 1.0, 0.0)
    q0 = quad[0].reshape(rows, -1) + mask * restart
    q1 = quad[1].reshape(rows, -1)
    table = down_y[...]
    left = [
        dot(jnp.concatenate(pair, 1), table)
        for pair in ((q0, q1), (paired(2), paired(4)), (restart, restart))
    ]
    spectral = dot(down_x[...], jnp.concatenate(left, 1))
    width = left[0].shape[1]
    for y in range(4):
        for c in range(2):
            kx = 2 * y + c
            block = spectral[kx * coarse : (kx + 1) * coarse, : 2 * width]
            send[4 * y + c] = block
            send[4 * y + 2 + c] = block
    hats[...] = spectral[:, width:]


def lanes_swapped(a):
    return pltpu.roll(a, a.shape[1] // 2, 1)


def left_half(a):
    return lax.broadcasted_iota(jnp.int32, a.shape, 1) < a.shape[1] // 2


def spectrum_kernel(place, shift_x, got, table, denom, lifted, offset, copies):
    depth = table.shape[0]
    half = depth // 2
    d = denom[...] - shift_x[place[4]]
    inv = 1.0 / d
    spectra = dot(table[...], got[...].reshape(depth, -1))
    width = d.shape[1]
    lift = spectra[:, :width] - (1.0 - d) * spectra[:, width:]
    weighted = lift * inv
    weighted = jnp.where(left_half(d), weighted * inv, weighted)
    total = weighted + lanes_swapped(weighted)
    lifted[...] = lift
    offset[...] = total
    packed = jnp.where(left_half(total[:half]), total[:half], total[half:])
    for i in range(copies.shape[0]):
        copies[i] = packed


def scan_kernel(place, shift_x, all_offsets, lifted, offset, denom, inverse_z, out):
    zl, block, zh = place[2], place[3], place[5]
    slices = all_offsets.shape[0]
    half = all_offsets.shape[1]
    d = denom[...] - shift_x[place[4]]
    inv = 1.0 / d
    left = left_half(inv[:half])
    inv_packed = jnp.where(left, inv[:half], inv[half:])
    inv2 = inv_packed * inv_packed
    prefix = jnp.zeros_like(inv2)
    total = jnp.zeros_like(inv2)
    power = jnp.ones_like(inv2)
    whole = jnp.ones_like(inv2)
    for m in range(slices):
        piece = all_offsets[m]
        total = total * inv2 + piece
        prefix = jnp.where(m < zl, prefix * inv2 + piece, prefix)
        power = jnp.where(m < zl, power * inv2, power)
        whole = whole * inv2
    inverse = inverse_z[zh]
    weights = jnp.where(left_half(inv), inv, inv * inv)
    own = jnp.where(left_half(inv), lifted[...] * inv, offset[...])
    carried = total * power
    targets = out.shape[0] // 8
    for xp in range(targets):
        packed = jnp.where(xp == block, prefix, jnp.where(xp > block, carried, 0.0))
        carried = jnp.where(xp > block, carried * whole, carried)
        turned = lanes_swapped(packed)
        begin = jnp.concatenate(
            [jnp.where(left, packed, turned), jnp.where(left, turned, packed)], 0
        )
        later = begin * weights + jnp.where(xp == block, own, 0.0)
        planar = dot(inverse, jnp.concatenate([later, begin], 1))
        out[8 * xp : 8 * xp + 8] = planar.reshape(8, -1, planar.shape[1])


def finish_kernel(place, w, got, hats, up_x, up_y, out):
    planes = out.shape[1]
    coarse = planes // 2
    rows = out.shape[2]
    cols = out.shape[3]
    total = got[0:8] + got[8:16] + (got[16:24] + got[24:32])
    delta = total.reshape(-1, total.shape[2]) - hats[...]
    half = delta.shape[1] // 2
    later = delta[:, :half]
    begin = jnp.where(place[0] == 0, 0.0, delta[:, half:])
    spread = dot(up_x[...], jnp.concatenate([later, begin], 1))
    table = up_y[...]
    after = dot(spread[:, :half], table)
    before = dot(spread[:, half:], table[:, :cols])
    parts = [before, after[:, :cols], after[:, cols:]]
    for m in range(5):
        mixed = None
        for c in range(3):
            weight = INTERP[m][c]
            if abs(weight) < 1e-14:
                continue
            term = parts[c] if weight == 1.0 else weight * parts[c]
            mixed = term if mixed is None else mixed + term
        for i in range(coarse):
            piece = mixed[i * rows : (i + 1) * rows]
            out[m, 2 * i] = w[m, REACH + 2 * i] + piece
            out[m, 2 * i + 1] = w[m, REACH + 2 * i + 1] + piece


def call(kernel, outs, scalars, *args, scratch=(), flops=0, blocked={}):
    smem = pl.BlockSpec(memory_space=pltpu.SMEM)
    vmem = pl.BlockSpec(memory_space=pltpu.VMEM)
    single = not isinstance(outs, list)
    shapes = [jax.ShapeDtypeStruct(s, jnp.float32) for s in ([outs] if single else outs)]
    result = pl.pallas_call(
        kernel,
        grid=(1,) if blocked else (),
        out_shape=shapes[0] if single else shapes,
        in_specs=[
            smem if i < len(scalars) else blocked.get(i, vmem)
            for i in range(len(scalars) + len(args))
        ],
        out_specs=vmem if single else [vmem] * len(shapes),
        scratch_shapes=[pltpu.VMEM(s, jnp.float32) for s in scratch],
        compiler_params=pltpu.CompilerParams(vmem_limit_bytes=32 * 1024 * 1024),
        cost_estimate=pl.CostEstimate(flops=flops, bytes_accessed=1 << 20, transcendentals=0),
    )(*scalars, *args)
    return result


def shards(u_old, u_init):
    planes, rows, cols = u_init.shape
    coarse, rows_c, cols_c = planes // 2, rows // 2, cols // 2
    slices = lax.axis_size(TM)
    blocks = lax.axis_size(SPACE)
    depth_c = coarse * blocks
    down_y, down_x, table_z, inverse_z, denom, shift_x, up_x, up_y = tables(
        coarse, rows, cols, depth_c
    )
    position = lax.axis_index(TM)
    core = lax.axis_index("c")
    kx = 2 * lax.axis_index("y") + core
    place = [position, core, lax.axis_index("zl"), lax.axis_index("x"), kx]
    place = jnp.stack(place + [lax.axis_index("zh"), slices]).astype(jnp.int32)

    last, start_out = call(
        last_kernel,
        [(planes, rows, cols), (REACH, rows, cols)],
        [place],
        u_old, u_init,
        blocked={1: pl.BlockSpec((1, 1, planes, rows, cols), lambda i: (0, 4, 0, 0, 0))},
    )

    def far_block(s):
        return (s + 1) % blocks if s % 2 else (s - 1) % blocks

    across = [
        (n * blocks + s, (n + 1) % slices * blocks + far_block(s))
        for n in range(slices)
        for s in range(blocks)
    ]
    start_far = lax.ppermute(start_out, TM + SPACE, across)
    previous = lax.ppermute(last, TM, [(i, i + 1) for i in range(slices - 1)])
    g, own_near, own_far = call(
        old_kernel,
        [(4, planes, rows, cols), (PACK, rows, cols), (PACK, rows, cols)],
        [place],
        u_old[0],
        flops=10**11,
    )
    start_far = call(relay_kernel, start_far.shape, [], start_far, flops=10**11)
    got_far = lax.ppermute(own_far, SPACE, [(s, far_block(s)) for s in range(blocks)])
    near_out = call(
        near_kernel, (PACK + REACH, rows, cols), [place], u_init, previous, own_near
    )
    near = lax.ppermute(near_out, "c", [(0, 1), (1, 0)])

    w, send, hats = call(
        sweep_kernel,
        [
            (5, planes + 2 * REACH, rows, cols),
            (blocks, coarse, 4 * cols_c),
            (rows_c * coarse, 4 * cols_c),
        ],
        [place],
        u_init, previous, near, start_far, g, own_near, own_far, got_far,
        down_y, down_x,
        scratch=[(2, coarse, rows, cols)],
    )
    columns = lax.all_to_all(send, SPACE, 0, 0, tiled=True)
    packed = (lax.axis_size("zl"), depth_c // 2, 2 * cols_c)
    lifted, offset, copies = call(
        spectrum_kernel,
        [(depth_c, 2 * cols_c), (depth_c, 2 * cols_c), packed],
        [place, shift_x],
        columns, table_z, denom,
    )
    gathered = lax.all_to_all(copies, "zl", 0, 0, tiled=True)
    back = call(
        scan_kernel,
        (4 * rows_c, coarse, 4 * cols_c),
        [place, shift_x],
        gathered, lifted, offset, denom, inverse_z,
    )
    returned = lax.all_to_all(back, ("x", "y", "c"), 0, 0, tiled=True)
    out = call(
        finish_kernel, (5, planes, rows, cols), [place], w, returned, hats, up_x, up_y
    )
    return out[None]


def solution(mesh):
    finer = Mesh(mesh.devices.reshape(4, 8, 4, 2, 2), TM + SPACE)
    in_specs = (P(TM, None, SPACE, None, None), P(SPACE, None, None))
    out_specs = P(TM, None, SPACE, None, None)
    return jax.shard_map(
        shards, mesh=finer, in_specs=in_specs, out_specs=out_specs, check_vma=False
    )
```

```python
import math

import jax
import jax.numpy as jnp
import numpy as np
from jax import lax
from jax.experimental import pallas as pl
from jax.experimental.pallas import tpu as pltpu
from jax.sharding import Mesh
from jax.sharding import PartitionSpec as P

TM = ("x", "zl")
SPACE = ("y", "zh", "c")

step_length = 0.4
diffusion = 1.0
reaction = 1.0

G_AT = (0, 3, 5, 6)
U_AT = 6
PACK = 10
REACH = 4


def basis_coefficients(nodes, chosen):
    polynomial = [1.0]
    for other, point in enumerate(nodes):
        if other == chosen:
            continue
        divisor = nodes[chosen] - point
        widened = [0.0] * (len(polynomial) + 1)
        for power, value in enumerate(polynomial):
            widened[power + 1] += value / divisor
            widened[power] -= value * point / divisor
        polynomial = widened
    return polynomial


def basis_value(nodes, chosen, where):
    result = 1.0
    for other, point in enumerate(nodes):
        if other != chosen:
            result *= (where - point) / (nodes[chosen] - point)
    return result


def node_tables():
    root = math.sqrt(3.0 / 7.0)
    fine_tau = [0.0, (1.0 - root) / 2.0, 0.5, (1.0 + root) / 2.0, 1.0]
    coarse_tau = [0.0, 0.5, 1.0]
    integ = []
    for j in range(4):
        row_values = []
        for k in range(5):
            polynomial = basis_coefficients(fine_tau, k)
            total = 0.0
            for power, value in enumerate(polynomial):
                total += (
                    value
                    * (fine_tau[j + 1] ** (power + 1) - fine_tau[j] ** (power + 1))
                    / (power + 1)
                )
            row_values.append(total)
        integ.append(row_values)
    interp = [[basis_value(coarse_tau, c, fine_tau[m]) for c in range(3)] for m in range(5)]
    spacing = [float(fine_tau[j + 1] - fine_tau[j]) for j in range(4)]
    return integ, spacing, interp


INTEG, SPACING, INTERP = node_tables()
MIX = [
    [step_length * (INTEG[j][k] - (SPACING[j] if j == k else 0.0)) for k in range(5)]
    for j in range(4)
]
COUPLING = 0.5 * step_length * diffusion * 0.25
QUAD = [[step_length * (INTEG[2 * c][k] + INTEG[2 * c + 1][k]) for k in range(5)] for c in range(2)]


def hartley(length):
    counter = np.arange(length)
    phase = 2.0 * np.pi * (counter[:, None] * counter[None, :] % length) / length
    return (np.cos(phase) + np.sin(phase)) / math.sqrt(length)


def block_pair(table):
    rows, cols = table.shape
    both = np.zeros((2 * rows, 2 * cols))
    both[:rows, :cols] = table
    both[rows:, cols:] = table
    return both


def tables(planes, rows, cols, depth):
    rows_c, cols_c = rows // 2, cols // 2
    hx, hy, hz = hartley(rows_c), hartley(cols_c), hartley(depth)
    down_y = 0.5 * np.repeat(hy, 2, 0)
    up_y = np.repeat(hy, 2, 0).T
    wide_x = np.repeat(hx, 2, 0)
    down_x = np.zeros((rows_c, planes, planes, rows))
    up_x = np.zeros((planes, rows, rows_c, planes))
    for p in range(planes):
        down_x[:, p, p, :] = 0.25 * wide_x.T
        up_x[p, :, :, p] = wide_x
    down_x = down_x.reshape(rows_c * planes, planes * rows)
    up_x = up_x.reshape(planes * rows, rows_c * planes)
    cos_z = np.cos(2.0 * np.pi * np.arange(depth) / depth)
    cos_y = np.cos(2.0 * np.pi * np.arange(cols_c) / cols_c)
    half = COUPLING
    cos_x = np.cos(2.0 * np.pi * np.arange(rows_c) / rows_c)
    stencil = half * (6.0 - 2.0 * cos_x[:, None, None] - 2.0 * cos_y[None, None, :])
    stencil = np.broadcast_to(stencil, (rows_c, planes, cols_c)).reshape(-1, cols_c)
    stencil = np.concatenate([stencil, stencil], 1)
    blocks = depth // planes
    forward_z = np.zeros((depth, blocks, 2, planes))
    forward_z[:, :, 0, :] = hz.reshape(depth, blocks, planes)
    for s in range(blocks):
        forward_z[:, s, 1, 0] = hz[:, (s * planes - 1) % depth]
        forward_z[:, s, 1, planes - 1] = hz[:, (s * planes + planes) % depth]
    forward_z = forward_z.reshape(depth, -1)
    denom = 1.0 - half * (2.0 * cos_z[:, None] + 2.0 * cos_y[None, :] - 6.0)
    denom = np.concatenate([denom, denom], 1)
    shift_x = half * 2.0 * cos_x
    inverse_z = hz.reshape(4, 2, 2, planes, depth).transpose(1, 0, 2, 3, 4)
    inverse_z = inverse_z.reshape(2, 8 * planes, depth)
    f32 = lambda a: jnp.asarray(a, jnp.float32)
    return (
        f32(block_pair(down_y)), f32(down_x), f32(stencil), f32(forward_z), f32(inverse_z),
        f32(denom), f32(shift_x), f32(up_x), f32(block_pair(up_y)),
    )


def lanes_swapped(a):
    return pltpu.roll(a, a.shape[1] // 2, 1)


def left_half(a):
    return lax.broadcasted_iota(jnp.int32, a.shape, 1) < a.shape[1] // 2


def dot(a, b):
    return jnp.dot(a, b, precision=lax.Precision.HIGHEST, preferred_element_type=jnp.float32)


def plane_part(f):
    near = pltpu.roll(f, 1, 0) + pltpu.roll(f, f.shape[0] - 1, 0)
    near = near + pltpu.roll(f, 1, 1) + pltpu.roll(f, f.shape[1] - 1, 1)
    return diffusion * near - f * ((6.0 * diffusion - reaction) + reaction * (f * f))


def old_kernel(place, u, g, near, far):
    planes = u.shape[1]
    core = place[1]

    for p in range(planes):
        total = [None] * 4
        for k in range(5):
            field = u[k, p]
            force = plane_part(field)
            if p > 0:
                force = force + diffusion * u[k, p - 1]
            if p < planes - 1:
                force = force + diffusion * u[k, p + 1]
            for j in range(4):
                term = MIX[j][k] * force
                total[j] = term if total[j] is None else total[j] + term
        for j in range(4):
            g[j, p] = total[j]

    def packed(out, plane_of):
        for j in range(4):
            for i in range(3 - j):
                out[G_AT[j] + i] = g[j, plane_of(i)]
            edge = plane_of(0)
            out[U_AT + j] = diffusion * sum(MIX[j][k] * u[k, edge] for k in range(5))

    top = lambda i: planes - 1 - i
    bottom = lambda i: i

    @pl.when(core == 0)
    def _():
        packed(near, top)
        packed(far, bottom)

    @pl.when(core != 0)
    def _():
        packed(near, bottom)
        packed(far, top)


def last_kernel(place, u, first, last, start_out, sems):
    position, core, slices = place[0], place[1], place[6]
    planes = last.shape[0]
    edge = pl.ds(core * (planes - REACH), REACH)
    whole = pltpu.make_async_copy(u.at[0, 4], last, sems.at[0])
    whole.start()

    @pl.when(position == slices - 1)
    def _():
        part = pltpu.make_async_copy(first.at[edge], start_out, sems.at[1])
        part.start()
        part.wait()

    @pl.when(position != slices - 1)
    def _():
        part = pltpu.make_async_copy(u.at[0, 4, edge], start_out, sems.at[1])
        part.start()
        part.wait()

    whole.wait()


def relay_kernel(got, out):
    out[...] = got[...]


def near_kernel(place, first, previous, own_near, out):
    position, core = place[0], place[1]
    edge = pl.ds((1 - core) * (first.shape[0] - REACH), REACH)
    out[:PACK] = own_near[...]

    @pl.when(position == 0)
    def _():
        out[PACK:] = first[edge]

    @pl.when(position != 0)
    def _():
        out[PACK:] = previous[edge]


def sweep_kernel(
    place, first, previous, near, start_far, g, own_near, own_far, got_far,
    down_y, down_x, stencil, w, send, hats, quad,
):
    got_near, start_near = near.at[:PACK], near.at[PACK:]
    planes = first.shape[0]
    coarse = planes // 2
    position, core = place[0], place[1]

    def with_sides(body):
        @pl.when(core == 0)
        def _():
            body(start_far, own_far, got_far, start_near, own_near, got_near)

        @pl.when(core != 0)
        def _():
            body(start_near, own_near, got_near, start_far, own_far, got_far)

    @pl.when(position == 0)
    def _():
        w[0, REACH : REACH + planes] = first[...]

    @pl.when(position != 0)
    def _():
        w[0, REACH : REACH + planes] = previous[...]

    def run(start_lo, own_lo, got_lo, start_hi, own_hi, got_hi):
        w[0, :REACH] = start_lo[...]
        w[0, REACH + planes :] = start_hi[...]
        for m in range(5):
            margin = max(3 - m, 0)
            held = None
            for p in range(-margin, planes + margin):
                at = p + REACH
                field = w[m, at]
                force = plane_part(field)
                if m < 4 or p > 0:
                    force = force + diffusion * w[m, at - 1]
                if m < 4 or p < planes - 1:
                    force = force + diffusion * w[m, at + 1]
                if m < 4:
                    if p < 0:
                        source = got_lo[G_AT[m] - p - 1]
                        if p == -1:
                            source = source + own_lo[U_AT + m]
                    elif p >= planes:
                        source = got_hi[G_AT[m] + p - planes]
                        if p == planes:
                            source = source + own_hi[U_AT + m]
                    else:
                        source = g[m, p]
                        if p == 0:
                            source = source + got_lo[U_AT + m]
                        if p == planes - 1:
                            source = source + got_hi[U_AT + m]
                    w[m + 1, at] = field + step_length * SPACING[m] * force + source
                if 0 <= p < planes:
                    if p % 2 == 0:
                        held = force
                    else:
                        both = held + force
                        for c in range(2):
                            term = QUAD[c][m] * both
                            quad[c, p // 2] = term if m == 0 else quad[c, p // 2] + term

    with_sides(run)

    def paired(m):
        return jnp.concatenate(
            [w[m, REACH + 2 * i] + w[m, REACH + 2 * i + 1] for i in range(coarse)], 0
        )

    rows = coarse * first.shape[1]
    restart = paired(0)
    mask = jnp.where(position == 0, 1.0, 0.0)
    q0 = quad[0].reshape(rows, -1) + mask * restart
    q1 = quad[1].reshape(rows, -1)
    table = down_y[...]
    edge_rows = first.shape[1]
    middle = jnp.zeros((rows - 2 * edge_rows, first.shape[2]), jnp.float32)
    edges = jnp.concatenate([w[4, REACH], middle, w[4, REACH + planes - 1]], 0)
    left = [
        dot(jnp.concatenate(pair, 1), table)
        for pair in ((q0, q1), (paired(2), paired(4)), (restart, edges))
    ]
    spectral = dot(down_x[...], jnp.concatenate(left, 1))
    width = left[0].shape[1]
    states = spectral[:, width : 2 * width]
    third = spectral[:, 2 * width :]
    count = spectral.shape[0]
    level = lax.broadcasted_iota(jnp.int32, states.shape, 0) % coarse
    near_z = jnp.where(level > 0, pltpu.roll(states, 1, 0), 0.0)
    near_z = near_z + jnp.where(level < coarse - 1, pltpu.roll(states, count - 1, 0), 0.0)
    inside = spectral[:, :width] + stencil[...] * states - COUPLING * near_z
    is_left = left_half(states)
    last = jnp.where(is_left, lanes_swapped(third), third)
    last = last * jnp.where(is_left, diffusion * QUAD[0][4], diffusion * QUAD[1][4])
    spill = last - COUPLING * states
    spill = jnp.where((level == 0) | (level == coarse - 1), spill, 0.0)
    for y in range(4):
        for c in range(2):
            kx = 2 * y + c
            span = slice(kx * coarse, (kx + 1) * coarse)
            for zh in range(2):
                send[4 * y + 2 * zh + c, :coarse] = inside[span]
                send[4 * y + 2 * zh + c, coarse:] = spill[span]
    hats[...] = spectral[:, width:]


def spectrum_kernel(place, shift_x, got, table, denom, lifted, offset, copies):
    depth = table.shape[0]
    half = depth // 2
    d = denom[...] - shift_x[place[4]]
    inv = 1.0 / d
    lift = dot(table[...], got[...].reshape(-1, d.shape[1]))
    weighted = lift * inv
    weighted = jnp.where(left_half(d), weighted * inv, weighted)
    total = weighted + lanes_swapped(weighted)
    lifted[...] = lift
    offset[...] = total
    packed = jnp.where(left_half(total[:half]), total[:half], total[half:])
    for i in range(copies.shape[0]):
        copies[i] = packed


def scan_kernel(place, shift_x, all_offsets, lifted, offset, denom, inverse_z, out):
    zl, block, zh = place[2], place[3], place[5]
    slices = all_offsets.shape[0]
    half = all_offsets.shape[1]
    d = denom[...] - shift_x[place[4]]
    inv = 1.0 / d
    left = left_half(inv[:half])
    inv_packed = jnp.where(left, inv[:half], inv[half:])
    inv2 = inv_packed * inv_packed
    prefix = jnp.zeros_like(inv2)
    total = jnp.zeros_like(inv2)
    power = jnp.ones_like(inv2)
    whole = jnp.ones_like(inv2)
    for m in range(slices):
        piece = all_offsets[m]
        total = total * inv2 + piece
        prefix = jnp.where(m < zl, prefix * inv2 + piece, prefix)
        power = jnp.where(m < zl, power * inv2, power)
        whole = whole * inv2
    inverse = inverse_z[zh]
    weights = jnp.where(left_half(inv), inv, inv * inv)
    own = jnp.where(left_half(inv), lifted[...] * inv, offset[...])
    carried = total * power
    targets = out.shape[0] // 8
    for xp in range(targets):
        packed = jnp.where(xp == block, prefix, jnp.where(xp > block, carried, 0.0))
        carried = jnp.where(xp > block, carried * whole, carried)
        turned = lanes_swapped(packed)
        begin = jnp.concatenate(
            [jnp.where(left, packed, turned), jnp.where(left, turned, packed)], 0
        )
        later = begin * weights + jnp.where(xp == block, own, 0.0)
        planar = dot(inverse, jnp.concatenate([later, begin], 1))
        out[8 * xp : 8 * xp + 8] = planar.reshape(8, -1, planar.shape[1])


def finish_kernel(place, w, got, hats, up_x, up_y, out):
    planes = out.shape[1]
    coarse = planes // 2
    rows = out.shape[2]
    cols = out.shape[3]
    total = got[0:8] + got[8:16] + (got[16:24] + got[24:32])
    delta = total.reshape(-1, total.shape[2]) - hats[...]
    half = delta.shape[1] // 2
    later = delta[:, :half]
    begin = jnp.where(place[0] == 0, 0.0, delta[:, half:])
    spread = dot(up_x[...], jnp.concatenate([later, begin], 1))
    table = up_y[...]
    after = dot(spread[:, :half], table)
    before = dot(spread[:, half:], table[:, :cols])
    parts = [before, after[:, :cols], after[:, cols:]]
    for m in range(5):
        mixed = None
        for c in range(3):
            weight = INTERP[m][c]
            if abs(weight) < 1e-14:
                continue
            term = parts[c] if weight == 1.0 else weight * parts[c]
            mixed = term if mixed is None else mixed + term
        for i in range(coarse):
            piece = mixed[i * rows : (i + 1) * rows]
            out[m, 2 * i] = w[m, REACH + 2 * i] + piece
            out[m, 2 * i + 1] = w[m, REACH + 2 * i + 1] + piece


def call(kernel, outs, scalars, *args, scratch=(), flops=0, in_hbm=False):
    smem = pl.BlockSpec(memory_space=pltpu.SMEM)
    vmem = pl.BlockSpec(memory_space=pltpu.VMEM)
    hbm = pl.BlockSpec(memory_space=pltpu.HBM)
    single = not isinstance(outs, list)
    shapes = [jax.ShapeDtypeStruct(s, jnp.float32) for s in ([outs] if single else outs)]
    result = pl.pallas_call(
        kernel,
        out_shape=shapes[0] if single else shapes,
        in_specs=[smem] * len(scalars) + [hbm if in_hbm else vmem] * len(args),
        out_specs=vmem if single else [vmem] * len(shapes),
        scratch_shapes=list(scratch),
        compiler_params=pltpu.CompilerParams(
            vmem_limit_bytes=(63 if in_hbm else 32) * 1024 * 1024
        ),
        cost_estimate=pl.CostEstimate(flops=flops, bytes_accessed=1 << 20, transcendentals=0),
    )(*scalars, *args)
    return result


def shards(u_old, u_init):
    planes, rows, cols = u_init.shape
    coarse, rows_c, cols_c = planes // 2, rows // 2, cols // 2
    slices = lax.axis_size(TM)
    blocks = lax.axis_size(SPACE)
    depth_c = coarse * blocks
    down_y, down_x, stencil, forward_z, inverse_z, denom, shift_x, up_x, up_y = tables(
        coarse, rows, cols, depth_c
    )
    position = lax.axis_index(TM)
    core = lax.axis_index("c")
    kx = 2 * lax.axis_index("y") + core
    place = [position, core, lax.axis_index("zl"), lax.axis_index("x"), kx]
    place = jnp.stack(place + [lax.axis_index("zh"), slices]).astype(jnp.int32)

    last, start_out = call(
        last_kernel,
        [(planes, rows, cols), (REACH, rows, cols)],
        [place],
        u_old, u_init,
        scratch=[pltpu.SemaphoreType.DMA((2,))],
        in_hbm=True,
    )

    def far_block(s):
        return (s + 1) % blocks if s % 2 else (s - 1) % blocks

    across = [
        (n * blocks + s, (n + 1) % slices * blocks + far_block(s))
        for n in range(slices)
        for s in range(blocks)
    ]
    start_far = lax.ppermute(start_out, TM + SPACE, across)
    previous = lax.ppermute(last, TM, [(i, i + 1) for i in range(slices - 1)])
    g, own_near, own_far = call(
        old_kernel,
        [(4, planes, rows, cols), (PACK, rows, cols), (PACK, rows, cols)],
        [place],
        u_old[0],
        flops=10**11,
    )
    start_far = call(relay_kernel, start_far.shape, [], start_far, flops=10**11)
    got_far = lax.ppermute(own_far, SPACE, [(s, far_block(s)) for s in range(blocks)])
    near_out = call(
        near_kernel, (PACK + REACH, rows, cols), [place], u_init, previous, own_near
    )
    near = lax.ppermute(near_out, "c", [(0, 1), (1, 0)])

    w, send, hats = call(
        sweep_kernel,
        [
            (5, planes + 2 * REACH, rows, cols),
            (blocks, 2 * coarse, 2 * cols_c),
            (rows_c * coarse, 4 * cols_c),
        ],
        [place],
        u_init, previous, near, start_far, g, own_near, own_far, got_far,
        down_y, down_x, stencil,
        scratch=[pltpu.VMEM((2, coarse, rows, cols), jnp.float32)],
    )
    columns = lax.all_to_all(send, SPACE, 0, 0, tiled=True)
    packed = (lax.axis_size("zl"), depth_c // 2, 2 * cols_c)
    lifted, offset, copies = call(
        spectrum_kernel,
        [(depth_c, 2 * cols_c), (depth_c, 2 * cols_c), packed],
        [place, shift_x],
        columns, forward_z, denom,
    )
    gathered = lax.all_to_all(copies, "zl", 0, 0, tiled=True)
    back = call(
        scan_kernel,
        (4 * rows_c, coarse, 4 * cols_c),
        [place, shift_x],
        gathered, lifted, offset, denom, inverse_z,
    )
    returned = lax.all_to_all(back, ("x", "y", "c"), 0, 0, tiled=True)
    out = call(
        finish_kernel, (5, planes, rows, cols), [place], w, returned, hats, up_x, up_y
    )
    return out[None]


def solution(mesh):
    finer = Mesh(mesh.devices.reshape(4, 8, 4, 2, 2), TM + SPACE)
    in_specs = (P(TM, None, SPACE, None, None), P(SPACE, None, None))
    out_specs = P(TM, None, SPACE, None, None)
    return jax.shard_map(
        shards, mesh=finer, in_specs=in_specs, out_specs=out_specs, check_vma=False
    )
```

```python
import math

import jax
import jax.numpy as jnp
import numpy as np
from jax import lax
from jax.experimental import pallas as pl
from jax.experimental.pallas import tpu as pltpu
from jax.sharding import Mesh
from jax.sharding import PartitionSpec as P

TM = ("x", "zb", "za")
SPACE = ("y", "zh", "c")

step_length = 0.4
diffusion = 1.0
reaction = 1.0

G_AT = (0, 3, 5, 6)
U_AT = 6
PACK = 10
REACH = 4


def basis_coefficients(nodes, chosen):
    polynomial = [1.0]
    for other, point in enumerate(nodes):
        if other == chosen:
            continue
        divisor = nodes[chosen] - point
        widened = [0.0] * (len(polynomial) + 1)
        for power, value in enumerate(polynomial):
            widened[power + 1] += value / divisor
            widened[power] -= value * point / divisor
        polynomial = widened
    return polynomial


def basis_value(nodes, chosen, where):
    result = 1.0
    for other, point in enumerate(nodes):
        if other != chosen:
            result *= (where - point) / (nodes[chosen] - point)
    return result


def node_tables():
    root = math.sqrt(3.0 / 7.0)
    fine_tau = [0.0, (1.0 - root) / 2.0, 0.5, (1.0 + root) / 2.0, 1.0]
    coarse_tau = [0.0, 0.5, 1.0]
    integ = []
    for j in range(4):
        row_values = []
        for k in range(5):
            polynomial = basis_coefficients(fine_tau, k)
            total = 0.0
            for power, value in enumerate(polynomial):
                total += (
                    value
                    * (fine_tau[j + 1] ** (power + 1) - fine_tau[j] ** (power + 1))
                    / (power + 1)
                )
            row_values.append(total)
        integ.append(row_values)
    interp = [[basis_value(coarse_tau, c, fine_tau[m]) for c in range(3)] for m in range(5)]
    spacing = [float(fine_tau[j + 1] - fine_tau[j]) for j in range(4)]
    return integ, spacing, interp


INTEG, SPACING, INTERP = node_tables()
MIX = [
    [step_length * (INTEG[j][k] - (SPACING[j] if j == k else 0.0)) for k in range(5)]
    for j in range(4)
]
COUPLING = 0.5 * step_length * diffusion * 0.25
QUAD = [[step_length * (INTEG[2 * c][k] + INTEG[2 * c + 1][k]) for k in range(5)] for c in range(2)]


def hartley(length):
    counter = np.arange(length)
    phase = 2.0 * np.pi * (counter[:, None] * counter[None, :] % length) / length
    return (np.cos(phase) + np.sin(phase)) / math.sqrt(length)


def block_pair(table):
    rows, cols = table.shape
    both = np.zeros((2 * rows, 2 * cols))
    both[:rows, :cols] = table
    both[rows:, cols:] = table
    return both


def tables(planes, rows, cols, depth):
    rows_c, cols_c = rows // 2, cols // 2
    hx, hy, hz = hartley(rows_c), hartley(cols_c), hartley(depth)
    down_y = 0.5 * np.repeat(hy, 2, 0)
    up_y = np.repeat(hy, 2, 0).T
    wide_x = np.repeat(hx, 2, 0)
    down_x = np.zeros((rows_c, planes, planes, rows))
    up_x = np.zeros((planes, rows, rows_c, planes))
    for p in range(planes):
        down_x[:, p, p, :] = 0.25 * wide_x.T
        up_x[p, :, :, p] = wide_x
    down_x = down_x.reshape(rows_c * planes, planes * rows)
    up_x = up_x.reshape(planes * rows, rows_c * planes)
    cos_z = np.cos(2.0 * np.pi * np.arange(depth) / depth)
    cos_y = np.cos(2.0 * np.pi * np.arange(cols_c) / cols_c)
    half = COUPLING
    cos_x = np.cos(2.0 * np.pi * np.arange(rows_c) / rows_c)
    stencil = half * (6.0 - 2.0 * cos_x[:, None, None] - 2.0 * cos_y[None, None, :])
    stencil = np.broadcast_to(stencil, (rows_c, planes, cols_c)).reshape(-1, cols_c)
    stencil = np.concatenate([stencil, stencil], 1)
    blocks = depth // planes
    forward_z = np.zeros((depth, blocks, 2, planes))
    forward_z[:, :, 0, :] = hz.reshape(depth, blocks, planes)
    for s in range(blocks):
        forward_z[:, s, 1, 0] = hz[:, (s * planes - 1) % depth]
        forward_z[:, s, 1, planes - 1] = hz[:, (s * planes + planes) % depth]
    forward_z = forward_z.reshape(depth, -1)
    denom = 1.0 - half * (2.0 * cos_z[:, None] + 2.0 * cos_y[None, :] - 6.0)
    denom = np.concatenate([denom, denom], 1)
    shift_x = half * 2.0 * cos_x
    inverse_z = hz.reshape(4, 2, 2, planes, depth).transpose(1, 0, 2, 3, 4)
    inverse_z = inverse_z.reshape(2, 8 * planes, depth)
    f32 = lambda a: jnp.asarray(a, jnp.float32)
    return (
        f32(block_pair(down_y)), f32(down_x), f32(stencil), f32(forward_z), f32(inverse_z),
        f32(denom), f32(shift_x), f32(up_x), f32(block_pair(up_y)),
    )


def lanes_swapped(a):
    return pltpu.roll(a, a.shape[1] // 2, 1)


def left_half(a):
    return lax.broadcasted_iota(jnp.int32, a.shape, 1) < a.shape[1] // 2


def dot(a, b):
    return jnp.dot(a, b, precision=lax.Precision.HIGHEST, preferred_element_type=jnp.float32)


def plane_part(f):
    near = pltpu.roll(f, 1, 0) + pltpu.roll(f, f.shape[0] - 1, 0)
    near = near + pltpu.roll(f, 1, 1) + pltpu.roll(f, f.shape[1] - 1, 1)
    return diffusion * near - f * ((6.0 * diffusion - reaction) + reaction * (f * f))


def old_kernel(place, u, g, near, far):
    planes = u.shape[1]
    core = place[1]

    for p in range(planes):
        total = [None] * 4
        for k in range(5):
            field = u[k, p]
            force = plane_part(field)
            if p > 0:
                force = force + diffusion * u[k, p - 1]
            if p < planes - 1:
                force = force + diffusion * u[k, p + 1]
            for j in range(4):
                term = MIX[j][k] * force
                total[j] = term if total[j] is None else total[j] + term
        for j in range(4):
            g[j, p] = total[j]

    def packed(out, plane_of):
        for j in range(4):
            for i in range(3 - j):
                out[G_AT[j] + i] = g[j, plane_of(i)]
            edge = plane_of(0)
            out[U_AT + j] = diffusion * sum(MIX[j][k] * u[k, edge] for k in range(5))

    top = lambda i: planes - 1 - i
    bottom = lambda i: i

    @pl.when(core == 0)
    def _():
        packed(near, top)
        packed(far, bottom)

    @pl.when(core != 0)
    def _():
        packed(near, bottom)
        packed(far, top)


def edge_kernel(place, last, first, start_out):
    position, core, slices = place[0], place[1], place[6]
    edge = pl.ds(core * (first.shape[0] - REACH), REACH)

    @pl.when(position == slices - 1)
    def _():
        start_out[...] = first[edge]

    @pl.when(position != slices - 1)
    def _():
        start_out[...] = last[edge]


def relay_kernel(got, out):
    out[...] = got[...]


def near_kernel(place, first, previous, own_near, out):
    position, core = place[0], place[1]
    edge = pl.ds((1 - core) * (first.shape[0] - REACH), REACH)
    out[:PACK] = own_near[...]

    @pl.when(position == 0)
    def _():
        out[PACK:] = first[edge]

    @pl.when(position != 0)
    def _():
        out[PACK:] = previous[edge]


def sweep_kernel(
    place, first, previous, near, start_far, g, own_near, own_far, got_far,
    down_y, down_x, stencil, w, send, hats, quad,
):
    got_near, start_near = near.at[:PACK], near.at[PACK:]
    planes = first.shape[0]
    coarse = planes // 2
    position, core = place[0], place[1]

    def with_sides(body):
        @pl.when(core == 0)
        def _():
            body(start_far, own_far, got_far, start_near, own_near, got_near)

        @pl.when(core != 0)
        def _():
            body(start_near, own_near, got_near, start_far, own_far, got_far)

    @pl.when(position == 0)
    def _():
        w[0, REACH : REACH + planes] = first[...]

    @pl.when(position != 0)
    def _():
        w[0, REACH : REACH + planes] = previous[...]

    def run(start_lo, own_lo, got_lo, start_hi, own_hi, got_hi):
        w[0, :REACH] = start_lo[...]
        w[0, REACH + planes :] = start_hi[...]
        for m in range(5):
            margin = max(3 - m, 0)
            held = None
            for p in range(-margin, planes + margin):
                at = p + REACH
                field = w[m, at]
                force = plane_part(field)
                if m < 4 or p > 0:
                    force = force + diffusion * w[m, at - 1]
                if m < 4 or p < planes - 1:
                    force = force + diffusion * w[m, at + 1]
                if m < 4:
                    if p < 0:
                        source = got_lo[G_AT[m] - p - 1]
                        if p == -1:
                            source = source + own_lo[U_AT + m]
                    elif p >= planes:
                        source = got_hi[G_AT[m] + p - planes]
                        if p == planes:
                            source = source + own_hi[U_AT + m]
                    else:
                        source = g[m, p]
                        if p == 0:
                            source = source + got_lo[U_AT + m]
                        if p == planes - 1:
                            source = source + got_hi[U_AT + m]
                    w[m + 1, at] = field + step_length * SPACING[m] * force + source
                if 0 <= p < planes:
                    if p % 2 == 0:
                        held = force
                    else:
                        both = held + force
                        for c in range(2):
                            term = QUAD[c][m] * both
                            quad[c, p // 2] = term if m == 0 else quad[c, p // 2] + term

    with_sides(run)

    def paired(m):
        return jnp.concatenate(
            [w[m, REACH + 2 * i] + w[m, REACH + 2 * i + 1] for i in range(coarse)], 0
        )

    rows = coarse * first.shape[1]
    restart = paired(0)
    mask = jnp.where(position == 0, 1.0, 0.0)
    q0 = quad[0].reshape(rows, -1) + mask * restart
    q1 = quad[1].reshape(rows, -1)
    table = down_y[...]
    edge_rows = first.shape[1]
    middle = jnp.zeros((rows - 2 * edge_rows, first.shape[2]), jnp.float32)
    edges = jnp.concatenate([w[4, REACH], middle, w[4, REACH + planes - 1]], 0)
    left = [
        dot(jnp.concatenate(pair, 1), table)
        for pair in ((q0, q1), (paired(2), paired(4)), (restart, edges))
    ]
    spectral = dot(down_x[...], jnp.concatenate(left, 1))
    width = left[0].shape[1]
    states = spectral[:, width : 2 * width]
    third = spectral[:, 2 * width :]
    count = spectral.shape[0]
    level = lax.broadcasted_iota(jnp.int32, states.shape, 0) % coarse
    near_z = jnp.where(level > 0, pltpu.roll(states, 1, 0), 0.0)
    near_z = near_z + jnp.where(level < coarse - 1, pltpu.roll(states, count - 1, 0), 0.0)
    inside = spectral[:, :width] + stencil[...] * states - COUPLING * near_z
    is_left = left_half(states)
    last = jnp.where(is_left, lanes_swapped(third), third)
    last = last * jnp.where(is_left, diffusion * QUAD[0][4], diffusion * QUAD[1][4])
    spill = last - COUPLING * states
    spill = jnp.where((level == 0) | (level == coarse - 1), spill, 0.0)
    for y in range(4):
        for c in range(2):
            kx = 2 * y + c
            span = slice(kx * coarse, (kx + 1) * coarse)
            for zh in range(2):
                send[4 * y + 2 * zh + c, :coarse] = inside[span]
                send[4 * y + 2 * zh + c, coarse:] = spill[span]
    hats[...] = spectral[:, width:]


def spectrum_kernel(place, shift_x, got, table, denom, lifted, offset, copies):
    depth = table.shape[0]
    half = depth // 2
    d = denom[...] - shift_x[place[4]]
    inv = 1.0 / d
    lift = dot(table[...], got[...].reshape(-1, d.shape[1]))
    weighted = lift * inv
    weighted = jnp.where(left_half(d), weighted * inv, weighted)
    total = weighted + lanes_swapped(weighted)
    lifted[...] = lift
    offset[...] = total
    packed = jnp.where(left_half(total[:half]), total[:half], total[half:])
    for i in range(copies.shape[0]):
        copies[i] = packed


def packed_inverse(place, shift_x, denom):
    d = denom[...] - shift_x[place[4]]
    inv = 1.0 / d
    half = inv.shape[0] // 2
    left = left_half(inv[:half])
    return inv, left, jnp.where(left, inv[:half], inv[half:])


def group_kernel(place, shift_x, offsets, denom, total_out, prefix_out):
    za = place[2]
    _, _, inv = packed_inverse(place, shift_x, denom)
    inv2 = inv * inv
    total = jnp.zeros_like(inv2)
    prefix = jnp.zeros_like(inv2)
    for m in range(offsets.shape[0]):
        piece = offsets[m]
        total = total * inv2 + piece
        prefix = jnp.where(m < za, prefix * inv2 + piece, prefix)
    total_out[...] = total
    prefix_out[...] = prefix


def scan_kernel(
    place, shift_x, own_total, other_total, own_prefix, lifted, offset, denom, inverse_z, out
):
    za, block, zh, zb = place[2], place[3], place[5], place[7]
    inv, left, inv_packed = packed_inverse(place, shift_x, denom)
    inv2 = inv_packed * inv_packed
    inv4 = inv2 * inv2
    inv8 = inv4 * inv4
    whole = inv8 * inv8
    power = jnp.where(za % 2 == 1, inv2, 1.0)
    power = jnp.where(za >= 2, power * inv4, power)
    early = jnp.where(zb == 0, own_total[...], other_total[...])
    late = jnp.where(zb == 0, other_total[...], own_total[...])
    prefix = own_prefix[...] + jnp.where(zb == 0, 0.0, power * early)
    total = early * inv8 + late
    power = jnp.where(zb == 0, power, power * inv8)
    inverse = inverse_z[zh]
    weights = jnp.where(left_half(inv), inv, inv * inv)
    own = jnp.where(left_half(inv), lifted[...] * inv, offset[...])
    carried = total * power
    targets = out.shape[0] // 8
    for xp in range(targets):
        packed = jnp.where(xp == block, prefix, jnp.where(xp > block, carried, 0.0))
        carried = jnp.where(xp > block, carried * whole, carried)
        turned = lanes_swapped(packed)
        begin = jnp.concatenate(
            [jnp.where(left, packed, turned), jnp.where(left, turned, packed)], 0
        )
        later = begin * weights + jnp.where(xp == block, own, 0.0)
        planar = dot(inverse, jnp.concatenate([later, begin], 1))
        out[8 * xp : 8 * xp + 8] = planar.reshape(8, -1, planar.shape[1])


def finish_kernel(place, w, got, hats, up_x, up_y, out):
    planes = out.shape[1]
    coarse = planes // 2
    rows = out.shape[2]
    cols = out.shape[3]
    total = got[0:8] + got[8:16] + (got[16:24] + got[24:32])
    delta = total.reshape(-1, total.shape[2]) - hats[...]
    half = delta.shape[1] // 2
    later = delta[:, :half]
    begin = jnp.where(place[0] == 0, 0.0, delta[:, half:])
    spread = dot(up_x[...], jnp.concatenate([later, begin], 1))
    table = up_y[...]
    after = dot(spread[:, :half], table)
    before = dot(spread[:, half:], table[:, :cols])
    parts = [before, after[:, :cols], after[:, cols:]]
    for m in range(5):
        mixed = None
        for c in range(3):
            weight = INTERP[m][c]
            if abs(weight) < 1e-14:
                continue
            term = parts[c] if weight == 1.0 else weight * parts[c]
            mixed = term if mixed is None else mixed + term
        for i in range(coarse):
            piece = mixed[i * rows : (i + 1) * rows]
            out[m, 2 * i] = w[m, REACH + 2 * i] + piece
            out[m, 2 * i + 1] = w[m, REACH + 2 * i + 1] + piece


def call(kernel, outs, scalars, *args, scratch=(), flops=0):
    smem = pl.BlockSpec(memory_space=pltpu.SMEM)
    vmem = pl.BlockSpec(memory_space=pltpu.VMEM)
    single = not isinstance(outs, list)
    shapes = [jax.ShapeDtypeStruct(s, jnp.float32) for s in ([outs] if single else outs)]
    result = pl.pallas_call(
        kernel,
        out_shape=shapes[0] if single else shapes,
        in_specs=[smem] * len(scalars) + [vmem] * len(args),
        out_specs=vmem if single else [vmem] * len(shapes),
        scratch_shapes=list(scratch),
        compiler_params=pltpu.CompilerParams(vmem_limit_bytes=32 * 1024 * 1024),
        cost_estimate=pl.CostEstimate(flops=flops, bytes_accessed=1 << 20, transcendentals=0),
    )(*scalars, *args)
    return result


def shards(u_old, u_init):
    planes, rows, cols = u_init.shape
    coarse, rows_c, cols_c = planes // 2, rows // 2, cols // 2
    slices = lax.axis_size(TM)
    blocks = lax.axis_size(SPACE)
    depth_c = coarse * blocks
    down_y, down_x, stencil, forward_z, inverse_z, denom, shift_x, up_x, up_y = tables(
        coarse, rows, cols, depth_c
    )
    position = lax.axis_index(TM)
    core = lax.axis_index("c")
    kx = 2 * lax.axis_index("y") + core
    place = [position, core, lax.axis_index("za"), lax.axis_index("x"), kx]
    place = jnp.stack(place + [lax.axis_index("zh"), slices, lax.axis_index("zb")])
    place = place.astype(jnp.int32)

    last = u_old[0, 4]
    start_out = call(edge_kernel, (REACH, rows, cols), [place], last, u_init, flops=10**11)

    def far_block(s):
        return (s + 1) % blocks if s % 2 else (s - 1) % blocks

    across = [
        (n * blocks + s, (n + 1) % slices * blocks + far_block(s))
        for n in range(slices)
        for s in range(blocks)
    ]
    start_far = lax.ppermute(start_out, TM + SPACE, across)
    previous = lax.ppermute(last, TM, [(i, i + 1) for i in range(slices - 1)])
    g, own_near, own_far = call(
        old_kernel,
        [(4, planes, rows, cols), (PACK, rows, cols), (PACK, rows, cols)],
        [place],
        u_old[0],
        flops=10**11,
    )
    start_far = call(relay_kernel, start_far.shape, [], start_far, flops=10**11)
    got_far = lax.ppermute(own_far, SPACE, [(s, far_block(s)) for s in range(blocks)])
    near_out = call(
        near_kernel, (PACK + REACH, rows, cols), [place], u_init, previous, own_near
    )
    near = lax.ppermute(near_out, "c", [(0, 1), (1, 0)])

    w, send, hats = call(
        sweep_kernel,
        [
            (5, planes + 2 * REACH, rows, cols),
            (blocks, 2 * coarse, 2 * cols_c),
            (rows_c * coarse, 4 * cols_c),
        ],
        [place],
        u_init, previous, near, start_far, g, own_near, own_far, got_far,
        down_y, down_x, stencil,
        scratch=[pltpu.VMEM((2, coarse, rows, cols), jnp.float32)],
    )
    columns = lax.all_to_all(send, SPACE, 0, 0, tiled=True)
    packed = (depth_c // 2, 2 * cols_c)
    lifted, offset, copies = call(
        spectrum_kernel,
        [(depth_c, 2 * cols_c), (depth_c, 2 * cols_c), (4, *packed)],
        [place, shift_x],
        columns, forward_z, denom,
    )
    gathered = lax.all_to_all(copies, "za", 0, 0, tiled=True)
    own_total, own_prefix = call(
        group_kernel, [packed, packed], [place, shift_x], gathered, denom
    )
    other_total = lax.ppermute(own_total, "zb", [(0, 1), (1, 0)])
    back = call(
        scan_kernel,
        (4 * rows_c, coarse, 4 * cols_c),
        [place, shift_x],
        own_total, other_total, own_prefix, lifted, offset, denom, inverse_z,
    )
    returned = lax.all_to_all(back, ("x", "y", "c"), 0, 0, tiled=True)
    out = call(
        finish_kernel, (5, planes, rows, cols), [place], w, returned, hats, up_x, up_y
    )
    return out[None]


def solution(mesh):
    finer = Mesh(mesh.devices.reshape(4, 2, 4, 4, 2, 2), TM + SPACE)
    in_specs = (P(TM, None, SPACE, None, None), P(SPACE, None, None))
    out_specs = P(TM, None, SPACE, None, None)
    return jax.shard_map(
        shards, mesh=finer, in_specs=in_specs, out_specs=out_specs, check_vma=False
    )
```

```python
import math

import jax
import jax.numpy as jnp
import numpy as np
from jax import lax
from jax.experimental import pallas as pl
from jax.experimental.pallas import tpu as pltpu
from jax.sharding import Mesh
from jax.sharding import PartitionSpec as P

TM = ("x", "zb", "za")
SPACE = ("y", "zh", "c")

step_length = 0.4
diffusion = 1.0
reaction = 1.0

G_AT = (0, 3, 5, 6)
U_AT = 6
PACK = 10
REACH = 4


def basis_coefficients(nodes, chosen):
    polynomial = [1.0]
    for other, point in enumerate(nodes):
        if other == chosen:
            continue
        divisor = nodes[chosen] - point
        widened = [0.0] * (len(polynomial) + 1)
        for power, value in enumerate(polynomial):
            widened[power + 1] += value / divisor
            widened[power] -= value * point / divisor
        polynomial = widened
    return polynomial


def basis_value(nodes, chosen, where):
    result = 1.0
    for other, point in enumerate(nodes):
        if other != chosen:
            result *= (where - point) / (nodes[chosen] - point)
    return result


def node_tables():
    root = math.sqrt(3.0 / 7.0)
    fine_tau = [0.0, (1.0 - root) / 2.0, 0.5, (1.0 + root) / 2.0, 1.0]
    coarse_tau = [0.0, 0.5, 1.0]
    integ = []
    for j in range(4):
        row_values = []
        for k in range(5):
            polynomial = basis_coefficients(fine_tau, k)
            total = 0.0
            for power, value in enumerate(polynomial):
                total += (
                    value
                    * (fine_tau[j + 1] ** (power + 1) - fine_tau[j] ** (power + 1))
                    / (power + 1)
                )
            row_values.append(total)
        integ.append(row_values)
    interp = [[basis_value(coarse_tau, c, fine_tau[m]) for c in range(3)] for m in range(5)]
    spacing = [float(fine_tau[j + 1] - fine_tau[j]) for j in range(4)]
    return integ, spacing, interp


INTEG, SPACING, INTERP = node_tables()
MIX = [
    [step_length * (INTEG[j][k] - (SPACING[j] if j == k else 0.0)) for k in range(5)]
    for j in range(4)
]
COUPLING = 0.5 * step_length * diffusion * 0.25
QUAD = [[step_length * (INTEG[2 * c][k] + INTEG[2 * c + 1][k]) for k in range(5)] for c in range(2)]


def hartley(length):
    counter = np.arange(length)
    phase = 2.0 * np.pi * (counter[:, None] * counter[None, :] % length) / length
    return (np.cos(phase) + np.sin(phase)) / math.sqrt(length)


def block_pair(table):
    rows, cols = table.shape
    both = np.zeros((2 * rows, 2 * cols))
    both[:rows, :cols] = table
    both[rows:, cols:] = table
    return both


def tables(planes, rows, cols, depth):
    rows_c, cols_c = rows // 2, cols // 2
    hx, hy, hz = hartley(rows_c), hartley(cols_c), hartley(depth)
    down_y = 0.5 * np.repeat(hy, 2, 0)
    up_y = np.repeat(hy, 2, 0).T
    wide_x = np.repeat(hx, 2, 0)
    down_x = np.zeros((rows_c, planes, planes, rows))
    up_x = np.zeros((planes, rows, rows_c, planes))
    for p in range(planes):
        down_x[:, p, p, :] = 0.25 * wide_x.T
        up_x[p, :, :, p] = wide_x
    down_x = down_x.reshape(rows_c * planes, planes * rows)
    up_x = up_x.reshape(planes * rows, rows_c * planes)
    cos_z = np.cos(2.0 * np.pi * np.arange(depth) / depth)
    cos_y = np.cos(2.0 * np.pi * np.arange(cols_c) / cols_c)
    half = COUPLING
    cos_x = np.cos(2.0 * np.pi * np.arange(rows_c) / rows_c)
    stencil = half * (6.0 - 2.0 * cos_x[:, None, None] - 2.0 * cos_y[None, None, :])
    stencil = np.broadcast_to(stencil, (rows_c, planes, cols_c)).reshape(-1, cols_c)
    stencil = np.concatenate([stencil, stencil], 1)
    blocks = depth // planes
    forward_z = np.zeros((depth, blocks, 2, planes))
    forward_z[:, :, 0, :] = hz.reshape(depth, blocks, planes)
    for s in range(blocks):
        forward_z[:, s, 1, 0] = hz[:, (s * planes - 1) % depth]
        forward_z[:, s, 1, planes - 1] = hz[:, (s * planes + planes) % depth]
    forward_z = forward_z.reshape(depth, -1)
    denom = 1.0 - half * (2.0 * cos_z[:, None] + 2.0 * cos_y[None, :] - 6.0)
    denom = np.concatenate([denom, denom], 1)
    shift_x = half * 2.0 * cos_x
    inverse_z = hz.reshape(4, 2, 2, planes, depth).transpose(1, 0, 2, 3, 4)
    inverse_z = inverse_z.reshape(2, 8 * planes, depth)
    f32 = lambda a: jnp.asarray(a, jnp.float32)
    return (
        f32(block_pair(down_y)), f32(down_x), f32(stencil), f32(forward_z), f32(inverse_z),
        f32(denom), f32(shift_x), f32(up_x), f32(block_pair(up_y)),
    )


def lanes_swapped(a):
    return pltpu.roll(a, a.shape[1] // 2, 1)


def left_half(a):
    return lax.broadcasted_iota(jnp.int32, a.shape, 1) < a.shape[1] // 2


def dot(a, b):
    return jnp.dot(a, b, precision=lax.Precision.HIGHEST, preferred_element_type=jnp.float32)


def plane_part(f):
    near = pltpu.roll(f, 1, 0) + pltpu.roll(f, f.shape[0] - 1, 0)
    near = near + pltpu.roll(f, 1, 1) + pltpu.roll(f, f.shape[1] - 1, 1)
    return diffusion * near - f * ((6.0 * diffusion - reaction) + reaction * (f * f))


def old_kernel(place, u, first, g, near, far, edge_near, edge_far):
    planes = u.shape[1]
    position, core, slices = place[0], place[1], place[6]
    far_edge = pl.ds(core * (planes - REACH), REACH)
    near_edge = pl.ds((1 - core) * (planes - REACH), REACH)

    @pl.when(position == slices - 1)
    def _():
        edge_far[...] = first[far_edge]
        edge_near[...] = first[near_edge]

    @pl.when(position != slices - 1)
    def _():
        edge_far[...] = u[4, far_edge]
        edge_near[...] = u[4, near_edge]

    for p in range(planes):
        total = [None] * 4
        for k in range(5):
            field = u[k, p]
            force = plane_part(field)
            if p > 0:
                force = force + diffusion * u[k, p - 1]
            if p < planes - 1:
                force = force + diffusion * u[k, p + 1]
            for j in range(4):
                term = MIX[j][k] * force
                total[j] = term if total[j] is None else total[j] + term
        for j in range(4):
            g[j, p] = total[j]

    def packed(out, plane_of):
        for j in range(4):
            for i in range(3 - j):
                out[G_AT[j] + i] = g[j, plane_of(i)]
            edge = plane_of(0)
            out[U_AT + j] = diffusion * sum(MIX[j][k] * u[k, edge] for k in range(5))

    top = lambda i: planes - 1 - i
    bottom = lambda i: i

    @pl.when(core == 0)
    def _():
        packed(near, top)
        packed(far, bottom)

    @pl.when(core != 0)
    def _():
        packed(near, bottom)
        packed(far, top)


def relay_kernel(halo, edge, halo_out, edge_out):
    halo_out[...] = halo[...]
    edge_out[...] = edge[...]


def sweep_kernel(
    place, first, previous, start_near, start_far, g, own_near, own_far, got_near, got_far,
    down_y, down_x, stencil, w, send, hats, quad,
):
    planes = first.shape[0]
    coarse = planes // 2
    position, core = place[0], place[1]

    def with_sides(body):
        @pl.when(core == 0)
        def _():
            body(start_far, own_far, got_far, start_near, own_near, got_near)

        @pl.when(core != 0)
        def _():
            body(start_near, own_near, got_near, start_far, own_far, got_far)

    @pl.when(position == 0)
    def _():
        w[0, REACH : REACH + planes] = first[...]

    @pl.when(position != 0)
    def _():
        w[0, REACH : REACH + planes] = previous[...]

    def run(start_lo, own_lo, got_lo, start_hi, own_hi, got_hi):
        w[0, :REACH] = start_lo[...]
        w[0, REACH + planes :] = start_hi[...]
        for m in range(5):
            margin = max(3 - m, 0)
            held = None
            for p in range(-margin, planes + margin):
                at = p + REACH
                field = w[m, at]
                force = plane_part(field)
                if m < 4 or p > 0:
                    force = force + diffusion * w[m, at - 1]
                if m < 4 or p < planes - 1:
                    force = force + diffusion * w[m, at + 1]
                if m < 4:
                    if p < 0:
                        source = got_lo[G_AT[m] - p - 1]
                        if p == -1:
                            source = source + own_lo[U_AT + m]
                    elif p >= planes:
                        source = got_hi[G_AT[m] + p - planes]
                        if p == planes:
                            source = source + own_hi[U_AT + m]
                    else:
                        source = g[m, p]
                        if p == 0:
                            source = source + got_lo[U_AT + m]
                        if p == planes - 1:
                            source = source + got_hi[U_AT + m]
                    w[m + 1, at] = field + step_length * SPACING[m] * force + source
                if 0 <= p < planes:
                    if p % 2 == 0:
                        held = force
                    else:
                        both = held + force
                        for c in range(2):
                            term = QUAD[c][m] * both
                            quad[c, p // 2] = term if m == 0 else quad[c, p // 2] + term

    with_sides(run)

    def paired(m):
        return jnp.concatenate(
            [w[m, REACH + 2 * i] + w[m, REACH + 2 * i + 1] for i in range(coarse)], 0
        )

    rows = coarse * first.shape[1]
    restart = paired(0)
    mask = jnp.where(position == 0, 1.0, 0.0)
    q0 = quad[0].reshape(rows, -1) + mask * restart
    q1 = quad[1].reshape(rows, -1)
    table = down_y[...]
    edge_rows = first.shape[1]
    middle = jnp.zeros((rows - 2 * edge_rows, first.shape[2]), jnp.float32)
    edges = jnp.concatenate([w[4, REACH], middle, w[4, REACH + planes - 1]], 0)
    left = [
        dot(jnp.concatenate(pair, 1), table)
        for pair in ((q0, q1), (paired(2), paired(4)), (restart, edges))
    ]
    spectral = dot(down_x[...], jnp.concatenate(left, 1))
    width = left[0].shape[1]
    states = spectral[:, width : 2 * width]
    third = spectral[:, 2 * width :]
    count = spectral.shape[0]
    level = lax.broadcasted_iota(jnp.int32, states.shape, 0) % coarse
    near_z = jnp.where(level > 0, pltpu.roll(states, 1, 0), 0.0)
    near_z = near_z + jnp.where(level < coarse - 1, pltpu.roll(states, count - 1, 0), 0.0)
    inside = spectral[:, :width] + stencil[...] * states - COUPLING * near_z
    is_left = left_half(states)
    last = jnp.where(is_left, lanes_swapped(third), third)
    last = last * jnp.where(is_left, diffusion * QUAD[0][4], diffusion * QUAD[1][4])
    spill = last - COUPLING * states
    spill = jnp.where((level == 0) | (level == coarse - 1), spill, 0.0)
    for y in range(4):
        for c in range(2):
            kx = 2 * y + c
            span = slice(kx * coarse, (kx + 1) * coarse)
            for zh in range(2):
                send[4 * y + 2 * zh + c, :coarse] = inside[span]
                send[4 * y + 2 * zh + c, coarse:] = spill[span]
    hats[...] = spectral[:, width:]


def spectrum_kernel(place, shift_x, got, table, denom, lifted, offset, copies):
    depth = table.shape[0]
    half = depth // 2
    d = denom[...] - shift_x[place[4]]
    inv = 1.0 / d
    lift = dot(table[...], got[...].reshape(-1, d.shape[1]))
    weighted = lift * inv
    weighted = jnp.where(left_half(d), weighted * inv, weighted)
    total = weighted + lanes_swapped(weighted)
    lifted[...] = lift
    offset[...] = total
    packed = jnp.where(left_half(total[:half]), total[:half], total[half:])
    for i in range(copies.shape[0]):
        copies[i] = packed


def packed_inverse(place, shift_x, denom):
    d = denom[...] - shift_x[place[4]]
    inv = 1.0 / d
    half = inv.shape[0] // 2
    left = left_half(inv[:half])
    return inv, left, jnp.where(left, inv[:half], inv[half:])


def group_kernel(place, shift_x, offsets, denom, total_out, prefix_out):
    za = place[2]
    _, _, inv = packed_inverse(place, shift_x, denom)
    inv2 = inv * inv
    total = jnp.zeros_like(inv2)
    prefix = jnp.zeros_like(inv2)
    for m in range(offsets.shape[0]):
        piece = offsets[m]
        total = total * inv2 + piece
        prefix = jnp.where(m < za, prefix * inv2 + piece, prefix)
    total_out[...] = total
    prefix_out[...] = prefix


def scan_kernel(
    place, shift_x, own_total, other_total, own_prefix, lifted, offset, denom, inverse_z, out
):
    za, block, zh, zb = place[2], place[3], place[5], place[7]
    inv, left, inv_packed = packed_inverse(place, shift_x, denom)
    inv2 = inv_packed * inv_packed
    inv4 = inv2 * inv2
    inv8 = inv4 * inv4
    whole = inv8 * inv8
    power = jnp.where(za % 2 == 1, inv2, 1.0)
    power = jnp.where(za >= 2, power * inv4, power)
    early = jnp.where(zb == 0, own_total[...], other_total[...])
    late = jnp.where(zb == 0, other_total[...], own_total[...])
    prefix = own_prefix[...] + jnp.where(zb == 0, 0.0, power * early)
    total = early * inv8 + late
    power = jnp.where(zb == 0, power, power * inv8)
    inverse = inverse_z[zh]
    weights = jnp.where(left_half(inv), inv, inv * inv)
    own = jnp.where(left_half(inv), lifted[...] * inv, offset[...])
    carried = total * power
    targets = out.shape[0] // 8
    for xp in range(targets):
        packed = jnp.where(xp == block, prefix, jnp.where(xp > block, carried, 0.0))
        carried = jnp.where(xp > block, carried * whole, carried)
        turned = lanes_swapped(packed)
        begin = jnp.concatenate(
            [jnp.where(left, packed, turned), jnp.where(left, turned, packed)], 0
        )
        later = begin * weights + jnp.where(xp == block, own, 0.0)
        planar = dot(inverse, jnp.concatenate([later, begin], 1))
        out[8 * xp : 8 * xp + 8] = planar.reshape(8, -1, planar.shape[1])


def finish_kernel(place, w, got, hats, up_x, up_y, out):
    planes = out.shape[1]
    coarse = planes // 2
    rows = out.shape[2]
    cols = out.shape[3]
    total = got[0:8] + got[8:16] + (got[16:24] + got[24:32])
    delta = total.reshape(-1, total.shape[2]) - hats[...]
    half = delta.shape[1] // 2
    later = delta[:, :half]
    begin = jnp.where(place[0] == 0, 0.0, delta[:, half:])
    spread = dot(up_x[...], jnp.concatenate([later, begin], 1))
    table = up_y[...]
    after = dot(spread[:, :half], table)
    before = dot(spread[:, half:], table[:, :cols])
    parts = [before, after[:, :cols], after[:, cols:]]
    for m in range(5):
        mixed = None
        for c in range(3):
            weight = INTERP[m][c]
            if abs(weight) < 1e-14:
                continue
            term = parts[c] if weight == 1.0 else weight * parts[c]
            mixed = term if mixed is None else mixed + term
        for i in range(coarse):
            piece = mixed[i * rows : (i + 1) * rows]
            out[m, 2 * i] = w[m, REACH + 2 * i] + piece
            out[m, 2 * i + 1] = w[m, REACH + 2 * i + 1] + piece


def call(kernel, outs, scalars, *args, scratch=(), flops=0):
    smem = pl.BlockSpec(memory_space=pltpu.SMEM)
    vmem = pl.BlockSpec(memory_space=pltpu.VMEM)
    single = not isinstance(outs, list)
    shapes = [jax.ShapeDtypeStruct(s, jnp.float32) for s in ([outs] if single else outs)]
    result = pl.pallas_call(
        kernel,
        out_shape=shapes[0] if single else shapes,
        in_specs=[smem] * len(scalars) + [vmem] * len(args),
        out_specs=vmem if single else [vmem] * len(shapes),
        scratch_shapes=list(scratch),
        compiler_params=pltpu.CompilerParams(vmem_limit_bytes=32 * 1024 * 1024),
        cost_estimate=pl.CostEstimate(flops=flops, bytes_accessed=1 << 20, transcendentals=0),
    )(*scalars, *args)
    return result


def shards(u_old, u_init):
    planes, rows, cols = u_init.shape
    coarse, rows_c, cols_c = planes // 2, rows // 2, cols // 2
    slices = lax.axis_size(TM)
    blocks = lax.axis_size(SPACE)
    depth_c = coarse * blocks
    down_y, down_x, stencil, forward_z, inverse_z, denom, shift_x, up_x, up_y = tables(
        coarse, rows, cols, depth_c
    )
    position = lax.axis_index(TM)
    core = lax.axis_index("c")
    kx = 2 * lax.axis_index("y") + core
    place = [position, core, lax.axis_index("za"), lax.axis_index("x"), kx]
    place = jnp.stack(place + [lax.axis_index("zh"), slices, lax.axis_index("zb")])
    place = place.astype(jnp.int32)

    halo, edge = (PACK, rows, cols), (REACH, rows, cols)
    g, own_near, own_far, edge_near, edge_far = call(
        old_kernel,
        [(4, planes, rows, cols), halo, halo, edge, edge],
        [place],
        u_old[0], u_init,
        flops=10**11,
    )

    def far_block(s):
        return (s + 1) % blocks if s % 2 else (s - 1) % blocks

    def from_previous(partner):
        return [
            (n * blocks + s, (n + 1) % slices * blocks + partner(s))
            for n in range(slices)
            for s in range(blocks)
        ]

    got_far = lax.ppermute(own_far, SPACE, [(s, far_block(s)) for s in range(blocks)])
    start_far = lax.ppermute(edge_far, TM + SPACE, from_previous(far_block))
    got_far, start_far = call(relay_kernel, [halo, edge], [], got_far, start_far, flops=10**11)
    previous = lax.ppermute(u_old[0, 4], TM, [(i, i + 1) for i in range(slices - 1)])
    start_near = lax.ppermute(edge_near, TM + SPACE, from_previous(lambda s: s ^ 1))
    got_near = lax.ppermute(own_near, "c", [(0, 1), (1, 0)])

    w, send, hats = call(
        sweep_kernel,
        [
            (5, planes + 2 * REACH, rows, cols),
            (blocks, 2 * coarse, 2 * cols_c),
            (rows_c * coarse, 4 * cols_c),
        ],
        [place],
        u_init, previous, start_near, start_far, g, own_near, own_far, got_near, got_far,
        down_y, down_x, stencil,
        scratch=[pltpu.VMEM((2, coarse, rows, cols), jnp.float32)],
    )
    columns = lax.all_to_all(send, SPACE, 0, 0, tiled=True)
    packed = (depth_c // 2, 2 * cols_c)
    lifted, offset, copies = call(
        spectrum_kernel,
        [(depth_c, 2 * cols_c), (depth_c, 2 * cols_c), (4, *packed)],
        [place, shift_x],
        columns, forward_z, denom,
    )
    gathered = lax.all_to_all(copies, "za", 0, 0, tiled=True)
    own_total, own_prefix = call(
        group_kernel, [packed, packed], [place, shift_x], gathered, denom
    )
    other_total = lax.ppermute(own_total, "zb", [(0, 1), (1, 0)])
    back = call(
        scan_kernel,
        (4 * rows_c, coarse, 4 * cols_c),
        [place, shift_x],
        own_total, other_total, own_prefix, lifted, offset, denom, inverse_z,
    )
    returned = lax.all_to_all(back, ("x", "y", "c"), 0, 0, tiled=True)
    out = call(
        finish_kernel, (5, planes, rows, cols), [place], w, returned, hats, up_x, up_y
    )
    return out[None]


def solution(mesh):
    finer = Mesh(mesh.devices.reshape(4, 2, 4, 4, 2, 2), TM + SPACE)
    in_specs = (P(TM, None, SPACE, None, None), P(SPACE, None, None))
    out_specs = P(TM, None, SPACE, None, None)
    return jax.shard_map(
        shards, mesh=finer, in_specs=in_specs, out_specs=out_specs, check_vma=False
    )
```

```python
import math

import jax
import jax.numpy as jnp
import numpy as np
from jax import lax
from jax.experimental import pallas as pl
from jax.experimental.pallas import tpu as pltpu
from jax.sharding import Mesh
from jax.sharding import PartitionSpec as P

TM = ("x", "zb", "za")
SPACE = ("y", "zh", "c")

step_length = 0.4
diffusion = 1.0
reaction = 1.0

G_AT = (0, 3, 5, 6)
U_AT = 6
PACK = 10
REACH = 4


def basis_coefficients(nodes, chosen):
    polynomial = [1.0]
    for other, point in enumerate(nodes):
        if other == chosen:
            continue
        divisor = nodes[chosen] - point
        widened = [0.0] * (len(polynomial) + 1)
        for power, value in enumerate(polynomial):
            widened[power + 1] += value / divisor
            widened[power] -= value * point / divisor
        polynomial = widened
    return polynomial


def basis_value(nodes, chosen, where):
    result = 1.0
    for other, point in enumerate(nodes):
        if other != chosen:
            result *= (where - point) / (nodes[chosen] - point)
    return result


def node_tables():
    root = math.sqrt(3.0 / 7.0)
    fine_tau = [0.0, (1.0 - root) / 2.0, 0.5, (1.0 + root) / 2.0, 1.0]
    coarse_tau = [0.0, 0.5, 1.0]
    integ = []
    for j in range(4):
        row_values = []
        for k in range(5):
            polynomial = basis_coefficients(fine_tau, k)
            total = 0.0
            for power, value in enumerate(polynomial):
                total += (
                    value
                    * (fine_tau[j + 1] ** (power + 1) - fine_tau[j] ** (power + 1))
                    / (power + 1)
                )
            row_values.append(total)
        integ.append(row_values)
    interp = [[basis_value(coarse_tau, c, fine_tau[m]) for c in range(3)] for m in range(5)]
    spacing = [float(fine_tau[j + 1] - fine_tau[j]) for j in range(4)]
    return integ, spacing, interp


INTEG, SPACING, INTERP = node_tables()
MIX = [
    [step_length * (INTEG[j][k] - (SPACING[j] if j == k else 0.0)) for k in range(5)]
    for j in range(4)
]
COUPLING = 0.5 * step_length * diffusion * 0.25
QUAD = [[step_length * (INTEG[2 * c][k] + INTEG[2 * c + 1][k]) for k in range(5)] for c in range(2)]


def hartley(length):
    counter = np.arange(length)
    phase = 2.0 * np.pi * (counter[:, None] * counter[None, :] % length) / length
    return (np.cos(phase) + np.sin(phase)) / math.sqrt(length)


def block_pair(table):
    rows, cols = table.shape
    both = np.zeros((2 * rows, 2 * cols))
    both[:rows, :cols] = table
    both[rows:, cols:] = table
    return both


def tables(planes, rows, cols, depth):
    rows_c, cols_c = rows // 2, cols // 2
    hx, hy, hz = hartley(rows_c), hartley(cols_c), hartley(depth)
    down_y = 0.5 * np.repeat(hy, 2, 0)
    up_y = np.repeat(hy, 2, 0).T
    wide_x = np.repeat(hx, 2, 0)
    down_x = np.zeros((rows_c, planes, planes, rows))
    up_x = np.zeros((planes, rows, rows_c, planes))
    for p in range(planes):
        down_x[:, p, p, :] = 0.25 * wide_x.T
        up_x[p, :, :, p] = wide_x
    down_x = down_x.reshape(rows_c * planes, planes * rows)
    up_x = up_x.reshape(planes * rows, rows_c * planes)
    cos_z = np.cos(2.0 * np.pi * np.arange(depth) / depth)
    cos_y = np.cos(2.0 * np.pi * np.arange(cols_c) / cols_c)
    half = COUPLING
    cos_x = np.cos(2.0 * np.pi * np.arange(rows_c) / rows_c)
    stencil = half * (6.0 - 2.0 * cos_x[:, None, None] - 2.0 * cos_y[None, None, :])
    stencil = np.broadcast_to(stencil, (rows_c, planes, cols_c)).reshape(-1, cols_c)
    stencil = np.concatenate([stencil, stencil], 1)
    blocks = depth // planes
    forward_z = np.zeros((depth, blocks, 2, planes))
    forward_z[:, :, 0, :] = hz.reshape(depth, blocks, planes)
    for s in range(blocks):
        forward_z[:, s, 1, 0] = hz[:, (s * planes - 1) % depth]
        forward_z[:, s, 1, planes - 1] = hz[:, (s * planes + planes) % depth]
    forward_z = forward_z.reshape(depth, -1)
    denom = 1.0 - half * (2.0 * cos_z[:, None] + 2.0 * cos_y[None, :] - 6.0)
    denom = np.concatenate([denom, denom], 1)
    shift_x = half * 2.0 * cos_x
    inverse_z = hz.reshape(4, 2, 2, planes, depth).transpose(1, 0, 2, 3, 4)
    inverse_z = inverse_z.reshape(2, 8 * planes, depth)
    f32 = lambda a: jnp.asarray(a, jnp.float32)
    return (
        f32(block_pair(down_y)), f32(down_x), f32(stencil), f32(forward_z), f32(inverse_z),
        f32(denom), f32(shift_x), f32(up_x), f32(block_pair(up_y)),
    )


def lanes_swapped(a):
    return pltpu.roll(a, a.shape[1] // 2, 1)


def left_half(a):
    return lax.broadcasted_iota(jnp.int32, a.shape, 1) < a.shape[1] // 2


def dot(a, b):
    return jnp.dot(a, b, precision=lax.Precision.HIGHEST, preferred_element_type=jnp.float32)


def plane_part(f):
    near = pltpu.roll(f, 1, 0) + pltpu.roll(f, f.shape[0] - 1, 0)
    near = near + pltpu.roll(f, 1, 1) + pltpu.roll(f, f.shape[1] - 1, 1)
    return diffusion * near - f * ((6.0 * diffusion - reaction) + reaction * (f * f))


def old_kernel(place, u, first, g, near, far, edge_far):
    planes = u.shape[1]
    position, core, slices = place[0], place[1], place[6]
    far_edge = pl.ds(core * (planes - REACH), REACH)

    @pl.when(position == slices - 1)
    def _():
        edge_far[...] = first[far_edge]

    @pl.when(position != slices - 1)
    def _():
        edge_far[...] = u[4, far_edge]

    for p in range(planes):
        total = [None] * 4
        for k in range(5):
            field = u[k, p]
            force = plane_part(field)
            if p > 0:
                force = force + diffusion * u[k, p - 1]
            if p < planes - 1:
                force = force + diffusion * u[k, p + 1]
            for j in range(4):
                term = MIX[j][k] * force
                total[j] = term if total[j] is None else total[j] + term
        for j in range(4):
            g[j, p] = total[j]

    def packed(out, plane_of):
        for j in range(4):
            for i in range(3 - j):
                out[G_AT[j] + i] = g[j, plane_of(i)]
            edge = plane_of(0)
            out[U_AT + j] = diffusion * sum(MIX[j][k] * u[k, edge] for k in range(5))

    top = lambda i: planes - 1 - i
    bottom = lambda i: i

    @pl.when(core == 0)
    def _():
        packed(near, top)
        packed(far, bottom)

    @pl.when(core != 0)
    def _():
        packed(near, bottom)
        packed(far, top)


def near_kernel(place, first, previous, own_near, out):
    position, core = place[0], place[1]
    edge = pl.ds((1 - core) * (first.shape[0] - REACH), REACH)
    out[:PACK] = own_near[...]

    @pl.when(position == 0)
    def _():
        out[PACK:] = first[edge]

    @pl.when(position != 0)
    def _():
        out[PACK:] = previous[edge]


def relay_kernel(halo, halo_out):
    halo_out[...] = halo[...]


def sweep_kernel(
    place, first, previous, near, start_far, g, own_near, own_far, got_far,
    down_y, down_x, stencil, w, send, hats, quad,
):
    got_near, start_near = near.at[:PACK], near.at[PACK:]
    planes = first.shape[0]
    coarse = planes // 2
    position, core = place[0], place[1]

    def with_sides(body):
        @pl.when(core == 0)
        def _():
            body(start_far, own_far, got_far, start_near, own_near, got_near)

        @pl.when(core != 0)
        def _():
            body(start_near, own_near, got_near, start_far, own_far, got_far)

    @pl.when(position == 0)
    def _():
        w[0, REACH : REACH + planes] = first[...]

    @pl.when(position != 0)
    def _():
        w[0, REACH : REACH + planes] = previous[...]

    def run(start_lo, own_lo, got_lo, start_hi, own_hi, got_hi):
        w[0, :REACH] = start_lo[...]
        w[0, REACH + planes :] = start_hi[...]
        for m in range(5):
            margin = max(3 - m, 0)
            held = None
            for p in range(-margin, planes + margin):
                at = p + REACH
                field = w[m, at]
                force = plane_part(field)
                if m < 4 or p > 0:
                    force = force + diffusion * w[m, at - 1]
                if m < 4 or p < planes - 1:
                    force = force + diffusion * w[m, at + 1]
                if m < 4:
                    if p < 0:
                        source = got_lo[G_AT[m] - p - 1]
                        if p == -1:
                            source = source + own_lo[U_AT + m]
                    elif p >= planes:
                        source = got_hi[G_AT[m] + p - planes]
                        if p == planes:
                            source = source + own_hi[U_AT + m]
                    else:
                        source = g[m, p]
                        if p == 0:
                            source = source + got_lo[U_AT + m]
                        if p == planes - 1:
                            source = source + got_hi[U_AT + m]
                    w[m + 1, at] = field + step_length * SPACING[m] * force + source
                if 0 <= p < planes:
                    if p % 2 == 0:
                        held = force
                    else:
                        both = held + force
                        for c in range(2):
                            term = QUAD[c][m] * both
                            quad[c, p // 2] = term if m == 0 else quad[c, p // 2] + term

    with_sides(run)

    def paired(m):
        return jnp.concatenate(
            [w[m, REACH + 2 * i] + w[m, REACH + 2 * i + 1] for i in range(coarse)], 0
        )

    rows = coarse * first.shape[1]
    restart = paired(0)
    mask = jnp.where(position == 0, 1.0, 0.0)
    q0 = quad[0].reshape(rows, -1) + mask * restart
    q1 = quad[1].reshape(rows, -1)
    table = down_y[...]
    edge_rows = first.shape[1]
    middle = jnp.zeros((rows - 2 * edge_rows, first.shape[2]), jnp.float32)
    edges = jnp.concatenate([w[4, REACH], middle, w[4, REACH + planes - 1]], 0)
    left = [
        dot(jnp.concatenate(pair, 1), table)
        for pair in ((q0, q1), (paired(2), paired(4)), (restart, edges))
    ]
    spectral = dot(down_x[...], jnp.concatenate(left, 1))
    width = left[0].shape[1]
    states = spectral[:, width : 2 * width]
    third = spectral[:, 2 * width :]
    count = spectral.shape[0]
    level = lax.broadcasted_iota(jnp.int32, states.shape, 0) % coarse
    near_z = jnp.where(level > 0, pltpu.roll(states, 1, 0), 0.0)
    near_z = near_z + jnp.where(level < coarse - 1, pltpu.roll(states, count - 1, 0), 0.0)
    inside = spectral[:, :width] + stencil[...] * states - COUPLING * near_z
    is_left = left_half(states)
    last = jnp.where(is_left, lanes_swapped(third), third)
    last = last * jnp.where(is_left, diffusion * QUAD[0][4], diffusion * QUAD[1][4])
    spill = last - COUPLING * states
    spill = jnp.where((level == 0) | (level == coarse - 1), spill, 0.0)
    for y in range(4):
        for c in range(2):
            kx = 2 * y + c
            span = slice(kx * coarse, (kx + 1) * coarse)
            for zh in range(2):
                send[4 * y + 2 * zh + c, :coarse] = inside[span]
                send[4 * y + 2 * zh + c, coarse:] = spill[span]
    hats[...] = spectral[:, width:]


def spectrum_kernel(place, shift_x, got, table, denom, lifted, offset, copies):
    depth = table.shape[0]
    half = depth // 2
    d = denom[...] - shift_x[place[4]]
    inv = 1.0 / d
    lift = dot(table[...], got[...].reshape(-1, d.shape[1]))
    weighted = lift * inv
    weighted = jnp.where(left_half(d), weighted * inv, weighted)
    total = weighted + lanes_swapped(weighted)
    lifted[...] = lift
    offset[...] = total
    packed = jnp.where(left_half(total[:half]), total[:half], total[half:])
    for i in range(copies.shape[0]):
        copies[i] = packed


def packed_inverse(place, shift_x, denom):
    d = denom[...] - shift_x[place[4]]
    inv = 1.0 / d
    half = inv.shape[0] // 2
    left = left_half(inv[:half])
    return inv, left, jnp.where(left, inv[:half], inv[half:])


def group_kernel(place, shift_x, offsets, denom, total_out, prefix_out):
    za = place[2]
    _, _, inv = packed_inverse(place, shift_x, denom)
    inv2 = inv * inv
    total = jnp.zeros_like(inv2)
    prefix = jnp.zeros_like(inv2)
    for m in range(offsets.shape[0]):
        piece = offsets[m]
        total = total * inv2 + piece
        prefix = jnp.where(m < za, prefix * inv2 + piece, prefix)
    total_out[...] = total
    prefix_out[...] = prefix


def scan_kernel(
    place, shift_x, own_total, other_total, own_prefix, lifted, offset, denom, inverse_z, out
):
    za, block, zh, zb = place[2], place[3], place[5], place[7]
    inv, left, inv_packed = packed_inverse(place, shift_x, denom)
    inv2 = inv_packed * inv_packed
    inv4 = inv2 * inv2
    inv8 = inv4 * inv4
    whole = inv8 * inv8
    power = jnp.where(za % 2 == 1, inv2, 1.0)
    power = jnp.where(za >= 2, power * inv4, power)
    early = jnp.where(zb == 0, own_total[...], other_total[...])
    late = jnp.where(zb == 0, other_total[...], own_total[...])
    prefix = own_prefix[...] + jnp.where(zb == 0, 0.0, power * early)
    total = early * inv8 + late
    power = jnp.where(zb == 0, power, power * inv8)
    inverse = inverse_z[zh]
    weights = jnp.where(left_half(inv), inv, inv * inv)
    own = jnp.where(left_half(inv), lifted[...] * inv, offset[...])
    carried = total * power
    targets = out.shape[0] // 8
    for xp in range(targets):
        packed = jnp.where(xp == block, prefix, jnp.where(xp > block, carried, 0.0))
        carried = jnp.where(xp > block, carried * whole, carried)
        turned = lanes_swapped(packed)
        begin = jnp.concatenate(
            [jnp.where(left, packed, turned), jnp.where(left, turned, packed)], 0
        )
        later = begin * weights + jnp.where(xp == block, own, 0.0)
        planar = dot(inverse, jnp.concatenate([later, begin], 1))
        out[8 * xp : 8 * xp + 8] = planar.reshape(8, -1, planar.shape[1])


def finish_kernel(place, w, got, hats, up_x, up_y, out):
    planes = out.shape[1]
    coarse = planes // 2
    rows = out.shape[2]
    cols = out.shape[3]
    total = got[0:8] + got[8:16] + (got[16:24] + got[24:32])
    delta = total.reshape(-1, total.shape[2]) - hats[...]
    half = delta.shape[1] // 2
    later = delta[:, :half]
    begin = jnp.where(place[0] == 0, 0.0, delta[:, half:])
    spread = dot(up_x[...], jnp.concatenate([later, begin], 1))
    table = up_y[...]
    after = dot(spread[:, :half], table)
    before = dot(spread[:, half:], table[:, :cols])
    parts = [before, after[:, :cols], after[:, cols:]]
    for m in range(5):
        mixed = None
        for c in range(3):
            weight = INTERP[m][c]
            if abs(weight) < 1e-14:
                continue
            term = parts[c] if weight == 1.0 else weight * parts[c]
            mixed = term if mixed is None else mixed + term
        for i in range(coarse):
            piece = mixed[i * rows : (i + 1) * rows]
            out[m, 2 * i] = w[m, REACH + 2 * i] + piece
            out[m, 2 * i + 1] = w[m, REACH + 2 * i + 1] + piece


def call(kernel, outs, scalars, *args, scratch=(), flops=0):
    smem = pl.BlockSpec(memory_space=pltpu.SMEM)
    vmem = pl.BlockSpec(memory_space=pltpu.VMEM)
    single = not isinstance(outs, list)
    shapes = [jax.ShapeDtypeStruct(s, jnp.float32) for s in ([outs] if single else outs)]
    result = pl.pallas_call(
        kernel,
        out_shape=shapes[0] if single else shapes,
        in_specs=[smem] * len(scalars) + [vmem] * len(args),
        out_specs=vmem if single else [vmem] * len(shapes),
        scratch_shapes=list(scratch),
        compiler_params=pltpu.CompilerParams(vmem_limit_bytes=32 * 1024 * 1024),
        cost_estimate=pl.CostEstimate(flops=flops, bytes_accessed=1 << 20, transcendentals=0),
    )(*scalars, *args)
    return result


def shards(u_old, u_init):
    planes, rows, cols = u_init.shape
    coarse, rows_c, cols_c = planes // 2, rows // 2, cols // 2
    slices = lax.axis_size(TM)
    blocks = lax.axis_size(SPACE)
    depth_c = coarse * blocks
    down_y, down_x, stencil, forward_z, inverse_z, denom, shift_x, up_x, up_y = tables(
        coarse, rows, cols, depth_c
    )
    position = lax.axis_index(TM)
    core = lax.axis_index("c")
    kx = 2 * lax.axis_index("y") + core
    place = [position, core, lax.axis_index("za"), lax.axis_index("x"), kx]
    place = jnp.stack(place + [lax.axis_index("zh"), slices, lax.axis_index("zb")])
    place = place.astype(jnp.int32)

    halo, edge = (PACK, rows, cols), (REACH, rows, cols)
    g, own_near, own_far, edge_far = call(
        old_kernel,
        [(4, planes, rows, cols), halo, halo, edge],
        [place],
        u_old[0], u_init,
        flops=10**11,
    )

    def far_block(s):
        return (s + 1) % blocks if s % 2 else (s - 1) % blocks

    across = [
        (n * blocks + s, (n + 1) % slices * blocks + far_block(s))
        for n in range(slices)
        for s in range(blocks)
    ]

    got_far = lax.ppermute(own_far, SPACE, [(s, far_block(s)) for s in range(blocks)])
    start_far = lax.ppermute(edge_far, TM + SPACE, across)
    got_far = call(relay_kernel, halo, [], got_far, flops=10**11)
    previous = lax.ppermute(u_old[0, 4], TM, [(i, i + 1) for i in range(slices - 1)])
    near_out = call(
        near_kernel, (PACK + REACH, rows, cols), [place], u_init, previous, own_near
    )
    near = lax.ppermute(near_out, "c", [(0, 1), (1, 0)])

    w, send, hats = call(
        sweep_kernel,
        [
            (5, planes + 2 * REACH, rows, cols),
            (blocks, 2 * coarse, 2 * cols_c),
            (rows_c * coarse, 4 * cols_c),
        ],
        [place],
        u_init, previous, near, start_far, g, own_near, own_far, got_far,
        down_y, down_x, stencil,
        scratch=[pltpu.VMEM((2, coarse, rows, cols), jnp.float32)],
    )
    columns = lax.all_to_all(send, SPACE, 0, 0, tiled=True)
    packed = (depth_c // 2, 2 * cols_c)
    lifted, offset, copies = call(
        spectrum_kernel,
        [(depth_c, 2 * cols_c), (depth_c, 2 * cols_c), (4, *packed)],
        [place, shift_x],
        columns, forward_z, denom,
    )
    gathered = lax.all_to_all(copies, "za", 0, 0, tiled=True)
    own_total, own_prefix = call(
        group_kernel, [packed, packed], [place, shift_x], gathered, denom
    )
    other_total = lax.ppermute(own_total, "zb", [(0, 1), (1, 0)])
    back = call(
        scan_kernel,
        (4 * rows_c, coarse, 4 * cols_c),
        [place, shift_x],
        own_total, other_total, own_prefix, lifted, offset, denom, inverse_z,
    )
    returned = lax.all_to_all(back, ("x", "y", "c"), 0, 0, tiled=True)
    out = call(
        finish_kernel, (5, planes, rows, cols), [place], w, returned, hats, up_x, up_y
    )
    return out[None]


def solution(mesh):
    finer = Mesh(mesh.devices.reshape(4, 2, 4, 4, 2, 2), TM + SPACE)
    in_specs = (P(TM, None, SPACE, None, None), P(SPACE, None, None))
    out_specs = P(TM, None, SPACE, None, None)
    return jax.shard_map(
        shards, mesh=finer, in_specs=in_specs, out_specs=out_specs, check_vma=False
    )
```

```python
import math

import jax
import jax.numpy as jnp
import numpy as np
from jax import lax
from jax.experimental import pallas as pl
from jax.experimental.pallas import tpu as pltpu
from jax.sharding import Mesh
from jax.sharding import PartitionSpec as P

TM = ("x", "zb", "za")
SPACE = ("y", "zh", "c")
FORWARD = ("zb", "y", "zh", "c")
ROWS = 10

step_length = 0.4
diffusion = 1.0
reaction = 1.0

G_AT = (0, 3, 5, 6)
U_AT = 6
PACK = 10
REACH = 4


def basis_coefficients(nodes, chosen):
    polynomial = [1.0]
    for other, point in enumerate(nodes):
        if other == chosen:
            continue
        divisor = nodes[chosen] - point
        widened = [0.0] * (len(polynomial) + 1)
        for power, value in enumerate(polynomial):
            widened[power + 1] += value / divisor
            widened[power] -= value * point / divisor
        polynomial = widened
    return polynomial


def basis_value(nodes, chosen, where):
    result = 1.0
    for other, point in enumerate(nodes):
        if other != chosen:
            result *= (where - point) / (nodes[chosen] - point)
    return result


def node_tables():
    root = math.sqrt(3.0 / 7.0)
    fine_tau = [0.0, (1.0 - root) / 2.0, 0.5, (1.0 + root) / 2.0, 1.0]
    coarse_tau = [0.0, 0.5, 1.0]
    integ = []
    for j in range(4):
        row_values = []
        for k in range(5):
            polynomial = basis_coefficients(fine_tau, k)
            total = 0.0
            for power, value in enumerate(polynomial):
                total += (
                    value
                    * (fine_tau[j + 1] ** (power + 1) - fine_tau[j] ** (power + 1))
                    / (power + 1)
                )
            row_values.append(total)
        integ.append(row_values)
    interp = [[basis_value(coarse_tau, c, fine_tau[m]) for c in range(3)] for m in range(5)]
    spacing = [float(fine_tau[j + 1] - fine_tau[j]) for j in range(4)]
    return integ, spacing, interp


INTEG, SPACING, INTERP = node_tables()
MIX = [
    [step_length * (INTEG[j][k] - (SPACING[j] if j == k else 0.0)) for k in range(5)]
    for j in range(4)
]
COUPLING = 0.5 * step_length * diffusion * 0.25
QUAD = [[step_length * (INTEG[2 * c][k] + INTEG[2 * c + 1][k]) for k in range(5)] for c in range(2)]


def hartley(length):
    counter = np.arange(length)
    phase = 2.0 * np.pi * (counter[:, None] * counter[None, :] % length) / length
    return (np.cos(phase) + np.sin(phase)) / math.sqrt(length)


def block_pair(table):
    rows, cols = table.shape
    both = np.zeros((2 * rows, 2 * cols))
    both[:rows, :cols] = table
    both[rows:, cols:] = table
    return both


def tables(planes, rows, cols, depth):
    rows_c, cols_c = rows // 2, cols // 2
    hx, hy, hz = hartley(rows_c), hartley(cols_c), hartley(depth)
    down_y = 0.5 * np.repeat(hy, 2, 0)
    up_y = np.repeat(hy, 2, 0).T
    wide_x = np.repeat(hx, 2, 0)
    down_x = np.zeros((rows_c, planes, planes, rows))
    up_x = np.zeros((planes, rows, rows_c, planes))
    for p in range(planes):
        down_x[:, p, p, :] = 0.25 * wide_x.T
        up_x[p, :, :, p] = wide_x
    down_x = down_x.reshape(rows_c * planes, planes * rows)
    up_x = up_x.reshape(planes * rows, rows_c * planes)
    cos_z = np.cos(2.0 * np.pi * np.arange(depth) / depth)
    cos_y = np.cos(2.0 * np.pi * np.arange(cols_c) / cols_c)
    half = COUPLING
    cos_x = np.cos(2.0 * np.pi * np.arange(rows_c) / rows_c)
    stencil = half * (6.0 - 2.0 * cos_x[:, None, None] - 2.0 * cos_y[None, None, :])
    stencil = np.broadcast_to(stencil, (rows_c, planes, cols_c)).reshape(-1, cols_c)
    stencil = np.concatenate([stencil, stencil], 1)
    blocks = depth // planes
    forward_z = np.zeros((depth, ROWS, blocks))
    for s in range(blocks):
        forward_z[:, :planes, s] = hz[:, s * planes : (s + 1) * planes]
        forward_z[:, planes, s] = hz[:, (s * planes - 1) % depth]
        forward_z[:, planes + 1, s] = hz[:, (s * planes + planes) % depth]
    forward_z = forward_z.reshape(depth, -1)
    denom = 1.0 - half * (2.0 * cos_z[:, None] + 2.0 * cos_y[None, :] - 6.0)
    denom = np.concatenate([denom, denom], 1)
    shift_x = half * 2.0 * cos_x
    inverse_z = hz.reshape(4, 2, 2, planes, depth).transpose(1, 0, 2, 3, 4)
    inverse_z = inverse_z.reshape(2, 8 * planes, depth)
    f32 = lambda a: jnp.asarray(a, jnp.float32)
    return (
        f32(block_pair(down_y)), f32(down_x), f32(stencil), f32(forward_z), f32(inverse_z),
        f32(denom), f32(shift_x), f32(up_x), f32(block_pair(up_y)),
    )


def lanes_swapped(a):
    return pltpu.roll(a, a.shape[1] // 2, 1)


def left_half(a):
    return lax.broadcasted_iota(jnp.int32, a.shape, 1) < a.shape[1] // 2


def dot(a, b):
    return jnp.dot(a, b, precision=lax.Precision.HIGHEST, preferred_element_type=jnp.float32)


def plane_part(f):
    near = pltpu.roll(f, 1, 0) + pltpu.roll(f, f.shape[0] - 1, 0)
    near = near + pltpu.roll(f, 1, 1) + pltpu.roll(f, f.shape[1] - 1, 1)
    return diffusion * near - f * ((6.0 * diffusion - reaction) + reaction * (f * f))


def last_kernel(u, last):
    last[...] = u[4]


def old_kernel(place, u, first, g, near, far, edge_far):
    planes = u.shape[1]
    position, core, slices = place[0], place[1], place[6]
    far_edge = pl.ds(core * (planes - REACH), REACH)

    @pl.when(position == slices - 1)
    def _():
        edge_far[...] = first[far_edge]

    @pl.when(position != slices - 1)
    def _():
        edge_far[...] = u[4, far_edge]

    for p in range(planes):
        total = [None] * 4
        for k in range(5):
            field = u[k, p]
            force = plane_part(field)
            if p > 0:
                force = force + diffusion * u[k, p - 1]
            if p < planes - 1:
                force = force + diffusion * u[k, p + 1]
            for j in range(4):
                term = MIX[j][k] * force
                total[j] = term if total[j] is None else total[j] + term
        for j in range(4):
            g[j, p] = total[j]

    def packed(out, plane_of):
        for j in range(4):
            for i in range(3 - j):
                out[G_AT[j] + i] = g[j, plane_of(i)]
            edge = plane_of(0)
            out[U_AT + j] = diffusion * sum(MIX[j][k] * u[k, edge] for k in range(5))

    top = lambda i: planes - 1 - i
    bottom = lambda i: i

    @pl.when(core == 0)
    def _():
        packed(near, top)
        packed(far, bottom)

    @pl.when(core != 0)
    def _():
        packed(near, bottom)
        packed(far, top)


def near_kernel(place, first, previous, own_near, out):
    position, core = place[0], place[1]
    edge = pl.ds((1 - core) * (first.shape[0] - REACH), REACH)
    out[:PACK] = own_near[...]

    @pl.when(position == 0)
    def _():
        out[PACK:] = first[edge]

    @pl.when(position != 0)
    def _():
        out[PACK:] = previous[edge]


def relay_kernel(halo, halo_out):
    halo_out[...] = halo[...]


def sweep_kernel(
    place, first, previous, near, start_far, g, own_near, own_far, got_far,
    down_y, down_x, stencil, w, send, hats, quad,
):
    got_near, start_near = near.at[:PACK], near.at[PACK:]
    planes = first.shape[0]
    coarse = planes // 2
    position, core = place[0], place[1]

    def with_sides(body):
        @pl.when(core == 0)
        def _():
            body(start_far, own_far, got_far, start_near, own_near, got_near)

        @pl.when(core != 0)
        def _():
            body(start_near, own_near, got_near, start_far, own_far, got_far)

    @pl.when(position == 0)
    def _():
        w[0, REACH : REACH + planes] = first[...]

    @pl.when(position != 0)
    def _():
        w[0, REACH : REACH + planes] = previous[...]

    def run(start_lo, own_lo, got_lo, start_hi, own_hi, got_hi):
        w[0, :REACH] = start_lo[...]
        w[0, REACH + planes :] = start_hi[...]
        for m in range(5):
            margin = max(3 - m, 0)
            held = None
            for p in range(-margin, planes + margin):
                at = p + REACH
                field = w[m, at]
                force = plane_part(field)
                if m < 4 or p > 0:
                    force = force + diffusion * w[m, at - 1]
                if m < 4 or p < planes - 1:
                    force = force + diffusion * w[m, at + 1]
                if m < 4:
                    if p < 0:
                        source = got_lo[G_AT[m] - p - 1]
                        if p == -1:
                            source = source + own_lo[U_AT + m]
                    elif p >= planes:
                        source = got_hi[G_AT[m] + p - planes]
                        if p == planes:
                            source = source + own_hi[U_AT + m]
                    else:
                        source = g[m, p]
                        if p == 0:
                            source = source + got_lo[U_AT + m]
                        if p == planes - 1:
                            source = source + got_hi[U_AT + m]
                    w[m + 1, at] = field + step_length * SPACING[m] * force + source
                if 0 <= p < planes:
                    if p % 2 == 0:
                        held = force
                    else:
                        both = held + force
                        for c in range(2):
                            term = QUAD[c][m] * both
                            quad[c, p // 2] = term if m == 0 else quad[c, p // 2] + term

    with_sides(run)

    def paired(m):
        return jnp.concatenate(
            [w[m, REACH + 2 * i] + w[m, REACH + 2 * i + 1] for i in range(coarse)], 0
        )

    rows = coarse * first.shape[1]
    restart = paired(0)
    mask = jnp.where(position == 0, 1.0, 0.0)
    q0 = quad[0].reshape(rows, -1) + mask * restart
    q1 = quad[1].reshape(rows, -1)
    table = down_y[...]
    edge_rows = first.shape[1]
    middle = jnp.zeros((rows - 2 * edge_rows, first.shape[2]), jnp.float32)
    edges = jnp.concatenate([w[4, REACH], middle, w[4, REACH + planes - 1]], 0)
    left = [
        dot(jnp.concatenate(pair, 1), table)
        for pair in ((q0, q1), (paired(2), paired(4)), (restart, edges))
    ]
    spectral = dot(down_x[...], jnp.concatenate(left, 1))
    width = left[0].shape[1]
    states = spectral[:, width : 2 * width]
    third = spectral[:, 2 * width :]
    count = spectral.shape[0]
    level = lax.broadcasted_iota(jnp.int32, states.shape, 0) % coarse
    near_z = jnp.where(level > 0, pltpu.roll(states, 1, 0), 0.0)
    near_z = near_z + jnp.where(level < coarse - 1, pltpu.roll(states, count - 1, 0), 0.0)
    inside = spectral[:, :width] + stencil[...] * states - COUPLING * near_z
    is_left = left_half(states)
    last = jnp.where(is_left, lanes_swapped(third), third)
    last = last * jnp.where(is_left, diffusion * QUAD[0][4], diffusion * QUAD[1][4])
    spill = last - COUPLING * states
    spill = jnp.where((level == 0) | (level == coarse - 1), spill, 0.0)
    for y in range(4):
        for c in range(2):
            kx = 2 * y + c
            at = kx * coarse
            lines = [inside[at + p : at + p + 1] for p in range(coarse)]
            lines += [spill[at : at + 1], spill[at + coarse - 1 : at + coarse]]
            for zb in range(2):
                for zh in range(2):
                    peer = 16 * zb + 4 * y + 2 * zh + c
                    for r in range(ROWS):
                        send[peer, :, r * width : (r + 1) * width] = lines[r]
    hats[...] = spectral[:, width:]


def spectrum_kernel(place, shift_x, got, table, denom, lifted, offset, copies, lines):
    zb = place[7]
    depth = table.shape[0]
    half = depth // 2
    d = denom[...] - shift_x[place[4]]
    inv = 1.0 / d
    width = d.shape[1]
    blocks = got.shape[0] // 2
    for part in range(2):
        for r in range(ROWS):
            span = slice(r * width, (r + 1) * width)
            for s in range(blocks):
                at = r * blocks + s
                lines[at : at + 1, part * width : (part + 1) * width] = got[part * blocks + s, :, span]
    both = dot(table[...], lines[...])
    totals = []
    for part in range(2):
        lift = both[:, part * width : (part + 1) * width]
        weighted = lift * inv
        weighted = jnp.where(left_half(d), weighted * inv, weighted)
        total = weighted + lanes_swapped(weighted)
        totals.append(total)
        packed = jnp.where(left_half(total[:half]), total[:half], total[half:])
        for i in range(copies.shape[0]):
            copies[i, part * half : (part + 1) * half] = packed
    lifted[...] = jnp.where(zb == 0, both[:, :width], both[:, width:])
    offset[...] = jnp.where(zb == 0, totals[0], totals[1])


def packed_inverse(place, shift_x, denom):
    d = denom[...] - shift_x[place[4]]
    inv = 1.0 / d
    half = inv.shape[0] // 2
    left = left_half(inv[:half])
    return inv, left, jnp.where(left, inv[:half], inv[half:])


def scan_kernel(place, shift_x, offsets, lifted, offset, denom, inverse_z, out):
    za, block, zh, zb = place[2], place[3], place[5], place[7]
    half = denom.shape[0] // 2
    inv, left, inv_packed = packed_inverse(place, shift_x, denom)
    inv2 = inv_packed * inv_packed
    inv4 = inv2 * inv2
    inv8 = inv4 * inv4
    whole = inv8 * inv8
    slice_at = zb * 4 + za
    prefix = jnp.zeros_like(inv2)
    total = jnp.zeros_like(inv2)
    for m in range(8):
        piece = offsets[m % 4, (m // 4) * half : (m // 4 + 1) * half]
        total = total * inv2 + piece
        prefix = jnp.where(m < slice_at, prefix * inv2 + piece, prefix)
    power = jnp.where(za % 2 == 1, inv2, 1.0)
    power = jnp.where(za >= 2, power * inv4, power)
    power = jnp.where(zb == 0, power, power * inv8)
    inverse = inverse_z[zh]
    weights = jnp.where(left_half(inv), inv, inv * inv)
    own = jnp.where(left_half(inv), lifted[...] * inv, offset[...])
    carried = total * power
    targets = out.shape[0] // 8
    for xp in range(targets):
        packed = jnp.where(xp == block, prefix, jnp.where(xp > block, carried, 0.0))
        carried = jnp.where(xp > block, carried * whole, carried)
        turned = lanes_swapped(packed)
        begin = jnp.concatenate(
            [jnp.where(left, packed, turned), jnp.where(left, turned, packed)], 0
        )
        later = begin * weights + jnp.where(xp == block, own, 0.0)
        planar = dot(inverse, jnp.concatenate([later, begin], 1))
        out[8 * xp : 8 * xp + 8] = planar.reshape(8, -1, planar.shape[1])


def finish_kernel(place, w, got, hats, up_x, up_y, out):
    planes = out.shape[1]
    coarse = planes // 2
    rows = out.shape[2]
    cols = out.shape[3]
    total = got[0:8] + got[8:16] + (got[16:24] + got[24:32])
    delta = total.reshape(-1, total.shape[2]) - hats[...]
    half = delta.shape[1] // 2
    later = delta[:, :half]
    begin = jnp.where(place[0] == 0, 0.0, delta[:, half:])
    spread = dot(up_x[...], jnp.concatenate([later, begin], 1))
    table = up_y[...]
    after = dot(spread[:, :half], table)
    before = dot(spread[:, half:], table[:, :cols])
    parts = [before, after[:, :cols], after[:, cols:]]
    for m in range(5):
        mixed = None
        for c in range(3):
            weight = INTERP[m][c]
            if abs(weight) < 1e-14:
                continue
            term = parts[c] if weight == 1.0 else weight * parts[c]
            mixed = term if mixed is None else mixed + term
        for i in range(coarse):
            piece = mixed[i * rows : (i + 1) * rows]
            out[m, 2 * i] = w[m, REACH + 2 * i] + piece
            out[m, 2 * i + 1] = w[m, REACH + 2 * i + 1] + piece


def call(kernel, outs, scalars, *args, scratch=(), flops=0):
    smem = pl.BlockSpec(memory_space=pltpu.SMEM)
    vmem = pl.BlockSpec(memory_space=pltpu.VMEM)
    single = not isinstance(outs, list)
    shapes = [jax.ShapeDtypeStruct(s, jnp.float32) for s in ([outs] if single else outs)]
    result = pl.pallas_call(
        kernel,
        out_shape=shapes[0] if single else shapes,
        in_specs=[smem] * len(scalars) + [vmem] * len(args),
        out_specs=vmem if single else [vmem] * len(shapes),
        scratch_shapes=list(scratch),
        compiler_params=pltpu.CompilerParams(vmem_limit_bytes=32 * 1024 * 1024),
        cost_estimate=pl.CostEstimate(flops=flops, bytes_accessed=1 << 20, transcendentals=0),
    )(*scalars, *args)
    return result


def shards(u_old, u_init):
    planes, rows, cols = u_init.shape
    coarse, rows_c, cols_c = planes // 2, rows // 2, cols // 2
    slices = lax.axis_size(TM)
    blocks = lax.axis_size(SPACE)
    depth_c = coarse * blocks
    down_y, down_x, stencil, forward_z, inverse_z, denom, shift_x, up_x, up_y = tables(
        coarse, rows, cols, depth_c
    )
    position = lax.axis_index(TM)
    core = lax.axis_index("c")
    kx = 2 * lax.axis_index("y") + core
    place = [position, core, lax.axis_index("za"), lax.axis_index("x"), kx]
    place = jnp.stack(place + [lax.axis_index("zh"), slices, lax.axis_index("zb")])
    place = place.astype(jnp.int32)

    last = call(last_kernel, (planes, rows, cols), [], u_old[0])
    halo, edge = (PACK, rows, cols), (REACH, rows, cols)
    g, own_near, own_far, edge_far = call(
        old_kernel,
        [(4, planes, rows, cols), halo, halo, edge],
        [place],
        u_old[0], u_init,
        flops=10**11,
    )

    def far_block(s):
        return (s + 1) % blocks if s % 2 else (s - 1) % blocks

    across = [
        (n * blocks + s, (n + 1) % slices * blocks + far_block(s))
        for n in range(slices)
        for s in range(blocks)
    ]

    got_far = lax.ppermute(own_far, SPACE, [(s, far_block(s)) for s in range(blocks)])
    start_far = lax.ppermute(edge_far, TM + SPACE, across)
    got_far = call(relay_kernel, halo, [], got_far, flops=10**11)
    previous = lax.ppermute(last, TM, [(i, i + 1) for i in range(slices - 1)])
    near_out = call(
        near_kernel, (PACK + REACH, rows, cols), [place], u_init, previous, own_near
    )
    near = lax.ppermute(near_out, "c", [(0, 1), (1, 0)])

    w, send, hats = call(
        sweep_kernel,
        [
            (5, planes + 2 * REACH, rows, cols),
            (2 * blocks, 1, ROWS * 2 * cols_c),
            (rows_c * coarse, 4 * cols_c),
        ],
        [place],
        u_init, previous, near, start_far, g, own_near, own_far, got_far,
        down_y, down_x, stencil,
        scratch=[pltpu.VMEM((2, coarse, rows, cols), jnp.float32)],
    )
    columns = lax.all_to_all(send, FORWARD, 0, 0, tiled=True)
    lifted, offset, copies = call(
        spectrum_kernel,
        [(depth_c, 2 * cols_c), (depth_c, 2 * cols_c), (4, depth_c, 2 * cols_c)],
        [place, shift_x],
        columns, forward_z, denom,
        scratch=[pltpu.VMEM((ROWS * blocks, 4 * cols_c), jnp.float32)],
    )
    gathered = lax.all_to_all(copies, "za", 0, 0, tiled=True)
    back = call(
        scan_kernel,
        (4 * rows_c, coarse, 4 * cols_c),
        [place, shift_x],
        gathered, lifted, offset, denom, inverse_z,
    )
    returned = lax.all_to_all(back, ("x", "y", "c"), 0, 0, tiled=True)
    out = call(
        finish_kernel, (5, planes, rows, cols), [place], w, returned, hats, up_x, up_y
    )
    return out[None]


def solution(mesh):
    finer = Mesh(mesh.devices.reshape(4, 2, 4, 4, 2, 2), TM + SPACE)
    in_specs = (P(TM, None, SPACE, None, None), P(SPACE, None, None))
    out_specs = P(TM, None, SPACE, None, None)
    return jax.shard_map(
        shards, mesh=finer, in_specs=in_specs, out_specs=out_specs, check_vma=False
    )
```

```python
import math

import jax
import jax.numpy as jnp
import numpy as np
from jax import lax
from jax.experimental import pallas as pl
from jax.experimental.pallas import tpu as pltpu
from jax.sharding import Mesh
from jax.sharding import PartitionSpec as P

TM = ("x", "zb", "za")
SPACE = ("y", "zh", "c")
FORWARD = ("zb", "y", "zh", "c")
ROWS = 10

step_length = 0.4
diffusion = 1.0
reaction = 1.0

G_AT = (0, 3, 5, 6)
U_AT = 6
PACK = 10
REACH = 4


def basis_coefficients(nodes, chosen):
    polynomial = [1.0]
    for other, point in enumerate(nodes):
        if other == chosen:
            continue
        divisor = nodes[chosen] - point
        widened = [0.0] * (len(polynomial) + 1)
        for power, value in enumerate(polynomial):
            widened[power + 1] += value / divisor
            widened[power] -= value * point / divisor
        polynomial = widened
    return polynomial


def basis_value(nodes, chosen, where):
    result = 1.0
    for other, point in enumerate(nodes):
        if other != chosen:
            result *= (where - point) / (nodes[chosen] - point)
    return result


def node_tables():
    root = math.sqrt(3.0 / 7.0)
    fine_tau = [0.0, (1.0 - root) / 2.0, 0.5, (1.0 + root) / 2.0, 1.0]
    coarse_tau = [0.0, 0.5, 1.0]
    integ = []
    for j in range(4):
        row_values = []
        for k in range(5):
            polynomial = basis_coefficients(fine_tau, k)
            total = 0.0
            for power, value in enumerate(polynomial):
                total += (
                    value
                    * (fine_tau[j + 1] ** (power + 1) - fine_tau[j] ** (power + 1))
                    / (power + 1)
                )
            row_values.append(total)
        integ.append(row_values)
    interp = [[basis_value(coarse_tau, c, fine_tau[m]) for c in range(3)] for m in range(5)]
    spacing = [float(fine_tau[j + 1] - fine_tau[j]) for j in range(4)]
    return integ, spacing, interp


INTEG, SPACING, INTERP = node_tables()
MIX = [
    [step_length * (INTEG[j][k] - (SPACING[j] if j == k else 0.0)) for k in range(5)]
    for j in range(4)
]
COUPLING = 0.5 * step_length * diffusion * 0.25
QUAD = [[step_length * (INTEG[2 * c][k] + INTEG[2 * c + 1][k]) for k in range(5)] for c in range(2)]


def hartley(length):
    counter = np.arange(length)
    phase = 2.0 * np.pi * (counter[:, None] * counter[None, :] % length) / length
    return (np.cos(phase) + np.sin(phase)) / math.sqrt(length)


def block_pair(table):
    rows, cols = table.shape
    both = np.zeros((2 * rows, 2 * cols))
    both[:rows, :cols] = table
    both[rows:, cols:] = table
    return both


def tables(planes, rows, cols, depth):
    rows_c, cols_c = rows // 2, cols // 2
    hx, hy, hz = hartley(rows_c), hartley(cols_c), hartley(depth)
    down_y = 0.5 * np.repeat(hy, 2, 0)
    up_y = np.repeat(hy, 2, 0).T
    wide_x = np.repeat(hx, 2, 0)
    down_x = np.zeros((rows_c, planes, planes, rows))
    up_x = np.zeros((planes, rows, rows_c, planes))
    for p in range(planes):
        down_x[:, p, p, :] = 0.25 * wide_x.T
        up_x[p, :, :, p] = wide_x
    down_x = down_x.reshape(rows_c * planes, planes * rows)
    up_x = up_x.reshape(planes * rows, rows_c * planes)
    cos_z = np.cos(2.0 * np.pi * np.arange(depth) / depth)
    cos_y = np.cos(2.0 * np.pi * np.arange(cols_c) / cols_c)
    half = COUPLING
    cos_x = np.cos(2.0 * np.pi * np.arange(rows_c) / rows_c)
    stencil = half * (6.0 - 2.0 * cos_x[:, None, None] - 2.0 * cos_y[None, None, :])
    stencil = np.broadcast_to(stencil, (rows_c, planes, cols_c)).reshape(-1, cols_c)
    stencil = np.concatenate([stencil, stencil], 1)
    blocks = depth // planes
    forward_z = np.zeros((depth, ROWS, blocks))
    for s in range(blocks):
        forward_z[:, :planes, s] = hz[:, s * planes : (s + 1) * planes]
        forward_z[:, planes, s] = hz[:, (s * planes - 1) % depth]
        forward_z[:, planes + 1, s] = hz[:, (s * planes + planes) % depth]
    forward_z = forward_z.reshape(depth, -1)
    denom = 1.0 - half * (2.0 * cos_z[:, None] + 2.0 * cos_y[None, :] - 6.0)
    denom = np.concatenate([denom, denom], 1)
    shift_x = half * 2.0 * cos_x
    inverse_z = hz.reshape(4, 2, 2, planes, depth).transpose(1, 0, 2, 3, 4)
    inverse_z = inverse_z.reshape(2, 8 * planes, depth)
    f32 = lambda a: jnp.asarray(a, jnp.float32)
    return (
        table_halves(block_pair(down_y), 0), table_halves(down_x, 1), f32(stencil),
        table_halves(forward_z, 1), table_halves(inverse_z, 2), f32(denom), f32(shift_x),
        table_halves(up_x, 1), table_halves(block_pair(up_y), 0),
    )


def lanes_swapped(a):
    return pltpu.roll(a, a.shape[1] // 2, 1)


def left_half(a):
    return lax.broadcasted_iota(jnp.int32, a.shape, 1) < a.shape[1] // 2


def halves(a):
    high = a.astype(jnp.bfloat16)
    return high, (a - high.astype(jnp.float32)).astype(jnp.bfloat16)


def table_halves(table, axis):
    table = np.asarray(table, np.float32)
    high = table.astype(jnp.bfloat16)
    low = (table - high.astype(np.float32)).astype(jnp.bfloat16)
    return jnp.asarray(np.concatenate([high, high, low], axis))


def table_times(table, b):
    high, low = halves(b)
    parts = jnp.concatenate([high, low, high], 0)
    return jnp.dot(table, parts, preferred_element_type=jnp.float32)


def times_table(a, table):
    high, low = halves(a)
    parts = jnp.concatenate([high, low, high], 1)
    return jnp.dot(parts, table, preferred_element_type=jnp.float32)


def plane_part(f):
    near = pltpu.roll(f, 1, 0) + pltpu.roll(f, f.shape[0] - 1, 0)
    near = near + pltpu.roll(f, 1, 1) + pltpu.roll(f, f.shape[1] - 1, 1)
    return diffusion * near - f * ((6.0 * diffusion - reaction) + reaction * (f * f))


def last_kernel(u, last):
    last[...] = u[4]


def old_kernel(place, u, first, g, near, far, edge_far):
    planes = u.shape[1]
    position, core, slices = place[0], place[1], place[6]
    far_edge = pl.ds(core * (planes - REACH), REACH)

    @pl.when(position == slices - 1)
    def _():
        edge_far[...] = first[far_edge]

    @pl.when(position != slices - 1)
    def _():
        edge_far[...] = u[4, far_edge]

    for p in range(planes):
        total = [None] * 4
        for k in range(5):
            field = u[k, p]
            force = plane_part(field)
            if p > 0:
                force = force + diffusion * u[k, p - 1]
            if p < planes - 1:
                force = force + diffusion * u[k, p + 1]
            for j in range(4):
                term = MIX[j][k] * force
                total[j] = term if total[j] is None else total[j] + term
        for j in range(4):
            g[j, p] = total[j]

    def packed(out, plane_of):
        for j in range(4):
            for i in range(3 - j):
                out[G_AT[j] + i] = g[j, plane_of(i)]
            edge = plane_of(0)
            out[U_AT + j] = diffusion * sum(MIX[j][k] * u[k, edge] for k in range(5))

    top = lambda i: planes - 1 - i
    bottom = lambda i: i

    @pl.when(core == 0)
    def _():
        packed(near, top)
        packed(far, bottom)

    @pl.when(core != 0)
    def _():
        packed(near, bottom)
        packed(far, top)


def near_kernel(place, first, previous, own_near, out):
    position, core = place[0], place[1]
    edge = pl.ds((1 - core) * (first.shape[0] - REACH), REACH)
    out[:PACK] = own_near[...]

    @pl.when(position == 0)
    def _():
        out[PACK:] = first[edge]

    @pl.when(position != 0)
    def _():
        out[PACK:] = previous[edge]


def relay_kernel(halo, halo_out):
    halo_out[...] = halo[...]


def sweep_kernel(
    place, first, previous, near, start_far, g, own_near, own_far, got_far,
    down_y, down_x, stencil, w, send, hats, quad,
):
    got_near, start_near = near.at[:PACK], near.at[PACK:]
    planes = first.shape[0]
    coarse = planes // 2
    position, core = place[0], place[1]

    def with_sides(body):
        @pl.when(core == 0)
        def _():
            body(start_far, own_far, got_far, start_near, own_near, got_near)

        @pl.when(core != 0)
        def _():
            body(start_near, own_near, got_near, start_far, own_far, got_far)

    @pl.when(position == 0)
    def _():
        w[0, REACH : REACH + planes] = first[...]

    @pl.when(position != 0)
    def _():
        w[0, REACH : REACH + planes] = previous[...]

    def run(start_lo, own_lo, got_lo, start_hi, own_hi, got_hi):
        w[0, :REACH] = start_lo[...]
        w[0, REACH + planes :] = start_hi[...]
        for m in range(5):
            margin = max(3 - m, 0)
            held = None
            for p in range(-margin, planes + margin):
                at = p + REACH
                field = w[m, at]
                force = plane_part(field)
                if m < 4 or p > 0:
                    force = force + diffusion * w[m, at - 1]
                if m < 4 or p < planes - 1:
                    force = force + diffusion * w[m, at + 1]
                if m < 4:
                    if p < 0:
                        source = got_lo[G_AT[m] - p - 1]
                        if p == -1:
                            source = source + own_lo[U_AT + m]
                    elif p >= planes:
                        source = got_hi[G_AT[m] + p - planes]
                        if p == planes:
                            source = source + own_hi[U_AT + m]
                    else:
                        source = g[m, p]
                        if p == 0:
                            source = source + got_lo[U_AT + m]
                        if p == planes - 1:
                            source = source + got_hi[U_AT + m]
                    w[m + 1, at] = field + step_length * SPACING[m] * force + source
                if 0 <= p < planes:
                    if p % 2 == 0:
                        held = force
                    else:
                        both = held + force
                        for c in range(2):
                            term = QUAD[c][m] * both
                            quad[c, p // 2] = term if m == 0 else quad[c, p // 2] + term

    with_sides(run)

    def paired(m):
        return jnp.concatenate(
            [w[m, REACH + 2 * i] + w[m, REACH + 2 * i + 1] for i in range(coarse)], 0
        )

    rows = coarse * first.shape[1]
    restart = paired(0)
    mask = jnp.where(position == 0, 1.0, 0.0)
    q0 = quad[0].reshape(rows, -1) + mask * restart
    q1 = quad[1].reshape(rows, -1)
    table = down_y[...]
    edge_rows = first.shape[1]
    middle = jnp.zeros((rows - 2 * edge_rows, first.shape[2]), jnp.float32)
    edges = jnp.concatenate([w[4, REACH], middle, w[4, REACH + planes - 1]], 0)
    left = [
        times_table(jnp.concatenate(pair, 1), table)
        for pair in ((q0, q1), (paired(2), paired(4)), (restart, edges))
    ]
    spectral = table_times(down_x[...], jnp.concatenate(left, 1))
    width = left[0].shape[1]
    states = spectral[:, width : 2 * width]
    third = spectral[:, 2 * width :]
    count = spectral.shape[0]
    level = lax.broadcasted_iota(jnp.int32, states.shape, 0) % coarse
    near_z = jnp.where(level > 0, pltpu.roll(states, 1, 0), 0.0)
    near_z = near_z + jnp.where(level < coarse - 1, pltpu.roll(states, count - 1, 0), 0.0)
    inside = spectral[:, :width] + stencil[...] * states - COUPLING * near_z
    is_left = left_half(states)
    last = jnp.where(is_left, lanes_swapped(third), third)
    last = last * jnp.where(is_left, diffusion * QUAD[0][4], diffusion * QUAD[1][4])
    spill = last - COUPLING * states
    spill = jnp.where((level == 0) | (level == coarse - 1), spill, 0.0)
    for y in range(4):
        for c in range(2):
            kx = 2 * y + c
            at = kx * coarse
            lines = [inside[at + p : at + p + 1] for p in range(coarse)]
            lines += [spill[at : at + 1], spill[at + coarse - 1 : at + coarse]]
            for zb in range(2):
                for zh in range(2):
                    peer = 16 * zb + 4 * y + 2 * zh + c
                    for r in range(ROWS):
                        send[peer, :, r * width : (r + 1) * width] = lines[r]
    hats[...] = spectral[:, width:]


def spectrum_kernel(place, shift_x, got, table, denom, lifted, offset, copies, lines):
    zb = place[7]
    depth = table.shape[0]
    half = depth // 2
    d = denom[...] - shift_x[place[4]]
    inv = 1.0 / d
    width = d.shape[1]
    blocks = got.shape[0] // 2
    for part in range(2):
        for r in range(ROWS):
            span = slice(r * width, (r + 1) * width)
            for s in range(blocks):
                at = r * blocks + s
                lines[at : at + 1, part * width : (part + 1) * width] = got[part * blocks + s, :, span]
    both = table_times(table[...], lines[...])
    totals = []
    for part in range(2):
        lift = both[:, part * width : (part + 1) * width]
        weighted = lift * inv
        weighted = jnp.where(left_half(d), weighted * inv, weighted)
        total = weighted + lanes_swapped(weighted)
        totals.append(total)
        packed = jnp.where(left_half(total[:half]), total[:half], total[half:])
        for i in range(copies.shape[0]):
            copies[i, part * half : (part + 1) * half] = packed
    lifted[...] = jnp.where(zb == 0, both[:, :width], both[:, width:])
    offset[...] = jnp.where(zb == 0, totals[0], totals[1])


def packed_inverse(place, shift_x, denom):
    d = denom[...] - shift_x[place[4]]
    inv = 1.0 / d
    half = inv.shape[0] // 2
    left = left_half(inv[:half])
    return inv, left, jnp.where(left, inv[:half], inv[half:])


def scan_kernel(place, shift_x, offsets, lifted, offset, denom, inverse_z, out):
    za, block, zh, zb = place[2], place[3], place[5], place[7]
    half = denom.shape[0] // 2
    inv, left, inv_packed = packed_inverse(place, shift_x, denom)
    inv2 = inv_packed * inv_packed
    inv4 = inv2 * inv2
    inv8 = inv4 * inv4
    whole = inv8 * inv8
    slice_at = zb * 4 + za
    prefix = jnp.zeros_like(inv2)
    total = jnp.zeros_like(inv2)
    for m in range(8):
        piece = offsets[m % 4, (m // 4) * half : (m // 4 + 1) * half]
        total = total * inv2 + piece
        prefix = jnp.where(m < slice_at, prefix * inv2 + piece, prefix)
    power = jnp.where(za % 2 == 1, inv2, 1.0)
    power = jnp.where(za >= 2, power * inv4, power)
    power = jnp.where(zb == 0, power, power * inv8)
    inverse = inverse_z[zh]
    weights = jnp.where(left_half(inv), inv, inv * inv)
    own = jnp.where(left_half(inv), lifted[...] * inv, offset[...])
    carried = total * power
    targets = out.shape[0] // 8
    for xp in range(targets):
        packed = jnp.where(xp == block, prefix, jnp.where(xp > block, carried, 0.0))
        carried = jnp.where(xp > block, carried * whole, carried)
        turned = lanes_swapped(packed)
        begin = jnp.concatenate(
            [jnp.where(left, packed, turned), jnp.where(left, turned, packed)], 0
        )
        later = begin * weights + jnp.where(xp == block, own, 0.0)
        planar = table_times(inverse, jnp.concatenate([later, begin], 1))
        out[8 * xp : 8 * xp + 8] = planar.reshape(8, -1, planar.shape[1])


def finish_kernel(place, w, got, hats, up_x, up_y, out):
    planes = out.shape[1]
    coarse = planes // 2
    rows = out.shape[2]
    cols = out.shape[3]
    total = got[0:8] + got[8:16] + (got[16:24] + got[24:32])
    delta = total.reshape(-1, total.shape[2]) - hats[...]
    half = delta.shape[1] // 2
    later = delta[:, :half]
    begin = jnp.where(place[0] == 0, 0.0, delta[:, half:])
    spread = table_times(up_x[...], jnp.concatenate([later, begin], 1))
    table = up_y[...]
    after = times_table(spread[:, :half], table)
    before = times_table(spread[:, half:], table[:, :cols])
    parts = [before, after[:, :cols], after[:, cols:]]
    for m in range(5):
        mixed = None
        for c in range(3):
            weight = INTERP[m][c]
            if abs(weight) < 1e-14:
                continue
            term = parts[c] if weight == 1.0 else weight * parts[c]
            mixed = term if mixed is None else mixed + term
        for i in range(coarse):
            piece = mixed[i * rows : (i + 1) * rows]
            out[m, 2 * i] = w[m, REACH + 2 * i] + piece
            out[m, 2 * i + 1] = w[m, REACH + 2 * i + 1] + piece


def call(kernel, outs, scalars, *args, scratch=(), flops=0):
    smem = pl.BlockSpec(memory_space=pltpu.SMEM)
    vmem = pl.BlockSpec(memory_space=pltpu.VMEM)
    single = not isinstance(outs, list)
    shapes = [jax.ShapeDtypeStruct(s, jnp.float32) for s in ([outs] if single else outs)]
    result = pl.pallas_call(
        kernel,
        out_shape=shapes[0] if single else shapes,
        in_specs=[smem] * len(scalars) + [vmem] * len(args),
        out_specs=vmem if single else [vmem] * len(shapes),
        scratch_shapes=list(scratch),
        compiler_params=pltpu.CompilerParams(vmem_limit_bytes=32 * 1024 * 1024),
        cost_estimate=pl.CostEstimate(flops=flops, bytes_accessed=1 << 20, transcendentals=0),
    )(*scalars, *args)
    return result


def shards(u_old, u_init):
    planes, rows, cols = u_init.shape
    coarse, rows_c, cols_c = planes // 2, rows // 2, cols // 2
    slices = lax.axis_size(TM)
    blocks = lax.axis_size(SPACE)
    depth_c = coarse * blocks
    down_y, down_x, stencil, forward_z, inverse_z, denom, shift_x, up_x, up_y = tables(
        coarse, rows, cols, depth_c
    )
    position = lax.axis_index(TM)
    core = lax.axis_index("c")
    kx = 2 * lax.axis_index("y") + core
    place = [position, core, lax.axis_index("za"), lax.axis_index("x"), kx]
    place = jnp.stack(place + [lax.axis_index("zh"), slices, lax.axis_index("zb")])
    place = place.astype(jnp.int32)

    last = call(last_kernel, (planes, rows, cols), [], u_old[0])
    halo, edge = (PACK, rows, cols), (REACH, rows, cols)
    g, own_near, own_far, edge_far = call(
        old_kernel,
        [(4, planes, rows, cols), halo, halo, edge],
        [place],
        u_old[0], u_init,
        flops=10**11,
    )

    def far_block(s):
        return (s + 1) % blocks if s % 2 else (s - 1) % blocks

    across = [
        (n * blocks + s, (n + 1) % slices * blocks + far_block(s))
        for n in range(slices)
        for s in range(blocks)
    ]

    got_far = lax.ppermute(own_far, SPACE, [(s, far_block(s)) for s in range(blocks)])
    start_far = lax.ppermute(edge_far, TM + SPACE, across)
    got_far = call(relay_kernel, halo, [], got_far, flops=10**11)
    previous = lax.ppermute(last, TM, [(i, i + 1) for i in range(slices - 1)])
    near_out = call(
        near_kernel, (PACK + REACH, rows, cols), [place], u_init, previous, own_near
    )
    near = lax.ppermute(near_out, "c", [(0, 1), (1, 0)])

    w, send, hats = call(
        sweep_kernel,
        [
            (5, planes + 2 * REACH, rows, cols),
            (2 * blocks, 1, ROWS * 2 * cols_c),
            (rows_c * coarse, 4 * cols_c),
        ],
        [place],
        u_init, previous, near, start_far, g, own_near, own_far, got_far,
        down_y, down_x, stencil,
        scratch=[pltpu.VMEM((2, coarse, rows, cols), jnp.float32)],
    )
    columns = lax.all_to_all(send, FORWARD, 0, 0, tiled=True)
    lifted, offset, copies = call(
        spectrum_kernel,
        [(depth_c, 2 * cols_c), (depth_c, 2 * cols_c), (4, depth_c, 2 * cols_c)],
        [place, shift_x],
        columns, forward_z, denom,
        scratch=[pltpu.VMEM((ROWS * blocks, 4 * cols_c), jnp.float32)],
    )
    gathered = lax.all_to_all(copies, "za", 0, 0, tiled=True)
    back = call(
        scan_kernel,
        (4 * rows_c, coarse, 4 * cols_c),
        [place, shift_x],
        gathered, lifted, offset, denom, inverse_z,
    )
    returned = lax.all_to_all(back, ("x", "y", "c"), 0, 0, tiled=True)
    out = call(
        finish_kernel, (5, planes, rows, cols), [place], w, returned, hats, up_x, up_y
    )
    return out[None]


def solution(mesh):
    finer = Mesh(mesh.devices.reshape(4, 2, 4, 4, 2, 2), TM + SPACE)
    in_specs = (P(TM, None, SPACE, None, None), P(SPACE, None, None))
    out_specs = P(TM, None, SPACE, None, None)
    return jax.shard_map(
        shards, mesh=finer, in_specs=in_specs, out_specs=out_specs, check_vma=False
    )
```

```python
import math

import jax
import jax.numpy as jnp
import numpy as np
from jax import lax
from jax.experimental import pallas as pl
from jax.experimental.pallas import tpu as pltpu
from jax.sharding import Mesh
from jax.sharding import PartitionSpec as P

TM = ("x", "zb", "za")
SPACE = ("y", "zh", "c")
FORWARD = ("zb", "y", "zh", "c")
ROWS = 10

step_length = 0.4
diffusion = 1.0
reaction = 1.0

G_AT = (0, 3, 5, 6)
U_AT = 6
PACK = 10
REACH = 4


def basis_coefficients(nodes, chosen):
    polynomial = [1.0]
    for other, point in enumerate(nodes):
        if other == chosen:
            continue
        divisor = nodes[chosen] - point
        widened = [0.0] * (len(polynomial) + 1)
        for power, value in enumerate(polynomial):
            widened[power + 1] += value / divisor
            widened[power] -= value * point / divisor
        polynomial = widened
    return polynomial


def basis_value(nodes, chosen, where):
    result = 1.0
    for other, point in enumerate(nodes):
        if other != chosen:
            result *= (where - point) / (nodes[chosen] - point)
    return result


def node_tables():
    root = math.sqrt(3.0 / 7.0)
    fine_tau = [0.0, (1.0 - root) / 2.0, 0.5, (1.0 + root) / 2.0, 1.0]
    coarse_tau = [0.0, 0.5, 1.0]
    integ = []
    for j in range(4):
        row_values = []
        for k in range(5):
            polynomial = basis_coefficients(fine_tau, k)
            total = 0.0
            for power, value in enumerate(polynomial):
                total += (
                    value
                    * (fine_tau[j + 1] ** (power + 1) - fine_tau[j] ** (power + 1))
                    / (power + 1)
                )
            row_values.append(total)
        integ.append(row_values)
    interp = [[basis_value(coarse_tau, c, fine_tau[m]) for c in range(3)] for m in range(5)]
    spacing = [float(fine_tau[j + 1] - fine_tau[j]) for j in range(4)]
    return integ, spacing, interp


INTEG, SPACING, INTERP = node_tables()
MIX = [
    [step_length * (INTEG[j][k] - (SPACING[j] if j == k else 0.0)) for k in range(5)]
    for j in range(4)
]
COUPLING = 0.5 * step_length * diffusion * 0.25
QUAD = [[step_length * (INTEG[2 * c][k] + INTEG[2 * c + 1][k]) for k in range(5)] for c in range(2)]


def hartley(length):
    counter = np.arange(length)
    phase = 2.0 * np.pi * (counter[:, None] * counter[None, :] % length) / length
    return (np.cos(phase) + np.sin(phase)) / math.sqrt(length)


def block_pair(table):
    rows, cols = table.shape
    both = np.zeros((2 * rows, 2 * cols))
    both[:rows, :cols] = table
    both[rows:, cols:] = table
    return both


def tables(planes, rows, cols, depth):
    rows_c, cols_c = rows // 2, cols // 2
    hx, hy, hz = hartley(rows_c), hartley(cols_c), hartley(depth)
    down_y = 0.5 * np.repeat(hy, 2, 0)
    up_y = np.repeat(hy, 2, 0).T
    wide_x = np.repeat(hx, 2, 0)
    down_x = np.zeros((rows_c, planes, planes, rows))
    up_x = np.zeros((planes, rows, rows_c, planes))
    for p in range(planes):
        down_x[:, p, p, :] = 0.25 * wide_x.T
        up_x[p, :, :, p] = wide_x
    down_x = down_x.reshape(rows_c * planes, planes * rows)
    up_x = up_x.reshape(planes * rows, rows_c * planes)
    cos_z = np.cos(2.0 * np.pi * np.arange(depth) / depth)
    cos_y = np.cos(2.0 * np.pi * np.arange(cols_c) / cols_c)
    half = COUPLING
    cos_x = np.cos(2.0 * np.pi * np.arange(rows_c) / rows_c)
    stencil = half * (6.0 - 2.0 * cos_x[:, None, None] - 2.0 * cos_y[None, None, :])
    stencil = np.broadcast_to(stencil, (rows_c, planes, cols_c)).reshape(-1, cols_c)
    stencil = np.concatenate([stencil, stencil], 1)
    blocks = depth // planes
    forward_z = np.zeros((depth, ROWS, blocks))
    for s in range(blocks):
        forward_z[:, :planes, s] = hz[:, s * planes : (s + 1) * planes]
        forward_z[:, planes, s] = hz[:, (s * planes - 1) % depth]
        forward_z[:, planes + 1, s] = hz[:, (s * planes + planes) % depth]
    forward_z = forward_z.reshape(depth, -1)
    denom = 1.0 - half * (2.0 * cos_z[:, None] + 2.0 * cos_y[None, :] - 6.0)
    denom = np.concatenate([denom, denom], 1)
    shift_x = half * 2.0 * cos_x
    inverse_z = hz.reshape(4, 2, 2, planes, depth).transpose(1, 0, 2, 3, 4)
    inverse_z = inverse_z.reshape(2, 8 * planes, depth)
    f32 = lambda a: jnp.asarray(a, jnp.float32)
    return (
        table_halves(block_pair(down_y), 0), table_halves(down_x, 1), f32(stencil),
        table_halves(forward_z, 1), table_halves(inverse_z, 2), f32(denom), ShiftTable(shift_x),
        table_halves(up_x, 1), table_halves(block_pair(up_y), 0),
    )


def lanes_swapped(a):
    return pltpu.roll(a, a.shape[1] // 2, 1)


def left_half(a):
    return lax.broadcasted_iota(jnp.int32, a.shape, 1) < a.shape[1] // 2


def halves(a):
    high = a.astype(jnp.bfloat16)
    return high, (a - high.astype(jnp.float32)).astype(jnp.bfloat16)


def table_halves(table, axis):
    table = np.asarray(table, np.float32)
    high = table.astype(jnp.bfloat16)
    low = (table - high.astype(np.float32)).astype(jnp.bfloat16)
    return jnp.asarray(np.concatenate([high, high, low], axis))


def table_times(table, b):
    high, low = halves(b)
    parts = jnp.concatenate([high, low, high], 0)
    return jnp.dot(table, parts, preferred_element_type=jnp.float32)


def times_table(a, table):
    high, low = halves(a)
    parts = jnp.concatenate([high, low, high], 1)
    return jnp.dot(parts, table, preferred_element_type=jnp.float32)


def plane_part(f):
    near = pltpu.roll(f, 1, 0) + pltpu.roll(f, f.shape[0] - 1, 0)
    near = near + pltpu.roll(f, 1, 1) + pltpu.roll(f, f.shape[1] - 1, 1)
    return diffusion * near - f * ((6.0 * diffusion - reaction) + reaction * (f * f))


def last_kernel(u, last):
    last[...] = u[4]


def old_kernel(place, u, first, g, near, far, edge_far):
    planes = u.shape[1]
    position, core, slices = place[0], place[1], place[6]
    far_edge = pl.ds(core * (planes - REACH), REACH)

    @pl.when(position == slices - 1)
    def _():
        edge_far[...] = first[far_edge]

    @pl.when(position != slices - 1)
    def _():
        edge_far[...] = u[4, far_edge]

    for p in range(planes):
        total = [None] * 4
        for k in range(5):
            field = u[k, p]
            force = plane_part(field)
            if p > 0:
                force = force + diffusion * u[k, p - 1]
            if p < planes - 1:
                force = force + diffusion * u[k, p + 1]
            for j in range(4):
                term = MIX[j][k] * force
                total[j] = term if total[j] is None else total[j] + term
        for j in range(4):
            g[j, p] = total[j]

    def packed(out, plane_of):
        for j in range(4):
            for i in range(3 - j):
                out[G_AT[j] + i] = g[j, plane_of(i)]
            edge = plane_of(0)
            out[U_AT + j] = diffusion * sum(MIX[j][k] * u[k, edge] for k in range(5))

    top = lambda i: planes - 1 - i
    bottom = lambda i: i

    @pl.when(core == 0)
    def _():
        packed(near, top)
        packed(far, bottom)

    @pl.when(core != 0)
    def _():
        packed(near, bottom)
        packed(far, top)


def near_kernel(place, first, previous, own_near, out):
    position, core = place[0], place[1]
    edge = pl.ds((1 - core) * (first.shape[0] - REACH), REACH)
    out[:PACK] = own_near[...]

    @pl.when(position == 0)
    def _():
        out[PACK:] = first[edge]

    @pl.when(position != 0)
    def _():
        out[PACK:] = previous[edge]


def relay_kernel(halo, halo_out):
    halo_out[...] = halo[...]


def sweep_kernel(
    place, first, previous, near, start_far, g, own_near, own_far, got_far,
    down_y, down_x, stencil, w, send, hats, quad,
):
    got_near, start_near = near.at[:PACK], near.at[PACK:]
    planes = first.shape[0]
    coarse = planes // 2
    position, core = place[0], place[1]

    def with_sides(body):
        @pl.when(core == 0)
        def _():
            body(start_far, own_far, got_far, start_near, own_near, got_near)

        @pl.when(core != 0)
        def _():
            body(start_near, own_near, got_near, start_far, own_far, got_far)

    @pl.when(position == 0)
    def _():
        w[0, REACH : REACH + planes] = first[...]

    @pl.when(position != 0)
    def _():
        w[0, REACH : REACH + planes] = previous[...]

    def run(start_lo, own_lo, got_lo, start_hi, own_hi, got_hi):
        w[0, :REACH] = start_lo[...]
        w[0, REACH + planes :] = start_hi[...]
        for m in range(5):
            margin = max(3 - m, 0)
            held = None
            for p in range(-margin, planes + margin):
                at = p + REACH
                field = w[m, at]
                force = plane_part(field)
                if m < 4 or p > 0:
                    force = force + diffusion * w[m, at - 1]
                if m < 4 or p < planes - 1:
                    force = force + diffusion * w[m, at + 1]
                if m < 4:
                    if p < 0:
                        source = got_lo[G_AT[m] - p - 1]
                        if p == -1:
                            source = source + own_lo[U_AT + m]
                    elif p >= planes:
                        source = got_hi[G_AT[m] + p - planes]
                        if p == planes:
                            source = source + own_hi[U_AT + m]
                    else:
                        source = g[m, p]
                        if p == 0:
                            source = source + got_lo[U_AT + m]
                        if p == planes - 1:
                            source = source + got_hi[U_AT + m]
                    w[m + 1, at] = field + step_length * SPACING[m] * force + source
                if 0 <= p < planes:
                    if p % 2 == 0:
                        held = force
                    else:
                        both = held + force
                        for c in range(2):
                            term = QUAD[c][m] * both
                            quad[c, p // 2] = term if m == 0 else quad[c, p // 2] + term

    with_sides(run)

    def paired(m):
        return jnp.concatenate(
            [w[m, REACH + 2 * i] + w[m, REACH + 2 * i + 1] for i in range(coarse)], 0
        )

    rows = coarse * first.shape[1]
    restart = paired(0)
    mask = jnp.where(position == 0, 1.0, 0.0)
    q0 = quad[0].reshape(rows, -1) + mask * restart
    q1 = quad[1].reshape(rows, -1)
    table = down_y[...]
    edge_rows = first.shape[1]
    middle = jnp.zeros((rows - 2 * edge_rows, first.shape[2]), jnp.float32)
    edges = jnp.concatenate([w[4, REACH], middle, w[4, REACH + planes - 1]], 0)
    left = [
        times_table(jnp.concatenate(pair, 1), table)
        for pair in ((q0, q1), (paired(2), paired(4)), (restart, edges))
    ]
    spectral = table_times(down_x[...], jnp.concatenate(left, 1))
    width = left[0].shape[1]
    states = spectral[:, width : 2 * width]
    third = spectral[:, 2 * width :]
    count = spectral.shape[0]
    level = lax.broadcasted_iota(jnp.int32, states.shape, 0) % coarse
    near_z = jnp.where(level > 0, pltpu.roll(states, 1, 0), 0.0)
    near_z = near_z + jnp.where(level < coarse - 1, pltpu.roll(states, count - 1, 0), 0.0)
    inside = spectral[:, :width] + stencil[...] * states - COUPLING * near_z
    is_left = left_half(states)
    last = jnp.where(is_left, lanes_swapped(third), third)
    last = last * jnp.where(is_left, diffusion * QUAD[0][4], diffusion * QUAD[1][4])
    spill = last - COUPLING * states
    spill = jnp.where((level == 0) | (level == coarse - 1), spill, 0.0)
    for y in range(4):
        for c in range(2):
            kx = 2 * y + c
            at = kx * coarse
            lines = [inside[at + p : at + p + 1] for p in range(coarse)]
            lines += [spill[at : at + 1], spill[at + coarse - 1 : at + coarse]]
            for zb in range(2):
                for zh in range(2):
                    peer = 16 * zb + 4 * y + 2 * zh + c
                    for r in range(ROWS):
                        send[peer, :, r * width : (r + 1) * width] = lines[r]
    hats[...] = spectral[:, width:]


def spectrum_kernel(place, shift_x, got, table, denom, lifted, offset, copies, lines):
    zb = place[7]
    depth = table.shape[0]
    half = depth // 2
    d = denom[...] - shift_x[place[4]]
    inv = 1.0 / d
    width = d.shape[1]
    blocks = got.shape[0] // 2
    for part in range(2):
        for r in range(ROWS):
            span = slice(r * width, (r + 1) * width)
            for s in range(blocks):
                at = r * blocks + s
                lines[at : at + 1, part * width : (part + 1) * width] = got[part * blocks + s, :, span]
    both = table_times(table[...], lines[...])
    totals = []
    for part in range(2):
        lift = both[:, part * width : (part + 1) * width]
        weighted = lift * inv
        weighted = jnp.where(left_half(d), weighted * inv, weighted)
        total = weighted + lanes_swapped(weighted)
        totals.append(total)
        packed = jnp.where(left_half(total[:half]), total[:half], total[half:])
        for i in range(copies.shape[0]):
            copies[i, part * half : (part + 1) * half] = packed
    lifted[...] = jnp.where(zb == 0, both[:, :width], both[:, width:])
    offset[...] = jnp.where(zb == 0, totals[0], totals[1])


def packed_inverse(place, shift_x, denom):
    d = denom[...] - shift_x[place[4]]
    inv = 1.0 / d
    half = inv.shape[0] // 2
    left = left_half(inv[:half])
    return inv, left, jnp.where(left, inv[:half], inv[half:])


def scan_kernel(place, shift_x, offsets, lifted, offset, denom, inverse_z, out):
    za, block, zh, zb = place[2], place[3], place[5], place[7]
    half = denom.shape[0] // 2
    inv, left, inv_packed = packed_inverse(place, shift_x, denom)
    inv2 = inv_packed * inv_packed
    inv4 = inv2 * inv2
    inv8 = inv4 * inv4
    whole = inv8 * inv8
    slice_at = zb * 4 + za
    prefix = jnp.zeros_like(inv2)
    total = jnp.zeros_like(inv2)
    for m in range(8):
        piece = offsets[m % 4, (m // 4) * half : (m // 4 + 1) * half]
        total = total * inv2 + piece
        prefix = jnp.where(m < slice_at, prefix * inv2 + piece, prefix)
    power = jnp.where(za % 2 == 1, inv2, 1.0)
    power = jnp.where(za >= 2, power * inv4, power)
    power = jnp.where(zb == 0, power, power * inv8)
    inverse = inverse_z[zh]
    weights = jnp.where(left_half(inv), inv, inv * inv)
    own = jnp.where(left_half(inv), lifted[...] * inv, offset[...])
    carried = total * power
    targets = out.shape[0] // 8
    for xp in range(targets):
        packed = jnp.where(xp == block, prefix, jnp.where(xp > block, carried, 0.0))
        carried = jnp.where(xp > block, carried * whole, carried)
        turned = lanes_swapped(packed)
        begin = jnp.concatenate(
            [jnp.where(left, packed, turned), jnp.where(left, turned, packed)], 0
        )
        later = begin * weights + jnp.where(xp == block, own, 0.0)
        planar = table_times(inverse, jnp.concatenate([later, begin], 1))
        out[8 * xp : 8 * xp + 8] = planar.reshape(8, -1, planar.shape[1])


def finish_kernel(place, w, got, hats, up_x, up_y, out):
    planes = out.shape[1]
    coarse = planes // 2
    rows = out.shape[2]
    cols = out.shape[3]
    total = got[0:8] + got[8:16] + (got[16:24] + got[24:32])
    delta = total.reshape(-1, total.shape[2]) - hats[...]
    half = delta.shape[1] // 2
    later = delta[:, :half]
    begin = jnp.where(place[0] == 0, 0.0, delta[:, half:])
    spread = table_times(up_x[...], jnp.concatenate([later, begin], 1))
    table = up_y[...]
    after = times_table(spread[:, :half], table)
    before = times_table(spread[:, half:], table[:, :cols])
    parts = [before, after[:, :cols], after[:, cols:]]
    for m in range(5):
        mixed = None
        for c in range(3):
            weight = INTERP[m][c]
            if abs(weight) < 1e-14:
                continue
            term = parts[c] if weight == 1.0 else weight * parts[c]
            mixed = term if mixed is None else mixed + term
        for i in range(coarse):
            piece = mixed[i * rows : (i + 1) * rows]
            out[m, 2 * i] = w[m, REACH + 2 * i] + piece
            out[m, 2 * i + 1] = w[m, REACH + 2 * i + 1] + piece


def whereabouts():
    x, zb, za = (lax.axis_index(a) for a in TM)
    y, zh, core = (lax.axis_index(a) for a in SPACE)
    return ((x * 2 + zb) * 4 + za, core, za, x, 2 * y + core, zh, 32, zb)


class ShiftTable:
    def __init__(self, values):
        self.values = [float(v) for v in values]

    def __getitem__(self, at):
        found = self.values[0]
        for i, value in enumerate(self.values[1:], 1):
            found = jnp.where(at == i, value, found)
        return found


def call(kernel, outs, scalars, *args, scratch=(), flops=0):
    vmem = pl.BlockSpec(memory_space=pltpu.VMEM)
    single = not isinstance(outs, list)
    shapes = [jax.ShapeDtypeStruct(s, jnp.float32) for s in ([outs] if single else outs)]
    tables = scalars[1:]
    inner = kernel
    if scalars:
        kernel = lambda *refs: inner(whereabouts(), *tables, *refs)
    result = pl.pallas_call(
        kernel,
        out_shape=shapes[0] if single else shapes,
        in_specs=[vmem] * len(args),
        out_specs=vmem if single else [vmem] * len(shapes),
        scratch_shapes=list(scratch),
        compiler_params=pltpu.CompilerParams(vmem_limit_bytes=32 * 1024 * 1024),
        cost_estimate=pl.CostEstimate(flops=flops, bytes_accessed=1 << 20, transcendentals=0),
    )(*args)
    return result


def shards(u_old, u_init):
    planes, rows, cols = u_init.shape
    coarse, rows_c, cols_c = planes // 2, rows // 2, cols // 2
    slices = lax.axis_size(TM)
    blocks = lax.axis_size(SPACE)
    depth_c = coarse * blocks
    down_y, down_x, stencil, forward_z, inverse_z, denom, shift_x, up_x, up_y = tables(
        coarse, rows, cols, depth_c
    )
    place = None
    last = call(last_kernel, (planes, rows, cols), [], u_old[0])
    halo, edge = (PACK, rows, cols), (REACH, rows, cols)
    g, own_near, own_far, edge_far = call(
        old_kernel,
        [(4, planes, rows, cols), halo, halo, edge],
        [place],
        u_old[0], u_init,
        flops=10**11,
    )

    def far_block(s):
        return (s + 1) % blocks if s % 2 else (s - 1) % blocks

    across = [
        (n * blocks + s, (n + 1) % slices * blocks + far_block(s))
        for n in range(slices)
        for s in range(blocks)
    ]

    got_far = lax.ppermute(own_far, SPACE, [(s, far_block(s)) for s in range(blocks)])
    start_far = lax.ppermute(edge_far, TM + SPACE, across)
    got_far = call(relay_kernel, halo, [], got_far, flops=10**11)
    previous = lax.ppermute(last, TM, [(i, i + 1) for i in range(slices - 1)])
    near_out = call(
        near_kernel, (PACK + REACH, rows, cols), [place], u_init, previous, own_near
    )
    near = lax.ppermute(near_out, "c", [(0, 1), (1, 0)])

    w, send, hats = call(
        sweep_kernel,
        [
            (5, planes + 2 * REACH, rows, cols),
            (2 * blocks, 1, ROWS * 2 * cols_c),
            (rows_c * coarse, 4 * cols_c),
        ],
        [place],
        u_init, previous, near, start_far, g, own_near, own_far, got_far,
        down_y, down_x, stencil,
        scratch=[pltpu.VMEM((2, coarse, rows, cols), jnp.float32)],
    )
    columns = lax.all_to_all(send, FORWARD, 0, 0, tiled=True)
    lifted, offset, copies = call(
        spectrum_kernel,
        [(depth_c, 2 * cols_c), (depth_c, 2 * cols_c), (4, depth_c, 2 * cols_c)],
        [place, shift_x],
        columns, forward_z, denom,
        scratch=[pltpu.VMEM((ROWS * blocks, 4 * cols_c), jnp.float32)],
    )
    gathered = lax.all_to_all(copies, "za", 0, 0, tiled=True)
    back = call(
        scan_kernel,
        (4 * rows_c, coarse, 4 * cols_c),
        [place, shift_x],
        gathered, lifted, offset, denom, inverse_z,
    )
    returned = lax.all_to_all(back, ("x", "y", "c"), 0, 0, tiled=True)
    out = call(
        finish_kernel, (5, planes, rows, cols), [place], w, returned, hats, up_x, up_y
    )
    return out[None]


def solution(mesh):
    finer = Mesh(mesh.devices.reshape(4, 2, 4, 4, 2, 2), TM + SPACE)
    in_specs = (P(TM, None, SPACE, None, None), P(SPACE, None, None))
    out_specs = P(TM, None, SPACE, None, None)
    return jax.shard_map(
        shards, mesh=finer, in_specs=in_specs, out_specs=out_specs, check_vma=False
    )
```

```python
import math

import jax
import jax.numpy as jnp
import numpy as np
from jax import lax
from jax.experimental import pallas as pl
from jax.experimental.pallas import tpu as pltpu
from jax.sharding import Mesh
from jax.sharding import PartitionSpec as P

TM = ("x", "zb", "za")
SPACE = ("y", "zh", "c")
FORWARD = ("zb", "y", "zh", "c")
ROWS = 10

step_length = 0.4
diffusion = 1.0
reaction = 1.0

G_AT = (0, 3, 5, 6)
U_AT = 6
PACK = 10
REACH = 4


def basis_coefficients(nodes, chosen):
    polynomial = [1.0]
    for other, point in enumerate(nodes):
        if other == chosen:
            continue
        divisor = nodes[chosen] - point
        widened = [0.0] * (len(polynomial) + 1)
        for power, value in enumerate(polynomial):
            widened[power + 1] += value / divisor
            widened[power] -= value * point / divisor
        polynomial = widened
    return polynomial


def basis_value(nodes, chosen, where):
    result = 1.0
    for other, point in enumerate(nodes):
        if other != chosen:
            result *= (where - point) / (nodes[chosen] - point)
    return result


def node_tables():
    root = math.sqrt(3.0 / 7.0)
    fine_tau = [0.0, (1.0 - root) / 2.0, 0.5, (1.0 + root) / 2.0, 1.0]
    coarse_tau = [0.0, 0.5, 1.0]
    integ = []
    for j in range(4):
        row_values = []
        for k in range(5):
            polynomial = basis_coefficients(fine_tau, k)
            total = 0.0
            for power, value in enumerate(polynomial):
                total += (
                    value
                    * (fine_tau[j + 1] ** (power + 1) - fine_tau[j] ** (power + 1))
                    / (power + 1)
                )
            row_values.append(total)
        integ.append(row_values)
    interp = [[basis_value(coarse_tau, c, fine_tau[m]) for c in range(3)] for m in range(5)]
    spacing = [float(fine_tau[j + 1] - fine_tau[j]) for j in range(4)]
    return integ, spacing, interp


INTEG, SPACING, INTERP = node_tables()
MIX = [
    [step_length * (INTEG[j][k] - (SPACING[j] if j == k else 0.0)) for k in range(5)]
    for j in range(4)
]
COUPLING = 0.5 * step_length * diffusion * 0.25
QUAD = [[step_length * (INTEG[2 * c][k] + INTEG[2 * c + 1][k]) for k in range(5)] for c in range(2)]


def hartley(length):
    counter = np.arange(length)
    phase = 2.0 * np.pi * (counter[:, None] * counter[None, :] % length) / length
    return (np.cos(phase) + np.sin(phase)) / math.sqrt(length)


def block_pair(table):
    rows, cols = table.shape
    both = np.zeros((2 * rows, 2 * cols))
    both[:rows, :cols] = table
    both[rows:, cols:] = table
    return both


def tables(planes, rows, cols, depth):
    rows_c, cols_c = rows // 2, cols // 2
    hx, hy, hz = hartley(rows_c), hartley(cols_c), hartley(depth)
    down_y = 0.5 * np.repeat(hy, 2, 0)
    up_y = np.repeat(hy, 2, 0).T
    wide_x = np.repeat(hx, 2, 0)
    down_x = np.zeros((rows_c, planes, planes, rows))
    up_x = np.zeros((planes, rows, rows_c, planes))
    for p in range(planes):
        down_x[:, p, p, :] = 0.25 * wide_x.T
        up_x[p, :, :, p] = wide_x
    down_x = down_x.reshape(rows_c * planes, planes * rows)
    up_x = up_x.reshape(planes * rows, rows_c * planes)
    cos_z = np.cos(2.0 * np.pi * np.arange(depth) / depth)
    cos_y = np.cos(2.0 * np.pi * np.arange(cols_c) / cols_c)
    half = COUPLING
    cos_x = np.cos(2.0 * np.pi * np.arange(rows_c) / rows_c)
    stencil = half * (6.0 - 2.0 * cos_x[:, None, None] - 2.0 * cos_y[None, None, :])
    stencil = np.broadcast_to(stencil, (rows_c, planes, cols_c)).reshape(-1, cols_c)
    stencil = np.concatenate([stencil, stencil], 1)
    blocks = depth // planes
    forward_z = np.zeros((depth, ROWS, blocks))
    for s in range(blocks):
        forward_z[:, :planes, s] = hz[:, s * planes : (s + 1) * planes]
        forward_z[:, planes, s] = hz[:, (s * planes - 1) % depth]
        forward_z[:, planes + 1, s] = hz[:, (s * planes + planes) % depth]
    forward_z = forward_z.reshape(depth, -1)
    denom = 1.0 - half * (2.0 * cos_z[:, None] + 2.0 * cos_y[None, :] - 6.0)
    denom = np.concatenate([denom, denom], 1)
    shift_x = half * 2.0 * cos_x
    inverse_z = hz.reshape(4, 2, 2, planes, depth).transpose(1, 0, 2, 3, 4)
    inverse_z = inverse_z.reshape(2, 8 * planes, depth)
    f32 = lambda a: jnp.asarray(a, jnp.float32)
    return (
        table_halves(block_pair(down_y), 0), table_halves(down_x, 1), f32(stencil),
        table_halves(forward_z, 1), table_halves(inverse_z, 2), f32(denom), ShiftTable(shift_x),
        table_halves(up_x, 1), table_halves(block_pair(up_y), 0),
    )


def lanes_swapped(a):
    return pltpu.roll(a, a.shape[1] // 2, 1)


def left_half(a):
    return lax.broadcasted_iota(jnp.int32, a.shape, 1) < a.shape[1] // 2


def halves(a):
    high = a.astype(jnp.bfloat16)
    return high, (a - high.astype(jnp.float32)).astype(jnp.bfloat16)


def table_halves(table, axis):
    table = np.asarray(table, np.float32)
    high = table.astype(jnp.bfloat16)
    low = (table - high.astype(np.float32)).astype(jnp.bfloat16)
    return jnp.asarray(np.concatenate([high, high, low], axis))


def table_times(table, b):
    high, low = halves(b)
    parts = jnp.concatenate([high, low, high], 0)
    return jnp.dot(table, parts, preferred_element_type=jnp.float32)


def times_table(a, table):
    high, low = halves(a)
    parts = jnp.concatenate([high, low, high], 1)
    return jnp.dot(parts, table, preferred_element_type=jnp.float32)


def plane_part(f):
    near = pltpu.roll(f, 1, 0) + pltpu.roll(f, f.shape[0] - 1, 0)
    near = near + pltpu.roll(f, 1, 1) + pltpu.roll(f, f.shape[1] - 1, 1)
    return diffusion * near - f * ((6.0 * diffusion - reaction) + reaction * (f * f))


def last_kernel(u, last):
    last[...] = u[4]


def old_kernel(place, u, first, g, near, far, edge_far):
    planes = u.shape[1]
    position, core, slices = place[0], place[1], place[6]
    far_edge = pl.ds(core * (planes - REACH), REACH)

    @pl.when(position == slices - 1)
    def _():
        edge_far[...] = first[far_edge]

    @pl.when(position != slices - 1)
    def _():
        edge_far[...] = u[4, far_edge]

    for p in range(planes):
        total = [None] * 4
        for k in range(5):
            field = u[k, p]
            force = plane_part(field)
            if p > 0:
                force = force + diffusion * u[k, p - 1]
            if p < planes - 1:
                force = force + diffusion * u[k, p + 1]
            for j in range(4):
                term = MIX[j][k] * force
                total[j] = term if total[j] is None else total[j] + term
        for j in range(4):
            g[j, p] = total[j]

    def packed(out, plane_of):
        for j in range(4):
            for i in range(3 - j):
                out[G_AT[j] + i] = g[j, plane_of(i)]
            edge = plane_of(0)
            out[U_AT + j] = diffusion * sum(MIX[j][k] * u[k, edge] for k in range(5))

    top = lambda i: planes - 1 - i
    bottom = lambda i: i

    @pl.when(core == 0)
    def _():
        packed(near, top)
        packed(far, bottom)

    @pl.when(core != 0)
    def _():
        packed(near, bottom)
        packed(far, top)


def near_kernel(place, first, previous, own_near, out):
    position, core = place[0], place[1]
    edge = pl.ds((1 - core) * (first.shape[0] - REACH), REACH)
    out[:PACK] = own_near[...]

    @pl.when(position == 0)
    def _():
        out[PACK:] = first[edge]

    @pl.when(position != 0)
    def _():
        out[PACK:] = previous[edge]


def relay_kernel(halo, halo_out):
    halo_out[...] = halo[...]


def sweep_kernel(
    place, first, previous, near, start_far, g, own_near, own_far, got_far,
    down_y, down_x, stencil, w, send, hats, quad,
):
    got_near, start_near = near.at[:PACK], near.at[PACK:]
    planes = first.shape[0]
    coarse = planes // 2
    position, core = place[0], place[1]

    def with_sides(body):
        @pl.when(core == 0)
        def _():
            body(start_far, own_far, got_far, start_near, own_near, got_near)

        @pl.when(core != 0)
        def _():
            body(start_near, own_near, got_near, start_far, own_far, got_far)

    @pl.when(position == 0)
    def _():
        w[0, REACH : REACH + planes] = first[...]

    @pl.when(position != 0)
    def _():
        w[0, REACH : REACH + planes] = previous[...]

    def run(start_lo, own_lo, got_lo, start_hi, own_hi, got_hi):
        w[0, :REACH] = start_lo[...]
        w[0, REACH + planes :] = start_hi[...]
        for m in range(5):
            margin = max(3 - m, 0)
            held = None
            for p in range(-margin, planes + margin):
                at = p + REACH
                field = w[m, at]
                force = plane_part(field)
                if m < 4 or p > 0:
                    force = force + diffusion * w[m, at - 1]
                if m < 4 or p < planes - 1:
                    force = force + diffusion * w[m, at + 1]
                if m < 4:
                    if p < 0:
                        source = got_lo[G_AT[m] - p - 1]
                        if p == -1:
                            source = source + own_lo[U_AT + m]
                    elif p >= planes:
                        source = got_hi[G_AT[m] + p - planes]
                        if p == planes:
                            source = source + own_hi[U_AT + m]
                    else:
                        source = g[m, p]
                        if p == 0:
                            source = source + got_lo[U_AT + m]
                        if p == planes - 1:
                            source = source + got_hi[U_AT + m]
                    w[m + 1, at] = field + step_length * SPACING[m] * force + source
                if 0 <= p < planes:
                    if p % 2 == 0:
                        held = force
                    else:
                        both = held + force
                        for c in range(2):
                            term = QUAD[c][m] * both
                            quad[c, p // 2] = term if m == 0 else quad[c, p // 2] + term

    with_sides(run)

    def paired(m):
        return jnp.concatenate(
            [w[m, REACH + 2 * i] + w[m, REACH + 2 * i + 1] for i in range(coarse)], 0
        )

    rows = coarse * first.shape[1]
    restart = paired(0)
    mask = jnp.where(position == 0, 1.0, 0.0)
    q0 = quad[0].reshape(rows, -1) + mask * restart
    q1 = quad[1].reshape(rows, -1)
    table = down_y[...]
    edge_rows = first.shape[1]
    middle = jnp.zeros((rows - 2 * edge_rows, first.shape[2]), jnp.float32)
    edges = jnp.concatenate([w[4, REACH], middle, w[4, REACH + planes - 1]], 0)
    fields = jnp.concatenate([q0, q1, paired(2), paired(4), restart, edges], 1)
    lines = table_times(down_x[...], fields)
    pair_width = 2 * first.shape[2]
    spectral = jnp.concatenate(
        [times_table(lines[:, i * pair_width : (i + 1) * pair_width], table) for i in range(3)], 1
    )
    width = table.shape[1]
    states = spectral[:, width : 2 * width]
    third = spectral[:, 2 * width :]
    count = spectral.shape[0]
    level = lax.broadcasted_iota(jnp.int32, states.shape, 0) % coarse
    near_z = jnp.where(level > 0, pltpu.roll(states, 1, 0), 0.0)
    near_z = near_z + jnp.where(level < coarse - 1, pltpu.roll(states, count - 1, 0), 0.0)
    inside = spectral[:, :width] + stencil[...] * states - COUPLING * near_z
    is_left = left_half(states)
    last = jnp.where(is_left, lanes_swapped(third), third)
    last = last * jnp.where(is_left, diffusion * QUAD[0][4], diffusion * QUAD[1][4])
    spill = last - COUPLING * states
    spill = jnp.where((level == 0) | (level == coarse - 1), spill, 0.0)
    for y in range(4):
        for c in range(2):
            kx = 2 * y + c
            at = kx * coarse
            lines = [inside[at + p : at + p + 1] for p in range(coarse)]
            lines += [spill[at : at + 1], spill[at + coarse - 1 : at + coarse]]
            for zb in range(2):
                for zh in range(2):
                    peer = 16 * zb + 4 * y + 2 * zh + c
                    for r in range(ROWS):
                        send[peer, :, r * width : (r + 1) * width] = lines[r]
    hats[...] = spectral[:, width:]


def spectrum_kernel(place, shift_x, got, table, denom, lifted, offset, copies, lines):
    zb = place[7]
    depth = table.shape[0]
    half = depth // 2
    d = denom[...] - shift_x[place[4]]
    inv = 1.0 / d
    width = d.shape[1]
    blocks = got.shape[0] // 2
    for part in range(2):
        for r in range(ROWS):
            span = slice(r * width, (r + 1) * width)
            for s in range(blocks):
                at = r * blocks + s
                lines[at : at + 1, part * width : (part + 1) * width] = got[part * blocks + s, :, span]
    both = table_times(table[...], lines[...])
    totals = []
    for part in range(2):
        lift = both[:, part * width : (part + 1) * width]
        weighted = lift * inv
        weighted = jnp.where(left_half(d), weighted * inv, weighted)
        total = weighted + lanes_swapped(weighted)
        totals.append(total)
        packed = jnp.where(left_half(total[:half]), total[:half], total[half:])
        for i in range(copies.shape[0]):
            copies[i, part * half : (part + 1) * half] = packed
    lifted[...] = jnp.where(zb == 0, both[:, :width], both[:, width:])
    offset[...] = jnp.where(zb == 0, totals[0], totals[1])


def packed_inverse(place, shift_x, denom):
    d = denom[...] - shift_x[place[4]]
    inv = 1.0 / d
    half = inv.shape[0] // 2
    left = left_half(inv[:half])
    return inv, left, jnp.where(left, inv[:half], inv[half:])


def scan_kernel(place, shift_x, offsets, lifted, offset, denom, inverse_z, out):
    za, block, zh, zb = place[2], place[3], place[5], place[7]
    half = denom.shape[0] // 2
    inv, left, inv_packed = packed_inverse(place, shift_x, denom)
    inv2 = inv_packed * inv_packed
    inv4 = inv2 * inv2
    inv8 = inv4 * inv4
    whole = inv8 * inv8
    slice_at = zb * 4 + za
    prefix = jnp.zeros_like(inv2)
    total = jnp.zeros_like(inv2)
    for m in range(8):
        piece = offsets[m % 4, (m // 4) * half : (m // 4 + 1) * half]
        total = total * inv2 + piece
        prefix = jnp.where(m < slice_at, prefix * inv2 + piece, prefix)
    power = jnp.where(za % 2 == 1, inv2, 1.0)
    power = jnp.where(za >= 2, power * inv4, power)
    power = jnp.where(zb == 0, power, power * inv8)
    inverse = inverse_z[zh]
    weights = jnp.where(left_half(inv), inv, inv * inv)
    own = jnp.where(left_half(inv), lifted[...] * inv, offset[...])
    carried = total * power
    targets = out.shape[0] // 8
    for xp in range(targets):
        packed = jnp.where(xp == block, prefix, jnp.where(xp > block, carried, 0.0))
        carried = jnp.where(xp > block, carried * whole, carried)
        turned = lanes_swapped(packed)
        begin = jnp.concatenate(
            [jnp.where(left, packed, turned), jnp.where(left, turned, packed)], 0
        )
        later = begin * weights + jnp.where(xp == block, own, 0.0)
        planar = table_times(inverse, jnp.concatenate([later, begin], 1))
        out[8 * xp : 8 * xp + 8] = planar.reshape(8, -1, planar.shape[1])


def finish_kernel(place, w, got, hats, up_x, up_y, out):
    planes = out.shape[1]
    coarse = planes // 2
    rows = out.shape[2]
    cols = out.shape[3]
    total = got[0:8] + got[8:16] + (got[16:24] + got[24:32])
    delta = total.reshape(-1, total.shape[2]) - hats[...]
    half = delta.shape[1] // 2
    later = delta[:, :half]
    begin = jnp.where(place[0] == 0, 0.0, delta[:, half:])
    spread = table_times(up_x[...], jnp.concatenate([later, begin], 1))
    table = up_y[...]
    after = times_table(spread[:, :half], table)
    before = times_table(spread[:, half:], table[:, :cols])
    parts = [before, after[:, :cols], after[:, cols:]]
    for m in range(5):
        mixed = None
        for c in range(3):
            weight = INTERP[m][c]
            if abs(weight) < 1e-14:
                continue
            term = parts[c] if weight == 1.0 else weight * parts[c]
            mixed = term if mixed is None else mixed + term
        for i in range(coarse):
            piece = mixed[i * rows : (i + 1) * rows]
            out[m, 2 * i] = w[m, REACH + 2 * i] + piece
            out[m, 2 * i + 1] = w[m, REACH + 2 * i + 1] + piece


def whereabouts():
    x, zb, za = (lax.axis_index(a) for a in TM)
    y, zh, core = (lax.axis_index(a) for a in SPACE)
    return ((x * 2 + zb) * 4 + za, core, za, x, 2 * y + core, zh, 32, zb)


class ShiftTable:
    def __init__(self, values):
        self.values = [float(v) for v in values]

    def __getitem__(self, at):
        found = self.values[0]
        for i, value in enumerate(self.values[1:], 1):
            found = jnp.where(at == i, value, found)
        return found


def call(kernel, outs, scalars, *args, scratch=(), flops=0):
    vmem = pl.BlockSpec(memory_space=pltpu.VMEM)
    single = not isinstance(outs, list)
    shapes = [jax.ShapeDtypeStruct(s, jnp.float32) for s in ([outs] if single else outs)]
    tables = scalars[1:]
    inner = kernel
    if scalars:
        kernel = lambda *refs: inner(whereabouts(), *tables, *refs)
    result = pl.pallas_call(
        kernel,
        out_shape=shapes[0] if single else shapes,
        in_specs=[vmem] * len(args),
        out_specs=vmem if single else [vmem] * len(shapes),
        scratch_shapes=list(scratch),
        compiler_params=pltpu.CompilerParams(vmem_limit_bytes=32 * 1024 * 1024),
        cost_estimate=pl.CostEstimate(flops=flops, bytes_accessed=1 << 20, transcendentals=0),
    )(*args)
    return result


def shards(u_old, u_init):
    planes, rows, cols = u_init.shape
    coarse, rows_c, cols_c = planes // 2, rows // 2, cols // 2
    slices = lax.axis_size(TM)
    blocks = lax.axis_size(SPACE)
    depth_c = coarse * blocks
    down_y, down_x, stencil, forward_z, inverse_z, denom, shift_x, up_x, up_y = tables(
        coarse, rows, cols, depth_c
    )
    place = None
    last = call(last_kernel, (planes, rows, cols), [], u_old[0])
    halo, edge = (PACK, rows, cols), (REACH, rows, cols)
    g, own_near, own_far, edge_far = call(
        old_kernel,
        [(4, planes, rows, cols), halo, halo, edge],
        [place],
        u_old[0], u_init,
        flops=10**11,
    )

    def far_block(s):
        return (s + 1) % blocks if s % 2 else (s - 1) % blocks

    across = [
        (n * blocks + s, (n + 1) % slices * blocks + far_block(s))
        for n in range(slices)
        for s in range(blocks)
    ]

    got_far = lax.ppermute(own_far, SPACE, [(s, far_block(s)) for s in range(blocks)])
    start_far = lax.ppermute(edge_far, TM + SPACE, across)
    got_far = call(relay_kernel, halo, [], got_far, flops=10**11)
    previous = lax.ppermute(last, TM, [(i, i + 1) for i in range(slices - 1)])
    near_out = call(
        near_kernel, (PACK + REACH, rows, cols), [place], u_init, previous, own_near
    )
    near = lax.ppermute(near_out, "c", [(0, 1), (1, 0)])

    w, send, hats = call(
        sweep_kernel,
        [
            (5, planes + 2 * REACH, rows, cols),
            (2 * blocks, 1, ROWS * 2 * cols_c),
            (rows_c * coarse, 4 * cols_c),
        ],
        [place],
        u_init, previous, near, start_far, g, own_near, own_far, got_far,
        down_y, down_x, stencil,
        scratch=[pltpu.VMEM((2, coarse, rows, cols), jnp.float32)],
    )
    columns = lax.all_to_all(send, FORWARD, 0, 0, tiled=True)
    lifted, offset, copies = call(
        spectrum_kernel,
        [(depth_c, 2 * cols_c), (depth_c, 2 * cols_c), (4, depth_c, 2 * cols_c)],
        [place, shift_x],
        columns, forward_z, denom,
        scratch=[pltpu.VMEM((ROWS * blocks, 4 * cols_c), jnp.float32)],
    )
    gathered = lax.all_to_all(copies, "za", 0, 0, tiled=True)
    back = call(
        scan_kernel,
        (4 * rows_c, coarse, 4 * cols_c),
        [place, shift_x],
        gathered, lifted, offset, denom, inverse_z,
    )
    returned = lax.all_to_all(back, ("x", "y", "c"), 0, 0, tiled=True)
    out = call(
        finish_kernel, (5, planes, rows, cols), [place], w, returned, hats, up_x, up_y
    )
    return out[None]


def solution(mesh):
    finer = Mesh(mesh.devices.reshape(4, 2, 4, 4, 2, 2), TM + SPACE)
    in_specs = (P(TM, None, SPACE, None, None), P(SPACE, None, None))
    out_specs = P(TM, None, SPACE, None, None)
    return jax.shard_map(
        shards, mesh=finer, in_specs=in_specs, out_specs=out_specs, check_vma=False
    )
```
